32 devices in a mesh: dp: 8 (over y, x, core), tm: 4 (over z).
Axes of the slice: x: 2, y: 2, z: 4, core: 2. Of those that a mesh axis runs over, the one named last changes fastest.
Arguments:
- frames: bfloat16 [4096, 1024], P(('dp', 'tm')), may hold values from -40 to 40
- out_grad: bfloat16 [4096, 1024], P(('dp', 'tm')), may hold values from -0.25 to 0.25
- norm1_gain: float32 [1024], replicated, may hold values from 0.25 to 1.75
- w_query: bfloat16 [1024, 512], replicated, may hold values from -0.1875 to 0.1875
- w_kv: bfloat16 [1024, 1024], replicated, may hold values from -0.1875 to 0.1875
- w_out: bfloat16 [512, 1024], replicated, may hold values from -0.25 to 0.25
- norm2_gain: float32 [1024], replicated, may hold values from 0.25 to 1.75
- conv_kernel: float32 [31, 1024], replicated, may hold values from -1 to 1
- conv_bias: float32 [1024], replicated, may hold values from -3 to 3
- utt_blocks: int32 [8, 2], P('dp'), may hold values from 1 to 6, 8 in all within a row
- block_slot: int32 [8, 8], P('dp'), may hold values from 0 to 7, each once within a row
- left_count: int32 [8, 8], P('dp'), may hold values from 0 to 2
Outputs:
- layer_out: bfloat16 [4096, 1024], P(('dp', 'tm'))
- kv_grad: float32 [1024, 1024], P('dp', 'tm')
The draws below stay inside these ranges and needn't reach their ends.
Inputs may be any that keep to these rules, and one draw needn't show every extreme that they name: `utt_blocks`: the 2 lengths of a group add up to 8. `block_slot`: each group's row names every slot once; slot s lies on index s // 2 of tm.
All inputs are finite; a program needn't handle non-finite values.
Results may differ from the reference program's by a relative error of at most 0.018.
Values may be sent and summed in bfloat16 or wider, within the bound.
No kernel may reach another device: no remote copies, remote signals or barrier semaphores. Data moves between devices by JAX's collectives and lax.ppermute only.
A program may use at most 64 MiB of HBM per device.

```python
import math
import jax
import jax.numpy as jnp
import numpy as np
from jax import lax

D = 1024
HEADS = 8
HD = 64
KERNEL = 31
BLOCK = 64
LC = 2
HQ = 512
KVW = 1024
BLOCKS = 8
UTT = 2
MOST = 6
ROWS = 4096
N_DP = 8


def draw_frames(key, part):
    first_key, second_key, third_key = jax.random.split(key, 3)
    row_scale = jnp.exp(jax.random.uniform(first_key, (ROWS, 1), jnp.float32, -1.15, 1.15))
    col_scale = jnp.exp(jax.random.uniform(second_key, (1, D), jnp.float32, -1.15, 1.15))
    noise = jnp.clip(jax.random.normal(third_key, (ROWS, D), jnp.float32), -4.0, 4.0)
    return (noise * row_scale * col_scale).astype(jnp.bfloat16)


def with_ends(result, stream_key, least, largest):
    dims = result.shape
    index_at = [jax.random.randint(jax.random.fold_in(stream_key, axis), (), 0, dims[axis]) for axis in range(len(dims))]
    result = result.at[tuple(index_at)].set(least)
    longest = dims.index(max(dims))
    index_at[longest] = (index_at[longest] + 1) % dims[longest]
    return result.at[tuple(index_at)].set(largest)


def shard_levels(stream_key, extent, cuts, low, high):
    factor_of, own = 1.0, jax.random.fold_in(stream_key, 6)
    for axis_at, shards_of in cuts:
        heights = jnp.exp(jax.random.uniform(jax.random.fold_in(own, axis_at), (shards_of,), jnp.float32, low / len(cuts), high / len(cuts)))
        factor_of = factor_of * jnp.repeat(heights, extent[axis_at] // shards_of).reshape([-1 if axis == axis_at else 1 for axis in range(len(extent))])
    return factor_of


def split_up(count, total, most, lean):
    portions = [(1 << 20) // math.isqrt(rank ** lean) + 1 for rank in range(2, count + 1)]
    surplus, given = total - most - (count - 1), [1] * (count - 1)
    while surplus > 0:
        free = [i for i in range(count - 1) if given[i] < most]
        mass, budget = sum([portions[i] for i in free]), surplus
        for i in free:
            more = min(most - given[i], max(1, budget * portions[i] // mass), surplus)
            given[i] = given[i] + more
            surplus = surplus - more
    return np.array([most] + given)


def ragged_sizes(own_key, count, total, limit, lean):
    if count == 2:
        one = jax.random.randint(own_key, (), max(1, total - limit), min(limit, total - 1) + 1)
        return jnp.stack([one, total - one])
    sizes = jnp.asarray(split_up(count, total, limit, lean), jnp.int32)
    couples = (count - 1) // 2
    donor, taker = sizes[1:1 + 2 * couples:2], sizes[2:2 + 2 * couples:2]
    slack = jnp.minimum(donor - 1, limit - taker)
    passed = jax.random.randint(jax.random.fold_in(own_key, 1), (couples,), 0, 1 << 20) % (slack + 1)
    sizes = sizes.at[1:1 + 2 * couples:2].set(donor - passed).at[2:2 + 2 * couples:2].set(taker + passed)
    return sizes[jax.random.permutation(jax.random.fold_in(own_key, 2), count)]


def bell_draw(rng, extent, deviation, limit, cuts=(), kind=jnp.bfloat16):
    entries = deviation * jax.random.normal(rng, extent, jnp.float32)
    if cuts:
        entries = entries * shard_levels(rng, extent, cuts, -0.22, 0.18)
    return jnp.clip(entries, -limit, limit).astype(kind)


def setup_inputs(seed: int = 0) -> dict:
    keys = jax.random.split(jax.random.key(seed), 13)
    frames = draw_frames(jax.random.fold_in(keys[12], 71), 0)
    out_grad = bell_draw(keys[1], (ROWS, D), (ROWS // 9) ** -0.5, 0.25, ((0, 32),))
    norm1_gain = jnp.clip(1.0 + 0.15 * jax.random.normal(keys[2], (D,), jnp.float32), 0.25, 1.75)
    w_query = bell_draw(keys[3], (D, HQ), D ** -0.5, 0.1875)
    w_kv = bell_draw(keys[4], (D, KVW), D ** -0.5, 0.1875)
    w_out = bell_draw(keys[5], (HQ, D), HQ ** -0.5, 0.25)
    norm2_gain = jnp.clip(1.0 + 0.15 * jax.random.normal(keys[6], (D,), jnp.float32), 0.25, 1.75)
    conv_kernel = bell_draw(keys[7], (KERNEL, D), KERNEL ** -0.5, 1.0, (), jnp.float32)
    conv_bias = bell_draw(keys[8], (D,), 0.5, 3.0, (), jnp.float32)
    utt_blocks = jax.vmap(lambda own: ragged_sizes(own, UTT, BLOCKS, MOST, 2))(jax.random.split(keys[9], N_DP)).reshape((N_DP, UTT)).astype(jnp.int32)
    block_slot = jax.vmap(lambda own: jax.random.permutation(own, BLOCKS))(jax.random.split(keys[10], N_DP)).reshape((N_DP, BLOCKS)).astype(jnp.int32)
    left_count = with_ends(jax.random.randint(keys[11], (N_DP, BLOCKS), 0, LC + 1), jax.random.fold_in(keys[11], 1), 0, LC).astype(jnp.int32)
    return {"frames": frames, "out_grad": out_grad, "norm1_gain": norm1_gain, "w_query": w_query, "w_kv": w_kv, "w_out": w_out, "norm2_gain": norm2_gain, "conv_kernel": conv_kernel, "conv_bias": conv_bias, "utt_blocks": utt_blocks, "block_slot": block_slot, "left_count": left_count}


EPSILON = 1e-05
SOFT_CAP = 4.0

def to_bf16(values):
    return lax.optimization_barrier(values.astype(jnp.bfloat16))

def norm_parts(values):
    row_mean = lax.optimization_barrier(jnp.mean(values, axis=-1, keepdims=True))
    centred = values - row_mean
    scale_inv = lax.rsqrt(lax.optimization_barrier(jnp.mean(centred * centred, axis=-1, keepdims=True)) + EPSILON)
    return (centred * scale_inv, scale_inv)

def norm_back(grad_in, unit_rows, scale_inv, gain_row):
    scaled = grad_in * gain_row
    first_mean = lax.optimization_barrier(jnp.mean(scaled, axis=-1, keepdims=True))
    second_mean = lax.optimization_barrier(jnp.mean(scaled * unit_rows, axis=-1, keepdims=True))
    return scale_inv * (scaled - first_mean - unit_rows * second_mean)

def block_layout(lengths, counts, block_total):
    utter_ends = jnp.cumsum(lengths).astype(jnp.int32)
    utter_starts = (utter_ends - lengths).astype(jnp.int32)
    block_index = jnp.arange(block_total, dtype=jnp.int32)
    past_end = block_index[:, None] >= utter_ends[None, :]
    utterance = lax.optimization_barrier(jnp.sum(past_end.astype(jnp.int32), axis=1))
    matches = utterance[:, None] == jnp.arange(lengths.shape[0], dtype=jnp.int32)[None, :]
    first_block = lax.optimization_barrier(jnp.sum(jnp.where(matches, utter_starts[None, :], 0), axis=1)).astype(jnp.int32)
    position = (block_index - first_block).astype(jnp.int32)
    return (position, jnp.minimum(counts, position).astype(jnp.int32))

def attend(queries, keys_values, allowed):
    block_count, row_count, query_width = queries.shape
    query_heads = queries.astype(jnp.float32).reshape(block_count, row_count, HEADS, HD)
    key_heads = keys_values[..., :query_width].astype(jnp.float32).reshape(block_count, -1, HEADS, HD)
    value_heads = keys_values[..., query_width:].astype(jnp.float32).reshape(block_count, -1, HEADS, HD)
    raw_scores = jnp.einsum('nrhd,nkhd->nhrk', query_heads, key_heads)
    capped = SOFT_CAP * jnp.tanh(raw_scores / (SOFT_CAP * math.sqrt(HD)))
    exped = jnp.where(allowed[:, None], jnp.exp(capped), 0.0)
    attn_probs = exped / lax.optimization_barrier(jnp.sum(exped, axis=-1, keepdims=True))
    probs_b = to_bf16(attn_probs).astype(jnp.float32)
    context = jnp.einsum('nhrk,nkhd->nrhd', probs_b, value_heads)
    return (to_bf16(context).reshape(block_count, row_count, query_width), attn_probs, capped)

def attend_back(queries, keys_values, context, attn_probs, capped, grad_context):
    block_count, row_count, query_width = queries.shape
    query_heads = queries.astype(jnp.float32).reshape(block_count, row_count, HEADS, HD)
    value_heads = keys_values[..., query_width:].astype(jnp.float32).reshape(block_count, -1, HEADS, HD)
    grad_heads = grad_context.astype(jnp.float32).reshape(block_count, row_count, HEADS, HD)
    context_heads = context.astype(jnp.float32).reshape(block_count, row_count, HEADS, HD)
    grad_probs = jnp.einsum('nrhd,nkhd->nhrk', grad_heads, value_heads)
    delta_rows = jnp.transpose(lax.optimization_barrier(jnp.sum(grad_heads * context_heads, axis=-1)), (0, 2, 1))[..., None]
    grad_raw = attn_probs * (grad_probs - delta_rows) * (1.0 - (capped / SOFT_CAP) ** 2) / math.sqrt(HD)
    grad_raw_b = to_bf16(grad_raw).astype(jnp.float32)
    probs_b = to_bf16(attn_probs).astype(jnp.float32)
    key_part = jnp.einsum('nhrk,nrhd->nkhd', grad_raw_b, query_heads)
    value_part = jnp.einsum('nhrk,nrhd->nkhd', probs_b, grad_heads)
    key_rows = key_part.shape[1]
    joined = jnp.concatenate([key_part.reshape(block_count, key_rows, query_width), value_part.reshape(block_count, key_rows, query_width)], axis=-1)
    return to_bf16(joined)

def group_pass(frames, out_grad, lengths, slot_table, counts, norm1_gain, w_query, w_kv, w_out, norm2_gain, conv_kernel, conv_bias):
    block_total = slot_table.shape[0]
    tail_rows = KERNEL - 1
    span_blocks = LC + 1
    block_index = jnp.arange(block_total, dtype=jnp.int32)
    position, reach = block_layout(lengths, counts, block_total)
    in_blocks = jnp.take(frames.reshape(block_total, BLOCK, D), slot_table, axis=0)
    grad_blocks = jnp.take(out_grad.reshape(block_total, BLOCK, D), slot_table, axis=0)
    unit_first, unused_inv = norm_parts(in_blocks.astype(jnp.float32))
    normed = to_bf16(unit_first * norm1_gain)
    flat_normed = normed.reshape(block_total * BLOCK, D)
    queries = to_bf16(jnp.dot(flat_normed, w_query, preferred_element_type=jnp.float32)).reshape(block_total, BLOCK, HQ)
    keys_values = to_bf16(jnp.dot(flat_normed, w_kv, preferred_element_type=jnp.float32)).reshape(block_total, BLOCK, KVW)
    window = jnp.maximum(block_index[:, None] - LC + jnp.arange(span_blocks, dtype=jnp.int32)[None, :], 0).astype(jnp.int32)
    kv_window = jnp.take(keys_values, window, axis=0).reshape(block_total, span_blocks * BLOCK, KVW)
    block_ok = jnp.arange(span_blocks, dtype=jnp.int32)[None, :] >= LC - reach[:, None]
    allowed = jnp.broadcast_to(jnp.repeat(block_ok, BLOCK, axis=1)[:, None, :], (block_total, BLOCK, span_blocks * BLOCK))
    context, attn_probs, capped = attend(queries, kv_window, allowed)
    hidden = in_blocks.astype(jnp.float32) + jnp.dot(context.reshape(-1, HQ), w_out, preferred_element_type=jnp.float32).reshape(block_total, BLOCK, D)
    unit_second, inv_second = norm_parts(hidden)
    conv_in = to_bf16(unit_second * norm2_gain)
    prev_block = jnp.maximum(block_index - 1, 0).astype(jnp.int32)
    has_prev = position >= 1
    cache_rows = jnp.where(has_prev[:, None, None], jnp.take(conv_in, prev_block, axis=0)[:, BLOCK - tail_rows:], jnp.zeros((), jnp.bfloat16))
    extended = jnp.concatenate([cache_rows, conv_in], axis=1).astype(jnp.float32)
    mixed_conv = conv_bias + conv_kernel[0] * extended[:, :BLOCK]
    for tap_index in range(1, KERNEL):
        mixed_conv = mixed_conv + conv_kernel[tap_index] * extended[:, tap_index:tap_index + BLOCK]
    gate_value = jax.nn.sigmoid(mixed_conv)
    layer_out = (hidden + mixed_conv * gate_value).astype(jnp.bfloat16)
    out_grad_f = grad_blocks.astype(jnp.float32)
    grad_mixed = out_grad_f * gate_value * (1.0 + mixed_conv * (1.0 - gate_value))
    padded = jnp.pad(grad_mixed, ((0, 0), (tail_rows, tail_rows), (0, 0)))
    grad_ext = conv_kernel[0] * padded[:, tail_rows:tail_rows + BLOCK + tail_rows]
    for tap_index in range(1, KERNEL):
        grad_ext = grad_ext + conv_kernel[tap_index] * padded[:, tail_rows - tap_index:tail_rows - tap_index + BLOCK + tail_rows]
    carried = jnp.where(has_prev[:, None, None], grad_ext[:, :tail_rows], 0.0)
    grad_hidden = out_grad_f + norm_back(grad_ext[:, tail_rows:], unit_second, inv_second, norm2_gain)
    grad_carried = norm_back(carried, jnp.take(unit_second, prev_block, axis=0)[:, BLOCK - tail_rows:], jnp.take(inv_second, prev_block, axis=0)[:, BLOCK - tail_rows:], norm2_gain)
    grad_ctx_own = to_bf16(jnp.dot(to_bf16(grad_hidden).reshape(-1, D), w_out.T, preferred_element_type=jnp.float32)).reshape(block_total, BLOCK, HQ)
    grad_ctx_carried = to_bf16(jnp.dot(to_bf16(grad_carried).reshape(-1, D), w_out.T, preferred_element_type=jnp.float32)).reshape(block_total, tail_rows, HQ)
    term_own = attend_back(queries, kv_window, context, attn_probs, capped, grad_ctx_own)
    term_carried = attend_back(jnp.take(queries, prev_block, axis=0)[:, BLOCK - tail_rows:], jnp.take(kv_window, prev_block, axis=0), jnp.take(context, prev_block, axis=0)[:, BLOCK - tail_rows:], jnp.take(attn_probs, prev_block, axis=0)[:, :, BLOCK - tail_rows:], jnp.take(capped, prev_block, axis=0)[:, :, BLOCK - tail_rows:], grad_ctx_carried)
    normed_window = jnp.take(normed, window, axis=0).reshape(block_total, span_blocks * BLOCK, D).astype(jnp.float32)
    group_grad = jnp.einsum('nkd,nke->de', normed_window, term_own.astype(jnp.float32))
    group_grad = group_grad + jnp.einsum('nkd,nke->de', jnp.take(normed_window, prev_block, axis=0), term_carried.astype(jnp.float32))
    out_slots = jnp.zeros_like(layer_out).at[slot_table].set(layer_out)
    return (out_slots.reshape(block_total * BLOCK, D), group_grad)

def reference(frames, out_grad, norm1_gain, w_query, w_kv, w_out, norm2_gain, conv_kernel, conv_bias, utt_blocks, block_slot, left_count):
    group_total = utt_blocks.shape[0]
    group_rows = frames.shape[0] // group_total
    frames_grouped = frames.reshape(group_total, group_rows, D)
    grads_grouped = out_grad.reshape(group_total, group_rows, D)

    def step(running, item):
        frame_rows, grad_rows, lengths, slot_table, counts = item
        out_rows, group_grad = group_pass(frame_rows, grad_rows, lengths, slot_table, counts, norm1_gain, w_query, w_kv, w_out, norm2_gain, conv_kernel, conv_bias)
        return (running + group_grad, out_rows)
    start_grad = jnp.zeros((D, KVW), jnp.float32)
    kv_grad, outputs = lax.scan(step, start_grad, (frames_grouped, grads_grouped, utt_blocks, block_slot, left_count))
    return (outputs.reshape(frames.shape[0], D), kv_grad)
```

```python
import functools
import math

import jax
import jax.numpy as jnp
from jax import lax
from jax.experimental import pallas as pl
from jax.experimental.pallas import tpu as pltpu
from jax.sharding import PartitionSpec as P

HEADS = 8
KERNEL = 31
BLOCK = 64
LC = 2
SPAN = (LC + 1) * BLOCK
HALO = 32
PAD = LC + 1
EPSILON = 1e-05
SOFT_CAP = 4.0
LANES = 128

BF16 = jnp.bfloat16
F32 = jnp.float32


def dot_nn(a, b):
    return lax.dot_general(a, b, (((1,), (0,)), ((), ())), preferred_element_type=F32)


def dot_nt(a, b):
    return lax.dot_general(a, b, (((1,), (1,)), ((), ())), preferred_element_type=F32)


def dot_tn(a, b):
    return lax.dot_general(a, b, (((0,), (0,)), ((), ())), preferred_element_type=F32)


def norm_stats(values):
    row_mean = jnp.mean(values, axis=-1, keepdims=True)
    centred = values - row_mean
    scale_inv = lax.rsqrt(jnp.mean(centred * centred, axis=-1, keepdims=True) + EPSILON)
    return centred * scale_inv, scale_inv


class Layout:
    def __init__(self, utt_ref, slot_ref, left_ref):
        self.utt, self.slot, self.left = utt_ref, slot_ref, left_ref
        self.blocks = slot_ref.shape[1]

    def block_of(self, slot):
        found = jnp.int32(0)
        for b in range(self.blocks):
            found = jnp.where(self.slot[0, b] == slot, jnp.int32(b), found)
        return found

    def position(self, block):
        start = jnp.int32(0)
        first = jnp.int32(0)
        for u in range(self.utt.shape[1]):
            first = jnp.where(block >= start, start, first)
            start = start + self.utt[0, u]
        return block - first

    def reach(self, block):
        safe = jnp.clip(block, 0, self.blocks - 1)
        return jnp.minimum(self.left[0, safe], self.position(safe))


def diag_mask(heads, rows, head_size):
    shape = (heads * rows, heads * head_size)
    row_head = lax.broadcasted_iota(jnp.int32, shape, 0) // rows
    col_head = lax.broadcasted_iota(jnp.int32, shape, 1) // head_size
    return jnp.where(row_head == col_head, 1.0, 0.0).astype(F32)


def spread(rows, mask_b):
    copies = mask_b.shape[0] // rows.shape[0]
    return jnp.concatenate([rows] * copies, axis=0) * mask_b


def window_probs(diag_q, k_win, reach):
    raw = dot_nt(k_win, diag_q)
    unit = jnp.tanh(raw * (1.0 / (SOFT_CAP * math.sqrt(k_win.shape[1] // HEADS_IN(k_win)))))
    exped = jnp.exp(SOFT_CAP * unit)
    parts = []
    for w in range(LC):
        ok = jnp.where(reach >= LC - w, 1.0, 0.0).astype(F32)
        parts.append(exped[w * BLOCK : (w + 1) * BLOCK] * ok)
    parts.append(exped[LC * BLOCK :])
    exped = jnp.concatenate(parts, axis=0)
    total = jnp.sum(exped, axis=0, keepdims=True)
    return exped * (1.0 / total), unit


def HEADS_IN(k_win):
    return k_win.shape[1] // 64


def fold_heads(full, mask_f, rows):
    kept = full * mask_f
    total = kept[:rows]
    for h in range(1, full.shape[0] // rows):
        total = total + kept[h * rows : (h + 1) * rows]
    return total


def forward_kernel(tm, *refs):
    me_ref, utt_ref, slot_ref, left_ref = refs[:4]
    frame_refs = refs[4 : 4 + tm]
    refs = refs[4 + tm :]
    grad_refs = refs[:tm]
    (g1_ref, wq_ref, wkv_ref, wo_ref, g2_ref, ck_ref, cb_ref) = refs[tm : tm + 7]
    refs = refs[tm + 7 :]
    out_ref = refs[0]
    send_refs = refs[1 : 1 + tm]
    q4_ref, k4_ref, v4_ref, n_ref = refs[1 + tm : 5 + tm]
    f_s, q_s, kv_s, ctx_s, e_s, h_s, u_s, og_s, gr_s, gc_s = refs[5 + tm :]

    me = me_ref[0]
    table = Layout(utt_ref, slot_ref, left_ref)
    blocks = table.blocks
    local = blocks // tm
    width = f_s.shape[1]
    hq = wq_ref.shape[1]
    head_size = hq // HEADS
    share = q4_ref.shape[1]
    half = tm // 2

    g1 = g1_ref[...]
    zero_pad = jnp.zeros((PAD * BLOCK, width), BF16)
    n_ref[: PAD * BLOCK] = zero_pad
    n_ref[(PAD + blocks) * BLOCK :] = jnp.zeros((BLOCK, width), BF16)
    f_s[: PAD * BLOCK] = zero_pad
    f_s[(PAD + blocks) * BLOCK :] = jnp.zeros((BLOCK, width), BF16)
    for m in range(tm):
        for j in range(local):
            b = table.block_of((me ^ m) * local + j)
            at = pl.ds(pl.multiple_of((b + PAD) * BLOCK, BLOCK), BLOCK)
            rows = frame_refs[m][j * BLOCK : (j + 1) * BLOCK]
            f_s[at] = rows
            unit, _ = norm_stats(rows.astype(F32))
            n_ref[at] = (unit * g1).astype(BF16)

    chunk = 2 * BLOCK

    def project(i, carry):
        at = pl.ds(pl.multiple_of(i * chunk, chunk), chunk)
        n = n_ref[at]
        q_s[at] = dot_nn(n, wq_ref[...]).astype(BF16)
        kv_s[at] = dot_nn(n, wkv_ref[...]).astype(BF16)
        return carry

    lax.fori_loop(0, n_ref.shape[0] // chunk, project, 0)

    lead = pl.multiple_of((me % half) * share, share)
    q4_ref[...] = q_s[:, pl.ds(lead, share)]
    k4_ref[...] = kv_s[:, pl.ds(lead, share)]
    v4_ref[...] = kv_s[:, pl.ds(pl.multiple_of(hq + lead, share), share)]

    mid_heads = 256 // BLOCK
    mid_f = diag_mask(mid_heads, BLOCK, head_size)
    mid_b = mid_f.astype(BF16)
    side_f = diag_mask(HEADS, HALO, head_size)
    side_b = side_f.astype(BF16)

    for i in range(local):
        c = table.block_of(me * local + i)
        base = (c + PAD) * BLOCK
        pieces = [(c - 1, base - HALO, HALO, 0, HALO)]
        pieces += [(c, base, BLOCK, HALO, BLOCK)]
        pieces += [(c + 1, base + BLOCK, HALO, HALO + BLOCK, HALO)]
        for blk, row, count, put, _ in pieces:
            reach = table.reach(blk)
            win = pl.ds(pl.multiple_of((blk + PAD - LC) * BLOCK, BLOCK), SPAN)
            at = pl.ds(pl.multiple_of(row, HALO), count)
            if count == BLOCK:
                groups, mask_f, mask_b = HEADS // mid_heads, mid_f, mid_b
            else:
                groups, mask_f, mask_b = 1, side_f, side_b
            wide = hq // groups
            for g in range(groups):
                cols = slice(g * wide, (g + 1) * wide)
                vcols = slice(hq + g * wide, hq + (g + 1) * wide)
                diag_q = spread(q_s[at, cols], mask_b)
                probs, _ = window_probs(diag_q, kv_s[win, cols], reach)
                full = dot_tn(probs.astype(BF16), kv_s[win, vcols])
                ctx_s[put : put + count, cols] = fold_heads(full, mask_f, count).astype(BF16)

        span_at = pl.ds(pl.multiple_of(base - HALO, HALO), 2 * BLOCK)
        hidden = f_s[span_at].astype(F32) + dot_nn(ctx_s[...], wo_ref[...])
        unit, inv = norm_stats(hidden)
        conv_in = (unit * g2_ref[...]).astype(BF16).astype(F32)
        has_prev = table.position(c) >= 1
        e_s[:HALO] = conv_in[:HALO] * jnp.where(has_prev, 1.0, 0.0).astype(F32)
        e_s[HALO:] = conv_in[HALO:]
        h_s[...] = hidden[HALO : HALO + BLOCK]
        u_s[...] = unit[HALO : HALO + BLOCK]
        inv_own = inv[HALO : HALO + BLOCK]

        og_s[:BLOCK] = grad_refs[0][i * BLOCK : (i + 1) * BLOCK].astype(F32)
        nxt = jnp.minimum(c + 1, blocks - 1)
        has_next = jnp.logical_and(c + 1 < blocks, table.position(nxt) >= 1)
        next_slot = slot_ref[0, nxt]
        next_m = (next_slot // local) ^ me
        next_j = next_slot % local
        og_s[BLOCK:] = jnp.zeros((HALO, width), F32)
        for m in range(tm):
            stride = BLOCK if m == 0 else HALO

            @pl.when(jnp.logical_and(has_next, next_m == m))
            def _():
                start = pl.multiple_of(next_j * stride, HALO)
                og_s[BLOCK:] = grad_refs[m][pl.ds(start, HALO)].astype(F32)

        reach_rows = BLOCK + HALO

        def conv(k, carry):
            cols = pl.ds(pl.multiple_of(k * LANES, LANES), LANES)
            ext = e_s[:, cols]
            taps = ck_ref[:, cols]
            acc = jnp.broadcast_to(cb_ref[:, cols], (reach_rows, LANES))
            for s in range(8):
                moved = ext[s + 2 : s + 2 + reach_rows + 24]
                for a in range(4):
                    j = 8 * a + s
                    if j < KERNEL:
                        acc = acc + taps[j : j + 1] * moved[8 * a : 8 * a + reach_rows]
            gate = 0.5 * jnp.tanh(0.5 * acc) + 0.5
            out_ref[i * BLOCK : (i + 1) * BLOCK, cols] = (
                h_s[:, cols] + (acc * gate)[:BLOCK]
            ).astype(BF16)
            gm = og_s[:, cols] * gate * (1.0 + acc * (1.0 - gate))
            back = jnp.zeros((BLOCK, LANES), F32)
            for s in range(8):
                moved = gm[s : s + BLOCK + 24]
                for a in range(4):
                    j = 8 * a + s
                    if j < KERNEL:
                        flip = KERNEL - 1 - j
                        back = back + taps[flip : flip + 1] * moved[8 * a : 8 * a + BLOCK]
            gr_s[:, cols] = back
            return carry

        lax.fori_loop(0, width // LANES, conv, 0)

        scaled = gr_s[...] * g2_ref[...]
        unit_own = u_s[...]
        first = jnp.mean(scaled, axis=-1, keepdims=True)
        second = jnp.mean(scaled * unit_own, axis=-1, keepdims=True)
        grad_hidden = og_s[:BLOCK] + inv_own * (scaled - first - unit_own * second)
        gc_s[...] = dot_nt(grad_hidden.astype(BF16), wo_ref[...]).astype(BF16)
        for m in range(tm):
            cols = pl.ds(pl.multiple_of(((me ^ m) % half) * share, share), share)
            send_refs[m][i * BLOCK : (i + 1) * BLOCK] = gc_s[:, cols]


def probs_kernel(utt_ref, slot_ref, left_ref, q4_ref, k4_ref, p_ref, d_ref):
    table = Layout(utt_ref, slot_ref, left_ref)
    share = q4_ref.shape[1]
    head_size = 64
    heads = share // head_size
    mask_b = diag_mask(heads, BLOCK, head_size).astype(BF16)

    def step(c, carry):
        row = (c + PAD) * BLOCK
        diag_q = spread(q4_ref[pl.ds(pl.multiple_of(row, BLOCK), BLOCK)], mask_b)
        win = pl.ds(pl.multiple_of(row - LC * BLOCK, BLOCK), SPAN)
        probs, unit = window_probs(diag_q, k4_ref[win], table.reach(c))
        p_ref[c] = probs
        d_ref[c] = (1.0 - unit * unit) * (1.0 / math.sqrt(head_size))
        return carry

    lax.fori_loop(0, table.blocks, step, 0)


def backward_kernel(tm, *refs):
    me_ref, slot_ref, q4_ref, v4_ref, n_ref, p_ref, d_ref = refs[:7]
    g_refs = refs[7 : 7 + tm]
    out_refs = refs[7 + tm : -2]
    gt_s, t_s = refs[-2:]
    me = me_ref[0]
    blocks = slot_ref.shape[1]
    local = blocks // tm
    share = q4_ref.shape[1]
    head_size = 64
    heads = share // head_size
    mask_b = diag_mask(heads, BLOCK, head_size).astype(BF16)

    for m in range(tm):
        for j in range(local):
            slot = (me ^ m) * local + j
            b = jnp.int32(0)
            for k in range(blocks):
                b = jnp.where(slot_ref[0, k] == slot, jnp.int32(k), b)
            gt_s[pl.ds(pl.multiple_of(b * BLOCK, BLOCK), BLOCK)] = g_refs[m][
                j * BLOCK : (j + 1) * BLOCK
            ]
    t_s[...] = jnp.zeros(t_s.shape, F32)

    @pl.when(me >= tm // 2)
    def _():
        def step(c, carry):
            row = c * BLOCK
            diag_g = spread(gt_s[pl.ds(pl.multiple_of(row, BLOCK), BLOCK)], mask_b)
            win = pl.ds(pl.multiple_of(row + (PAD - LC) * BLOCK, BLOCK), SPAN)
            t_s[win] = t_s[win] + dot_nn(p_ref[c].astype(BF16), diag_g)
            return carry

        lax.fori_loop(0, blocks, step, 0)

    @pl.when(me < tm // 2)
    def _():
        def step(c, carry):
            row = c * BLOCK
            diag_g = spread(gt_s[pl.ds(pl.multiple_of(row, BLOCK), BLOCK)], mask_b)
            own = pl.ds(pl.multiple_of(row + PAD * BLOCK, BLOCK), BLOCK)
            diag_q = spread(q4_ref[own], mask_b)
            win = pl.ds(pl.multiple_of(row + (PAD - LC) * BLOCK, BLOCK), SPAN)
            grad_probs = dot_nt(v4_ref[win], diag_g)
            probs = p_ref[c]
            delta = jnp.sum(probs * grad_probs, axis=0, keepdims=True)
            grad_raw = probs * (grad_probs - delta) * d_ref[c]
            t_s[win] = t_s[win] + dot_nn(grad_raw.astype(BF16), diag_q)
            return carry

        lax.fori_loop(0, blocks, step, 0)

    rows = slice(PAD * BLOCK, (PAD + blocks) * BLOCK)
    full = dot_tn(t_s[rows].astype(BF16), n_ref[rows]).astype(BF16)
    part = out_refs[0].shape[1]
    if len(out_refs) == 1:
        out_refs[0][...] = full
    else:
        for m in range(len(out_refs)):
            out_refs[m][...] = full[:, m * part : (m + 1) * part]


def sum_kernel(*refs):
    total = refs[0][...].astype(F32)
    for ref in refs[1:-1]:
        total = total + ref[...].astype(F32)
    refs[-1][...] = total.T


def on_device(
    frames,
    out_grad,
    norm1_gain,
    w_query,
    w_kv,
    w_out,
    norm2_gain,
    conv_kernel,
    conv_bias,
    utt_blocks,
    block_slot,
    left_count,
):
    tm = lax.axis_size("tm")
    dp = lax.axis_size("dp")
    width = frames.shape[1]
    rows = frames.shape[0]
    blocks = block_slot.shape[1]
    local = rows // BLOCK
    hq = w_query.shape[1]
    share = w_kv.shape[1] // tm
    padded = (blocks + PAD + 1) * BLOCK

    def swap(value, axis, size, m):
        return lax.ppermute(value, axis, [(i, i ^ m) for i in range(size)])

    heads_rows = out_grad.reshape(local, BLOCK, width)[:, :HALO].reshape(local * HALO, width)
    order = sorted(range(1, tm), key=lambda m: -m)
    frame_parts = {0: frames}
    grad_parts = {0: out_grad}
    for m in order:
        frame_parts[m] = swap(frames, "tm", tm, m)
    for m in order:
        grad_parts[m] = swap(heads_rows, "tm", tm, m)
    me = lax.axis_index("tm").astype(jnp.int32).reshape(1)

    smem = pl.BlockSpec(memory_space=pltpu.SMEM)
    vmem = pl.BlockSpec(memory_space=pltpu.VMEM)
    shape = jax.ShapeDtypeStruct
    forward = pl.pallas_call(
        functools.partial(forward_kernel, tm),
        out_shape=[shape((rows, width), BF16)]
        + [shape((rows, share), BF16)] * tm
        + [shape((padded, share), BF16)] * 3
        + [shape((padded, width), BF16)],
        in_specs=[smem] * 4 + [vmem] * (2 * tm + 7),
        out_specs=[vmem] * (tm + 5),
        scratch_shapes=[
            pltpu.VMEM((padded, width), BF16),
            pltpu.VMEM((padded, hq), BF16),
            pltpu.VMEM((padded, 2 * hq), BF16),
            pltpu.VMEM((2 * BLOCK, hq), BF16),
            pltpu.VMEM((2 * BLOCK, width), F32),
            pltpu.VMEM((BLOCK, width), F32),
            pltpu.VMEM((BLOCK, width), F32),
            pltpu.VMEM((BLOCK + HALO, width), F32),
            pltpu.VMEM((BLOCK, width), F32),
            pltpu.VMEM((BLOCK, hq), BF16),
        ],
        compiler_params=pltpu.CompilerParams(vmem_limit_bytes=40 << 20),
        name="forward_pass",
    )
    results = forward(
        me,
        utt_blocks,
        block_slot,
        left_count,
        *[frame_parts[m] for m in range(tm)],
        *[grad_parts[m] for m in range(tm)],
        norm1_gain.reshape(1, -1),
        w_query,
        w_kv,
        w_out,
        norm2_gain.reshape(1, -1),
        conv_kernel,
        conv_bias.reshape(1, -1),
    )
    layer_out = results[0]
    sends = results[1 : 1 + tm]
    q4, k4, v4, normed = results[1 + tm :]
    got = [sends[0]] + [swap(sends[m], "tm", tm, m) for m in range(1, tm)]

    probs, slopes = pl.pallas_call(
        probs_kernel,
        out_shape=[shape((blocks, SPAN, share // 64 * BLOCK), F32)] * 2,
        in_specs=[smem] * 3 + [vmem] * 2,
        out_specs=[vmem] * 2,
        compiler_params=pltpu.CompilerParams(vmem_limit_bytes=24 << 20),
        name="window_probs",
        cost_estimate=pl.CostEstimate(
            flops=2 * 10**9, bytes_accessed=4 * 10**6, transcendentals=800000
        ),
    )(utt_blocks, block_slot, left_count, q4, k4)

    direct = dp <= 8
    parts = dp if direct else 1
    pieces = pl.pallas_call(
        functools.partial(backward_kernel, tm),
        out_shape=[shape((share, width // parts), BF16)] * parts,
        in_specs=[smem] * 2 + [vmem] * (5 + tm),
        out_specs=[vmem] * parts,
        scratch_shapes=[
            pltpu.VMEM((blocks * BLOCK, share), BF16),
            pltpu.VMEM((padded, share), F32),
        ],
        compiler_params=pltpu.CompilerParams(vmem_limit_bytes=32 << 20),
        name="key_value_terms",
    )(me, block_slot, q4, v4, normed, probs, slopes, *got)

    if direct:
        stacked = jnp.stack(pieces)
        mine = lax.all_to_all(stacked, "dp", 0, 0, tiled=False)
        terms = [mine[m] for m in range(dp)]
    else:
        terms = [lax.psum_scatter(pieces[0], "dp", scatter_dimension=1, tiled=True)]
    kv_grad = pl.pallas_call(
        sum_kernel,
        out_shape=shape((width // dp, share), F32),
        in_specs=[vmem] * len(terms),
        out_specs=vmem,
        name="sum_groups",
    )(*terms)
    return layer_out, kv_grad


def solution(mesh):
    return jax.shard_map(
        on_device,
        mesh=mesh,
        in_specs=(
            P(("dp", "tm"), None),
            P(("dp", "tm"), None),
            P(),
            P(),
            P(),
            P(),
            P(),
            P(),
            P(),
            P("dp", None),
            P("dp", None),
            P("dp", None),
        ),
        out_specs=(P(("dp", "tm"), None), P("dp", "tm")),
        check_vma=False,
    )
```

```python
import functools
import math

import jax
import jax.numpy as jnp
from jax import lax
from jax.experimental import pallas as pl
from jax.experimental.pallas import tpu as pltpu
from jax.sharding import PartitionSpec as P

HEADS = 8
KERNEL = 31
BLOCK = 64
LC = 2
SPAN = (LC + 1) * BLOCK
HALO = 32
ROWS = HALO + BLOCK
PAD = LC + 1
EPSILON = 1e-05
SOFT_CAP = 4.0
LANES = 128
SUB = 8

BF16 = jnp.bfloat16
F32 = jnp.float32


def dot_nn(a, b):
    return lax.dot_general(a, b, (((1,), (0,)), ((), ())), preferred_element_type=F32)


def dot_nt(a, b):
    return lax.dot_general(a, b, (((1,), (1,)), ((), ())), preferred_element_type=F32)


def dot_tn(a, b):
    return lax.dot_general(a, b, (((0,), (0,)), ((), ())), preferred_element_type=F32)


def norm_stats(values):
    row_mean = jnp.mean(values, axis=-1, keepdims=True)
    centred = values - row_mean
    scale_inv = lax.rsqrt(jnp.mean(centred * centred, axis=-1, keepdims=True) + EPSILON)
    return centred * scale_inv, scale_inv


class Layout:
    def __init__(self, meta_ref, utts, blocks):
        self.ref, self.utts, self.blocks = meta_ref, utts, blocks

    def me(self):
        return self.ref[0, 0]

    def dp(self):
        return self.ref[0, 1]

    def block_of(self, slot):
        found = jnp.int32(0)
        for b in range(self.blocks):
            found = jnp.where(self.ref[0, 2 + self.utts + b] == slot, jnp.int32(b), found)
        return found

    def position(self, block):
        start = jnp.int32(0)
        first = jnp.int32(0)
        for u in range(self.utts):
            first = jnp.where(block >= start, start, first)
            start = start + self.ref[0, 2 + u]
        return block - first

    def reach(self, block):
        safe = jnp.maximum(block, 0)
        left = self.ref[0, 2 + self.utts + self.blocks + safe]
        return jnp.minimum(left, self.position(safe))


def row_at(block, count=BLOCK, shift=0):
    return pl.ds(pl.multiple_of((block + PAD) * BLOCK + shift, math.gcd(BLOCK, shift)), count)


def diag_mask(heads, rows, head_size):
    shape = (heads * rows, heads * head_size)
    row_head = lax.broadcasted_iota(jnp.int32, shape, 0) // rows
    col_head = lax.broadcasted_iota(jnp.int32, shape, 1) // head_size
    return jnp.where(row_head == col_head, 1.0, 0.0).astype(F32)


def spread(rows, mask_b):
    copies = mask_b.shape[0] // rows.shape[0]
    return jnp.concatenate([rows] * copies, axis=0) * mask_b


def fold_heads(full, mask_f, rows):
    kept = full * mask_f
    total = kept[:rows]
    for h in range(1, full.shape[0] // rows):
        total = total + kept[h * rows : (h + 1) * rows]
    return total


def window_probs(diag_q, k_win, reach, head_size):
    raw = dot_nt(k_win, diag_q)
    unit = jnp.tanh(raw * (1.0 / (SOFT_CAP * math.sqrt(head_size))))
    exped = jnp.exp(SOFT_CAP * unit)
    parts = []
    for w in range(LC):
        ok = jnp.where(reach >= LC - w, 1.0, 0.0).astype(F32)
        parts.append(exped[w * BLOCK : (w + 1) * BLOCK] * ok)
    parts.append(exped[LC * BLOCK :])
    exped = jnp.concatenate(parts, axis=0)
    total = jnp.sum(exped, axis=0, keepdims=True)
    return exped * (1.0 / total), unit


def project_kernel(crossed_at, *refs):
    meta_ref, g1_ref, wq_ref, wkv_ref = refs[:4]
    if crossed_at:
        crossed_ref, handed_ref, n_ref, q_ref, kv_ref, x_ref = refs[4:]
        me = meta_ref[0, 0]
        middle = functools.reduce(jnp.logical_or, [me == t for t in crossed_at])
        rows = jnp.where(middle, crossed_ref[...], handed_ref[...])
        x_ref[...] = rows
    else:
        x_ref, n_ref, q_ref, kv_ref = refs[4:]
        rows = x_ref[...]
    unit, _ = norm_stats(rows.astype(F32))
    normed = (unit * g1_ref[...]).astype(BF16)
    n_ref[...] = normed
    q_ref[...] = dot_nn(normed, wq_ref[...]).astype(BF16)
    kv_ref[...] = dot_nn(normed, wkv_ref[...]).astype(BF16)


def forward_kernel(sizes, tm, head_size, *refs):
    meta_ref, grad_ref, wo_ref, small_ref = refs[:4]
    x_refs, q_refs, kv_refs = (refs[4 + k * tm : 4 + (k + 1) * tm] for k in range(3))
    refs = refs[4 + 3 * tm :]
    out_ref = refs[0]
    send_refs = refs[1 : 1 + tm]
    q4_ref, k4_ref, v4_ref = refs[1 + tm : 4 + tm]
    q_ref, kv_ref, tail_s, ctx_s, e_s, h_s, u_s, gr_s, gc_s, taps_s = refs[4 + tm :]

    table = Layout(meta_ref, *sizes)
    me = table.me()
    local = table.blocks // tm
    width = out_ref.shape[1]
    hq = q_ref.shape[1]
    share = q4_ref.shape[1]
    half = tm // 2

    for ref in (q_ref, kv_ref):
        ref[: PAD * BLOCK] = jnp.zeros((PAD * BLOCK, ref.shape[1]), BF16)
    tail_s[:HALO] = jnp.zeros((HALO, width), BF16)
    for m in range(tm):
        for j in range(local):
            b = table.block_of((me ^ m) * local + j)
            here = slice(j * BLOCK, (j + 1) * BLOCK)
            q_ref[row_at(b)] = q_refs[m][here]
            kv_ref[row_at(b)] = kv_refs[m][here]
            after = pl.ds(pl.multiple_of((b + 1) * HALO, HALO), HALO)
            tail_s[after] = x_refs[m][(j + 1) * BLOCK - HALO : (j + 1) * BLOCK]

    lead = pl.multiple_of((me % half) * share, share)
    q4_ref[...] = q_ref[:, pl.ds(lead, share)]
    k4_ref[...] = kv_ref[:, pl.ds(lead, share)]
    v4_ref[...] = kv_ref[:, pl.ds(pl.multiple_of(hq + lead, share), share)]
    for j in range(KERNEL):
        taps_s[j * SUB : (j + 1) * SUB] = jnp.broadcast_to(small_ref[j : j + 1], (SUB, width))

    mid_heads = 256 // BLOCK
    mid_f = diag_mask(mid_heads, BLOCK, head_size)
    mid_b = mid_f.astype(BF16)
    side_f = diag_mask(HEADS, HALO, head_size)
    side_b = side_f.astype(BF16)

    own = [table.block_of(me * local + i) for i in range(local)]
    keep = [jnp.where(table.position(c) >= 1, 1.0, 0.0).astype(F32) for c in own]
    for i, c in enumerate(own):
        for blk, shift, count, put in ((c - 1, HALO, HALO, 0), (c, 0, BLOCK, HALO)):
            reach = table.reach(blk)
            win = row_at(blk - LC, SPAN)
            at = row_at(blk, count, shift)
            if count == BLOCK:
                groups, mask_f, mask_b = HEADS // mid_heads, mid_f, mid_b
            else:
                groups, mask_f, mask_b = 1, side_f, side_b
            wide = hq // groups
            for g in range(groups):
                cols = slice(g * wide, (g + 1) * wide)
                vcols = slice(hq + g * wide, hq + (g + 1) * wide)
                probs, _ = window_probs(
                    spread(q_ref[at, cols], mask_b), kv_ref[win, cols], reach, head_size
                )
                full = dot_tn(probs.astype(BF16), kv_ref[win, vcols])
                ctx_s[i * ROWS + put : i * ROWS + put + count, cols] = fold_heads(
                    full, mask_f, count
                ).astype(BF16)

    gain = small_ref[KERNEL + 1 : KERNEL + 2]
    product = dot_nn(ctx_s[...], wo_ref[...])
    scales = []
    for i, c in enumerate(own):
        here = slice(i * ROWS, (i + 1) * ROWS)
        tail = tail_s[pl.ds(pl.multiple_of(c * HALO, HALO), HALO)]
        rows = jnp.concatenate([tail, x_refs[0][i * BLOCK : (i + 1) * BLOCK]], axis=0)
        hidden = rows.astype(F32) + product[here]
        unit, inv = norm_stats(hidden)
        conv_in = (unit * gain).astype(BF16).astype(F32)
        e_s[i * ROWS : i * ROWS + HALO] = conv_in[:HALO] * keep[i]
        e_s[i * ROWS + HALO : (i + 1) * ROWS] = conv_in[HALO:]
        h_s[i * BLOCK : (i + 1) * BLOCK] = hidden[HALO:]
        u_s[here] = unit
        scales.append(inv)

    groups = BLOCK // SUB

    def conv(k, carry):
        cols = pl.ds(pl.multiple_of(k * LANES, LANES), LANES)
        bias = jnp.broadcast_to(small_ref[KERNEL : KERNEL + 1, cols], (SUB, LANES))
        taps = lambda j: taps_s[j * SUB : (j + 1) * SUB, cols]
        for i in range(local):
            ext = e_s[i * ROWS : (i + 1) * ROWS, cols]
            acc = [bias] * groups
            for s in range(SUB):
                reps = (KERNEL - s + SUB - 1) // SUB
                moved = ext[s + 2 : s + 2 + BLOCK + SUB * (reps - 1)]
                for a in range(reps):
                    tap = taps(SUB * a + s)
                    for r in range(groups):
                        piece = moved[(a + r) * SUB : (a + r + 1) * SUB]
                        acc[r] = acc[r] + tap * piece
            mixed = jnp.concatenate(acc, axis=0)
            gate = 0.5 * jnp.tanh(0.5 * mixed) + 0.5
            rows = slice(i * BLOCK, (i + 1) * BLOCK)
            out_ref[rows, cols] = (h_s[rows, cols] + mixed * gate).astype(BF16)
            slope = gate * (1.0 + mixed * (1.0 - gate))
            gm = grad_ref[rows, cols].astype(F32) * slope
            zeros = jnp.zeros((HALO, LANES), F32)
            padded = jnp.concatenate([zeros, gm, zeros], axis=0)
            back = [None] * (ROWS // SUB)
            low = HALO // SUB - 1
            for s in range(SUB):
                reps = (KERNEL - s + SUB - 1) // SUB
                start = low if s else low + 1
                moved = padded[start * SUB + s : ROWS + s]
                for a in range(reps):
                    tap = taps(KERNEL - 1 - SUB * a - s)
                    for g in range(start, ROWS // SUB):
                        r = g - a
                        piece = tap * moved[(g - start) * SUB : (g - start + 1) * SUB]
                        back[r] = piece if back[r] is None else back[r] + piece
            for r in range(ROWS // SUB):
                scale = keep[i] if r < HALO // SUB else 1.0
                gr_s[i * ROWS + r * SUB : i * ROWS + (r + 1) * SUB, cols] = back[r] * scale
        return carry

    lax.fori_loop(0, width // LANES, conv, 0)

    for i in range(local):
        here = slice(i * ROWS, (i + 1) * ROWS)
        scaled = gr_s[here] * gain
        unit = u_s[here]
        first = jnp.mean(scaled, axis=-1, keepdims=True)
        second = jnp.mean(scaled * unit, axis=-1, keepdims=True)
        back = scales[i] * (scaled - first - unit * second)
        own_grad = grad_ref[i * BLOCK : (i + 1) * BLOCK].astype(F32) + back[HALO:]
        gc_s[i * ROWS : i * ROWS + HALO] = back[:HALO].astype(BF16)
        gc_s[i * ROWS + HALO : (i + 1) * ROWS] = own_grad.astype(BF16)
    for m in range(tm):
        at = pl.ds(pl.multiple_of(((me ^ m) % half) * share, share), share)
        send_refs[m][...] = dot_nt(gc_s[...], wo_ref[at]).astype(BF16)


def probs_kernel(sizes, head_size, meta_ref, q4_ref, k4_ref, p_ref, d_ref):
    table = Layout(meta_ref, *sizes)
    heads = q4_ref.shape[1] // head_size
    mask_b = diag_mask(heads, BLOCK, head_size).astype(BF16)
    for c in range(table.blocks):
        own = slice((c + PAD) * BLOCK, (c + PAD + 1) * BLOCK)
        win = slice((c + PAD - LC) * BLOCK, (c + PAD + 1) * BLOCK)
        diag_q = spread(q4_ref[own], mask_b)
        probs, unit = window_probs(diag_q, k4_ref[win], table.reach(c), head_size)
        p_ref[c] = probs
        d_ref[c] = (1.0 - unit * unit) * (1.0 / math.sqrt(head_size))


def backward_kernel(sizes, tm, part, head_size, *refs):
    meta_ref, q4_ref, v4_ref, p_ref, d_ref = refs[:5]
    n_refs = refs[5 : 5 + tm]
    g_refs = refs[5 + tm : 5 + 2 * tm]
    out_refs = refs[5 + 2 * tm : -3]
    gt_s, t_s, full_s = refs[-3:]
    table = Layout(meta_ref, *sizes)
    me = table.me()
    blocks = table.blocks
    local = blocks // tm
    share = q4_ref.shape[1]
    mask_b = diag_mask(share // head_size, BLOCK, head_size).astype(BF16)

    places = [(m, j, table.block_of((me ^ m) * local + j)) for m in range(tm) for j in range(local)]
    for m, j, b in places:
        gt_s[row_at(b)] = g_refs[m][j * ROWS + HALO : (j + 1) * ROWS].astype(F32)
    gt_s[(PAD - 1) * BLOCK : PAD * BLOCK] = jnp.zeros((BLOCK, share), F32)
    for m, j, b in places:
        at = row_at(b, HALO, -HALO)
        gt_s[at] = gt_s[at] + g_refs[m][j * ROWS : j * ROWS + HALO].astype(F32)
    t_s[...] = jnp.zeros(t_s.shape, F32)

    def spans(c):
        own = slice((c + PAD) * BLOCK, (c + PAD + 1) * BLOCK)
        win = slice((c + PAD - LC) * BLOCK, (c + PAD + 1) * BLOCK)
        return own, win, spread(gt_s[own].astype(BF16), mask_b)

    @pl.when(me >= tm // 2)
    def _():
        for c in range(blocks):
            own, win, diag_g = spans(c)
            t_s[win] = t_s[win] + dot_nn(p_ref[c].astype(BF16), diag_g)

    @pl.when(me < tm // 2)
    def _():
        for c in range(blocks):
            own, win, diag_g = spans(c)
            grad_probs = dot_nt(v4_ref[win], diag_g)
            probs = p_ref[c]
            delta = jnp.sum(probs * grad_probs, axis=0, keepdims=True)
            grad_raw = probs * (grad_probs - delta) * d_ref[c]
            t_s[win] = t_s[win] + dot_nn(grad_raw.astype(BF16), spread(q4_ref[own], mask_b))

    terms = jnp.concatenate([t_s[row_at(b)].astype(BF16) for _, _, b in places], axis=0)
    full = dot_tn(terms, jnp.concatenate([ref[...] for ref in n_refs], axis=0))
    if len(out_refs) == 1:
        out_refs[0][...] = full.astype(BF16)
        return
    full_s[...] = full
    chip, core = table.dp() // 2, table.dp() % 2
    for q in range(out_refs[0].shape[1] // part):
        for ref, side in zip(out_refs, (core, 1 - core)):
            at = pl.ds(pl.multiple_of(((chip ^ q) * 2 + side) * part, part), part)
            ref[:, q * part : (q + 1) * part] = full_s[:, at].astype(ref.dtype)


def pair_kernel(kept_ref, got_ref, *out_refs):
    part = out_refs[0].shape[1]
    for q, ref in enumerate(out_refs):
        cols = slice(q * part, (q + 1) * part)
        ref[...] = (kept_ref[:, cols] + got_ref[:, cols].astype(F32)).astype(ref.dtype)


def sum_kernel(*refs):
    total = refs[0][...].astype(F32)
    for ref in refs[1:-1]:
        total = total + ref[...].astype(F32)
    refs[-1][...] = total.T


def on_device(
    frames,
    out_grad,
    norm1_gain,
    w_query,
    w_kv,
    w_out,
    norm2_gain,
    conv_kernel,
    conv_bias,
    utt_blocks,
    block_slot,
    left_count,
):
    tm = lax.axis_size("tm")
    dp = lax.axis_size("dp")
    rows, width = frames.shape
    blocks = block_slot.shape[1]
    utts = utt_blocks.shape[1]
    sizes = (utts, blocks)
    local = rows // BLOCK
    hq = w_query.shape[1]
    head_size = hq // HEADS
    kv_width = w_kv.shape[1]
    share = kv_width // tm
    padded = (blocks + PAD) * BLOCK

    def swap(value, axis, size, m):
        return lax.ppermute(value, axis, [(i, i ^ m) for i in range(size)])

    meta = jnp.concatenate(
        [
            lax.axis_index("tm").astype(jnp.int32).reshape(1, 1),
            lax.axis_index("dp").astype(jnp.int32).reshape(1, 1),
            utt_blocks,
            block_slot,
            left_count,
        ],
        axis=1,
    )
    small = jnp.concatenate(
        [conv_kernel, conv_bias.reshape(1, -1), norm2_gain.reshape(1, -1)], axis=0
    )

    smem = pl.BlockSpec(memory_space=pltpu.SMEM)
    vmem = pl.BlockSpec(memory_space=pltpu.VMEM)
    shape = jax.ShapeDtypeStruct

    x, normed, queries, keys_values = {}, {}, {}, {}
    made = [shape((rows, w), BF16) for w in (width, hq, kv_width, width)]

    def project(m, parts):
        two = len(parts) == 2
        outs = pl.pallas_call(
            functools.partial(project_kernel, (1, 2) if two else ()),
            out_shape=made if two else made[:3],
            in_specs=[smem] + [vmem] * (3 + len(parts)),
            out_specs=[vmem] * (4 if two else 3),
            compiler_params=pltpu.CompilerParams(vmem_limit_bytes=32 << 20),
            cost_estimate=pl.CostEstimate(
                flops=2 * rows * width * (hq + kv_width), bytes_accessed=4 << 20, transcendentals=0
            ),
            name=f"project_rows_{m}",
        )(meta, norm1_gain.reshape(1, -1), w_query, w_kv, *parts)
        normed[m], queries[m], keys_values[m] = outs[:3]
        x[m] = outs[3] if two else parts[0]

    project(0, (frames,))
    if tm == 4:
        facing = swap(frames, "tm", tm, 2)
        beside = swap(frames, "tm", tm, 1)
        later, passed, normed[0] = lax.optimization_barrier((frames, facing, normed[0]))
        crossed = lax.ppermute(later, "tm", [(1, 2), (2, 1)])
        handed = lax.ppermute(passed, "tm", [(1, 0), (2, 3)])
        project(2, (passed,))
        project(1, (beside,))
        project(3, (crossed, handed))
    else:
        for m in range(1, tm):
            project(m, (swap(frames, "tm", tm, m),))

    def by_m(arrays):
        return [arrays[m] for m in range(tm)]

    own_rows = local * ROWS
    results = pl.pallas_call(
        functools.partial(forward_kernel, sizes, tm, head_size),
        out_shape=[shape((rows, width), BF16)]
        + [shape((own_rows, share), BF16)] * tm
        + [shape((padded, share), BF16)] * 3,
        in_specs=[smem] + [vmem] * (3 + 3 * tm),
        out_specs=[vmem] * (tm + 4),
        scratch_shapes=[
            pltpu.VMEM((padded, hq), BF16),
            pltpu.VMEM((padded, kv_width), BF16),
            pltpu.VMEM(((blocks + 1) * HALO, width), BF16),
            pltpu.VMEM((own_rows, hq), BF16),
            pltpu.VMEM((own_rows, width), F32),
            pltpu.VMEM((rows, width), F32),
            pltpu.VMEM((own_rows, width), F32),
            pltpu.VMEM((own_rows, width), F32),
            pltpu.VMEM((own_rows, width), BF16),
            pltpu.VMEM((KERNEL * SUB, width), F32),
        ],
        compiler_params=pltpu.CompilerParams(vmem_limit_bytes=32 << 20),
        name="forward_pass",
    )(meta, out_grad, w_out, small, *by_m(x), *by_m(queries), *by_m(keys_values))
    layer_out = results[0]
    sends = results[1 : 1 + tm]
    q4, k4, v4 = results[1 + tm :]
    got = [sends[0]] + [swap(sends[m], "tm", tm, m) for m in range(1, tm)]

    pair_width = share // head_size * BLOCK
    probs, slopes = pl.pallas_call(
        functools.partial(probs_kernel, sizes, head_size),
        out_shape=[shape((blocks, SPAN, pair_width), F32)] * 2,
        in_specs=[smem] + [vmem] * 2,
        out_specs=[vmem] * 2,
        compiler_params=pltpu.CompilerParams(vmem_limit_bytes=24 << 20),
        name="window_probs",
        cost_estimate=pl.CostEstimate(
            flops=2 * 10**9, bytes_accessed=4 * 10**6, transcendentals=800000
        ),
    )(meta, q4, k4)

    direct = dp <= 8
    half_width = width // 2
    if direct:
        piece_shapes = [shape((share, half_width), F32), shape((share, half_width), BF16)]
    else:
        piece_shapes = [shape((share, width), BF16)]
    pieces = pl.pallas_call(
        functools.partial(backward_kernel, sizes, tm, width // dp, head_size),
        out_shape=piece_shapes,
        in_specs=[smem] + [vmem] * (4 + 2 * tm),
        out_specs=[vmem] * len(piece_shapes),
        scratch_shapes=[
            pltpu.VMEM((padded, share), F32),
            pltpu.VMEM((padded, share), F32),
            pltpu.VMEM((share, width), F32),
        ],
        compiler_params=pltpu.CompilerParams(vmem_limit_bytes=32 << 20),
        name="key_value_terms",
    )(meta, q4, v4, probs, slopes, *by_m(normed), *got)

    if direct:
        kept, away = pieces
        arrived = swap(away, "dp", dp, 1)
        chips = dp // 2
        part = width // dp
        summed = pl.pallas_call(
            pair_kernel,
            out_shape=[shape((share, part), BF16)] * chips,
            in_specs=[vmem] * 2,
            out_specs=[vmem] * chips,
            name="sum_pair",
        )(kept, arrived)
        terms = [summed[0]] + [swap(summed[q], "dp", dp, 2 * q) for q in range(1, chips)]
    else:
        terms = [lax.psum_scatter(pieces[0], "dp", scatter_dimension=1, tiled=True)]
    kv_grad = pl.pallas_call(
        sum_kernel,
        out_shape=shape((width // dp, share), F32),
        in_specs=[vmem] * len(terms),
        out_specs=vmem,
        name="sum_groups",
    )(*terms)
    return layer_out, kv_grad


def solution(mesh):
    return jax.shard_map(
        on_device,
        mesh=mesh,
        in_specs=(
            P(("dp", "tm"), None),
            P(("dp", "tm"), None),
            P(),
            P(),
            P(),
            P(),
            P(),
            P(),
            P(),
            P("dp", None),
            P("dp", None),
            P("dp", None),
        ),
        out_specs=(P(("dp", "tm"), None), P("dp", "tm")),
        check_vma=False,
    )
```

```python
import functools
import math

import jax
import jax.numpy as jnp
from jax import lax
from jax.experimental import pallas as pl
from jax.experimental.pallas import tpu as pltpu
from jax.sharding import PartitionSpec as P

HEADS = 8
KERNEL = 31
BLOCK = 64
LC = 2
SPAN = (LC + 1) * BLOCK
HALO = 32
ROWS = HALO + BLOCK
PAD = LC + 1
EPSILON = 1e-05
SOFT_CAP = 4.0
LANES = 128
SUB = 8

BF16 = jnp.bfloat16
F32 = jnp.float32


def dot_nn(a, b):
    return lax.dot_general(a, b, (((1,), (0,)), ((), ())), preferred_element_type=F32)


def dot_nt(a, b):
    return lax.dot_general(a, b, (((1,), (1,)), ((), ())), preferred_element_type=F32)


def dot_tn(a, b):
    return lax.dot_general(a, b, (((0,), (0,)), ((), ())), preferred_element_type=F32)


def norm_stats(values):
    row_mean = jnp.mean(values, axis=-1, keepdims=True)
    centred = values - row_mean
    scale_inv = lax.rsqrt(jnp.mean(centred * centred, axis=-1, keepdims=True) + EPSILON)
    return centred * scale_inv, scale_inv


class Layout:
    def __init__(self, meta_ref, utts, blocks):
        self.ref, self.utts, self.blocks = meta_ref, utts, blocks

    def me(self):
        return self.ref[0, 0]

    def dp(self):
        return self.ref[0, 1]

    def block_of(self, slot):
        found = jnp.int32(0)
        for b in range(self.blocks):
            found = jnp.where(self.ref[0, 2 + self.utts + b] == slot, jnp.int32(b), found)
        return found

    def position(self, block):
        start = jnp.int32(0)
        first = jnp.int32(0)
        for u in range(self.utts):
            first = jnp.where(block >= start, start, first)
            start = start + self.ref[0, 2 + u]
        return block - first

    def reach(self, block):
        safe = jnp.maximum(block, 0)
        left = self.ref[0, 2 + self.utts + self.blocks + safe]
        return jnp.minimum(left, self.position(safe))


def row_at(block, count=BLOCK, shift=0):
    return pl.ds(pl.multiple_of((block + PAD) * BLOCK + shift, math.gcd(BLOCK, shift)), count)


def diag_mask(heads, rows, head_size):
    shape = (heads * rows, heads * head_size)
    row_head = lax.broadcasted_iota(jnp.int32, shape, 0) // rows
    col_head = lax.broadcasted_iota(jnp.int32, shape, 1) // head_size
    return jnp.where(row_head == col_head, 1.0, 0.0).astype(F32)


def spread(rows, mask_b):
    copies = mask_b.shape[0] // rows.shape[0]
    return jnp.concatenate([rows] * copies, axis=0) * mask_b


def fold_heads(full, mask_f, rows):
    kept = full * mask_f
    total = kept[:rows]
    for h in range(1, full.shape[0] // rows):
        total = total + kept[h * rows : (h + 1) * rows]
    return total


def window_probs(diag_q, k_win, reach, head_size):
    raw = dot_nt(k_win, diag_q)
    unit = jnp.tanh(raw * (1.0 / (SOFT_CAP * math.sqrt(head_size))))
    exped = jnp.exp(SOFT_CAP * unit)
    parts = []
    for w in range(LC):
        ok = jnp.where(reach >= LC - w, 1.0, 0.0).astype(F32)
        parts.append(exped[w * BLOCK : (w + 1) * BLOCK] * ok)
    parts.append(exped[LC * BLOCK :])
    exped = jnp.concatenate(parts, axis=0)
    total = jnp.sum(exped, axis=0, keepdims=True)
    return exped * (1.0 / total), unit


def taps_kernel(small_ref, taps_ref):
    for j in range(KERNEL):
        rows = jnp.broadcast_to(small_ref[j : j + 1], (SUB, small_ref.shape[1]))
        taps_ref[j * SUB : (j + 1) * SUB] = rows


def project_kernel(crossed_at, *refs):
    meta_ref, g1_ref, wq_ref, wkv_ref = refs[:4]
    if crossed_at:
        crossed_ref, handed_ref, n_ref, q_ref, kv_ref, x_ref = refs[4:]
        me = meta_ref[0, 0]
        middle = functools.reduce(jnp.logical_or, [me == t for t in crossed_at])
        rows = jnp.where(middle, crossed_ref[...], handed_ref[...])
        x_ref[...] = rows
    else:
        x_ref, n_ref, q_ref, kv_ref = refs[4:]
        rows = x_ref[...]
    unit, _ = norm_stats(rows.astype(F32))
    normed = (unit * g1_ref[...]).astype(BF16)
    n_ref[...] = normed
    q_ref[...] = dot_nn(normed, wq_ref[...]).astype(BF16)
    kv_ref[...] = dot_nn(normed, wkv_ref[...]).astype(BF16)


def forward_kernel(sizes, tm, head_size, *refs):
    meta_ref, grad_ref, wo_ref, small_ref, taps_ref = refs[:5]
    x_refs, q_refs, kv_refs = (refs[5 + k * tm : 5 + (k + 1) * tm] for k in range(3))
    refs = refs[5 + 3 * tm :]
    out_ref = refs[0]
    send_refs = refs[1 : 1 + tm]
    q_ref, kv_ref, tail_s, ctx_s, e_s, h_s, u_s, gr_s, gc_s = refs[1 + tm :]

    table = Layout(meta_ref, *sizes)
    me = table.me()
    local = table.blocks // tm
    width = out_ref.shape[1]
    hq = q_ref.shape[1]
    share = send_refs[0].shape[1]
    half = tm // 2

    for ref in (q_ref, kv_ref):
        ref[: PAD * BLOCK] = jnp.zeros((PAD * BLOCK, ref.shape[1]), BF16)
    tail_s[:HALO] = jnp.zeros((HALO, width), BF16)
    for m in range(tm):
        for j in range(local):
            b = table.block_of((me ^ m) * local + j)
            here = slice(j * BLOCK, (j + 1) * BLOCK)
            q_ref[row_at(b)] = q_refs[m][here]
            kv_ref[row_at(b)] = kv_refs[m][here]
            after = pl.ds(pl.multiple_of((b + 1) * HALO, HALO), HALO)
            tail_s[after] = x_refs[m][(j + 1) * BLOCK - HALO : (j + 1) * BLOCK]

    mid_heads = 256 // BLOCK
    mid_f = diag_mask(mid_heads, BLOCK, head_size)
    mid_b = mid_f.astype(BF16)
    side_f = diag_mask(HEADS, HALO, head_size)
    side_b = side_f.astype(BF16)

    own = [table.block_of(me * local + i) for i in range(local)]
    keep = [jnp.where(table.position(c) >= 1, 1.0, 0.0).astype(F32) for c in own]
    for i, c in enumerate(own):
        for blk, shift, count, put in ((c - 1, HALO, HALO, 0), (c, 0, BLOCK, HALO)):
            reach = table.reach(blk)
            win = row_at(blk - LC, SPAN)
            at = row_at(blk, count, shift)
            if count == BLOCK:
                groups, mask_f, mask_b = HEADS // mid_heads, mid_f, mid_b
            else:
                groups, mask_f, mask_b = 1, side_f, side_b
            wide = hq // groups
            for g in range(groups):
                cols = slice(g * wide, (g + 1) * wide)
                vcols = slice(hq + g * wide, hq + (g + 1) * wide)
                probs, _ = window_probs(
                    spread(q_ref[at, cols], mask_b), kv_ref[win, cols], reach, head_size
                )
                full = dot_tn(probs.astype(BF16), kv_ref[win, vcols])
                ctx_s[i * ROWS + put : i * ROWS + put + count, cols] = fold_heads(
                    full, mask_f, count
                ).astype(BF16)

    gain = small_ref[KERNEL + 1 : KERNEL + 2]
    product = dot_nn(ctx_s[...], wo_ref[...])
    scales = []
    for i, c in enumerate(own):
        here = slice(i * ROWS, (i + 1) * ROWS)
        tail = tail_s[pl.ds(pl.multiple_of(c * HALO, HALO), HALO)]
        rows = jnp.concatenate([tail, x_refs[0][i * BLOCK : (i + 1) * BLOCK]], axis=0)
        hidden = rows.astype(F32) + product[here]
        unit, inv = norm_stats(hidden)
        conv_in = (unit * gain).astype(BF16).astype(F32)
        e_s[i * ROWS : i * ROWS + HALO] = conv_in[:HALO] * keep[i]
        e_s[i * ROWS + HALO : (i + 1) * ROWS] = conv_in[HALO:]
        h_s[i * BLOCK : (i + 1) * BLOCK] = hidden[HALO:]
        u_s[here] = unit
        scales.append(inv)

    groups = BLOCK // SUB

    def conv(k, carry):
        cols = pl.ds(pl.multiple_of(k * LANES, LANES), LANES)
        bias = jnp.broadcast_to(small_ref[KERNEL : KERNEL + 1, cols], (SUB, LANES))
        taps = lambda j: taps_ref[j * SUB : (j + 1) * SUB, cols]
        for i in range(local):
            ext = e_s[i * ROWS : (i + 1) * ROWS, cols]
            acc = [bias] * groups
            for s in range(SUB):
                reps = (KERNEL - s + SUB - 1) // SUB
                moved = ext[s + 2 : s + 2 + BLOCK + SUB * (reps - 1)]
                for a in range(reps):
                    tap = taps(SUB * a + s)
                    for r in range(groups):
                        piece = moved[(a + r) * SUB : (a + r + 1) * SUB]
                        acc[r] = acc[r] + tap * piece
            mixed = jnp.concatenate(acc, axis=0)
            gate = 0.5 * jnp.tanh(0.5 * mixed) + 0.5
            rows = slice(i * BLOCK, (i + 1) * BLOCK)
            out_ref[rows, cols] = (h_s[rows, cols] + mixed * gate).astype(BF16)
            slope = gate * (1.0 + mixed * (1.0 - gate))
            gm = grad_ref[rows, cols].astype(F32) * slope
            zeros = jnp.zeros((HALO, LANES), F32)
            padded = jnp.concatenate([zeros, gm, zeros], axis=0)
            back = [None] * (ROWS // SUB)
            low = HALO // SUB - 1
            for s in range(SUB):
                reps = (KERNEL - s + SUB - 1) // SUB
                start = low if s else low + 1
                moved = padded[start * SUB + s : ROWS + s]
                for a in range(reps):
                    tap = taps(KERNEL - 1 - SUB * a - s)
                    for g in range(start, ROWS // SUB):
                        r = g - a
                        piece = tap * moved[(g - start) * SUB : (g - start + 1) * SUB]
                        back[r] = piece if back[r] is None else back[r] + piece
            for r in range(ROWS // SUB):
                scale = keep[i] if r < HALO // SUB else 1.0
                gr_s[i * ROWS + r * SUB : i * ROWS + (r + 1) * SUB, cols] = back[r] * scale
        return carry

    lax.fori_loop(0, width // LANES, conv, 0)

    for i in range(local):
        here = slice(i * ROWS, (i + 1) * ROWS)
        scaled = gr_s[here] * gain
        unit = u_s[here]
        first = jnp.mean(scaled, axis=-1, keepdims=True)
        second = jnp.mean(scaled * unit, axis=-1, keepdims=True)
        back = scales[i] * (scaled - first - unit * second)
        own_grad = grad_ref[i * BLOCK : (i + 1) * BLOCK].astype(F32) + back[HALO:]
        gc_s[i * ROWS : i * ROWS + HALO] = back[:HALO].astype(BF16)
        gc_s[i * ROWS + HALO : (i + 1) * ROWS] = own_grad.astype(BF16)
    for m in range(tm):
        at = pl.ds(pl.multiple_of(((me ^ m) % half) * share, share), share)
        send_refs[m][...] = dot_nt(gc_s[...], wo_ref[at]).astype(BF16)


def probs_kernel(sizes, tm, head_size, meta_ref, *refs):
    q_refs, kv_refs = refs[:tm], refs[tm : 2 * tm]
    q4_ref, v4_ref, p_ref, d_ref, k4_ref = refs[2 * tm :]
    table = Layout(meta_ref, *sizes)
    me = table.me()
    local = table.blocks // tm
    hq = q_refs[0].shape[1]
    share = q4_ref.shape[1]
    lead = pl.multiple_of((me % (tm // 2)) * share, share)
    for ref in (k4_ref, v4_ref):
        ref[: PAD * BLOCK] = jnp.zeros((PAD * BLOCK, share), BF16)
    for m in range(tm):
        for j in range(local):
            at = row_at(table.block_of((me ^ m) * local + j))
            here = slice(j * BLOCK, (j + 1) * BLOCK)
            q4_ref[at] = q_refs[m][here, pl.ds(lead, share)]
            k4_ref[at] = kv_refs[m][here, pl.ds(lead, share)]
            v4_ref[at] = kv_refs[m][here, pl.ds(pl.multiple_of(hq + lead, share), share)]
    heads = share // head_size
    mask_b = diag_mask(heads, BLOCK, head_size).astype(BF16)
    for c in range(table.blocks):
        own = slice((c + PAD) * BLOCK, (c + PAD + 1) * BLOCK)
        win = slice((c + PAD - LC) * BLOCK, (c + PAD + 1) * BLOCK)
        diag_q = spread(q4_ref[own], mask_b)
        probs, unit = window_probs(diag_q, k4_ref[win], table.reach(c), head_size)
        p_ref[c] = probs
        d_ref[c] = (1.0 - unit * unit) * (1.0 / math.sqrt(head_size))


def backward_kernel(sizes, tm, part, head_size, *refs):
    meta_ref, q4_ref, v4_ref, p_ref, d_ref = refs[:5]
    n_refs = refs[5 : 5 + tm]
    g_refs = refs[5 + tm : 5 + 2 * tm]
    out_refs = refs[5 + 2 * tm : -3]
    gt_s, t_s, full_s = refs[-3:]
    table = Layout(meta_ref, *sizes)
    me = table.me()
    blocks = table.blocks
    local = blocks // tm
    share = q4_ref.shape[1]
    mask_b = diag_mask(share // head_size, BLOCK, head_size).astype(BF16)

    places = [(m, j, table.block_of((me ^ m) * local + j)) for m in range(tm) for j in range(local)]
    for m, j, b in places:
        gt_s[row_at(b)] = g_refs[m][j * ROWS + HALO : (j + 1) * ROWS].astype(F32)
    gt_s[(PAD - 1) * BLOCK : PAD * BLOCK] = jnp.zeros((BLOCK, share), F32)
    for m, j, b in places:
        at = row_at(b, HALO, -HALO)
        gt_s[at] = gt_s[at] + g_refs[m][j * ROWS : j * ROWS + HALO].astype(F32)
    t_s[...] = jnp.zeros(t_s.shape, F32)

    def spans(c):
        own = slice((c + PAD) * BLOCK, (c + PAD + 1) * BLOCK)
        win = slice((c + PAD - LC) * BLOCK, (c + PAD + 1) * BLOCK)
        return own, win, spread(gt_s[own].astype(BF16), mask_b)

    @pl.when(me >= tm // 2)
    def _():
        for c in range(blocks):
            own, win, diag_g = spans(c)
            t_s[win] = t_s[win] + dot_nn(p_ref[c].astype(BF16), diag_g)

    @pl.when(me < tm // 2)
    def _():
        for c in range(blocks):
            own, win, diag_g = spans(c)
            grad_probs = dot_nt(v4_ref[win], diag_g)
            probs = p_ref[c]
            delta = jnp.sum(probs * grad_probs, axis=0, keepdims=True)
            grad_raw = probs * (grad_probs - delta) * d_ref[c]
            t_s[win] = t_s[win] + dot_nn(grad_raw.astype(BF16), spread(q4_ref[own], mask_b))

    terms = jnp.concatenate([t_s[row_at(b)].astype(BF16) for _, _, b in places], axis=0)
    full = dot_tn(terms, jnp.concatenate([ref[...] for ref in n_refs], axis=0))
    if len(out_refs) == 1:
        out_refs[0][...] = full.astype(BF16)
        return
    full_s[...] = full
    chip, core = table.dp() // 2, table.dp() % 2
    for q in range(out_refs[0].shape[1] // part):
        for ref, side in zip(out_refs, (core, 1 - core)):
            at = pl.ds(pl.multiple_of(((chip ^ q) * 2 + side) * part, part), part)
            ref[:, q * part : (q + 1) * part] = full_s[:, at].astype(ref.dtype)


def pair_kernel(kept_ref, got_ref, *out_refs):
    part = out_refs[0].shape[1]
    for q, ref in enumerate(out_refs):
        cols = slice(q * part, (q + 1) * part)
        ref[...] = (kept_ref[:, cols] + got_ref[:, cols].astype(F32)).astype(ref.dtype)


def sum_kernel(*refs):
    total = refs[0][...].astype(F32)
    for ref in refs[1:-1]:
        total = total + ref[...].astype(F32)
    refs[-1][...] = total.T


def on_device(
    frames,
    out_grad,
    norm1_gain,
    w_query,
    w_kv,
    w_out,
    norm2_gain,
    conv_kernel,
    conv_bias,
    utt_blocks,
    block_slot,
    left_count,
):
    tm = lax.axis_size("tm")
    dp = lax.axis_size("dp")
    rows, width = frames.shape
    blocks = block_slot.shape[1]
    utts = utt_blocks.shape[1]
    sizes = (utts, blocks)
    local = rows // BLOCK
    hq = w_query.shape[1]
    head_size = hq // HEADS
    kv_width = w_kv.shape[1]
    share = kv_width // tm
    padded = (blocks + PAD) * BLOCK

    def swap(value, axis, size, m):
        return lax.ppermute(value, axis, [(i, i ^ m) for i in range(size)])

    meta = jnp.concatenate(
        [
            lax.axis_index("tm").astype(jnp.int32).reshape(1, 1),
            lax.axis_index("dp").astype(jnp.int32).reshape(1, 1),
            utt_blocks,
            block_slot,
            left_count,
        ],
        axis=1,
    )
    small = jnp.concatenate(
        [conv_kernel, conv_bias.reshape(1, -1), norm2_gain.reshape(1, -1)], axis=0
    )

    smem = pl.BlockSpec(memory_space=pltpu.SMEM)
    vmem = pl.BlockSpec(memory_space=pltpu.VMEM)
    shape = jax.ShapeDtypeStruct

    taps = pl.pallas_call(
        taps_kernel,
        out_shape=shape((KERNEL * SUB, width), F32),
        in_specs=[vmem],
        out_specs=vmem,
        compiler_params=pltpu.CompilerParams(vmem_limit_bytes=8 << 20),
        cost_estimate=pl.CostEstimate(flops=10**6, bytes_accessed=1 << 20, transcendentals=0),
        name="spread_taps",
    )(small)

    x, normed, queries, keys_values = {}, {}, {}, {}
    made = [shape((rows, w), BF16) for w in (width, hq, kv_width, width)]

    def project(m, parts):
        two = len(parts) == 2
        outs = pl.pallas_call(
            functools.partial(project_kernel, (1, 2) if two else ()),
            out_shape=made if two else made[:3],
            in_specs=[smem] + [vmem] * (3 + len(parts)),
            out_specs=[vmem] * (4 if two else 3),
            compiler_params=pltpu.CompilerParams(vmem_limit_bytes=32 << 20),
            cost_estimate=pl.CostEstimate(
                flops=2 * rows * width * (hq + kv_width), bytes_accessed=4 << 20, transcendentals=0
            ),
            name=f"project_rows_{m}",
        )(meta, norm1_gain.reshape(1, -1), w_query, w_kv, *parts)
        normed[m], queries[m], keys_values[m] = outs[:3]
        x[m] = outs[3] if two else parts[0]

    project(0, (frames,))
    if tm == 4:
        facing = swap(frames, "tm", tm, 2)
        beside = swap(frames, "tm", tm, 1)
        later, passed, normed[0], taps = lax.optimization_barrier(
            (frames, facing, normed[0], taps)
        )
        crossed = lax.ppermute(later, "tm", [(1, 2), (2, 1)])
        handed = lax.ppermute(passed, "tm", [(1, 0), (2, 3)])
        project(2, (passed,))
        project(1, (beside,))
        project(3, (crossed, handed))
    else:
        for m in range(1, tm):
            project(m, (swap(frames, "tm", tm, m),))

    def by_m(arrays):
        return [arrays[m] for m in range(tm)]

    own_rows = local * ROWS
    results = pl.pallas_call(
        functools.partial(forward_kernel, sizes, tm, head_size),
        out_shape=[shape((rows, width), BF16)]
        + [shape((own_rows, share), BF16)] * tm,
        in_specs=[smem] + [vmem] * (4 + 3 * tm),
        out_specs=[vmem] * (tm + 1),
        scratch_shapes=[
            pltpu.VMEM((padded, hq), BF16),
            pltpu.VMEM((padded, kv_width), BF16),
            pltpu.VMEM(((blocks + 1) * HALO, width), BF16),
            pltpu.VMEM((own_rows, hq), BF16),
            pltpu.VMEM((own_rows, width), F32),
            pltpu.VMEM((rows, width), F32),
            pltpu.VMEM((own_rows, width), F32),
            pltpu.VMEM((own_rows, width), F32),
            pltpu.VMEM((own_rows, width), BF16),
        ],
        compiler_params=pltpu.CompilerParams(vmem_limit_bytes=32 << 20),
        name="forward_pass",
    )(meta, out_grad, w_out, small, taps, *by_m(x), *by_m(queries), *by_m(keys_values))
    layer_out = results[0]
    sends = results[1 : 1 + tm]
    got = [sends[0]] + [swap(sends[m], "tm", tm, m) for m in range(1, tm)]

    pair_width = share // head_size * BLOCK
    q4, v4, probs, slopes = pl.pallas_call(
        functools.partial(probs_kernel, sizes, tm, head_size),
        out_shape=[shape((padded, share), BF16)] * 2
        + [shape((blocks, SPAN, pair_width), F32)] * 2,
        in_specs=[smem] + [vmem] * (2 * tm),
        out_specs=[vmem] * 4,
        scratch_shapes=[pltpu.VMEM((padded, share), BF16)],
        compiler_params=pltpu.CompilerParams(vmem_limit_bytes=24 << 20),
        name="window_probs",
        cost_estimate=pl.CostEstimate(
            flops=2 * 10**9, bytes_accessed=4 * 10**6, transcendentals=800000
        ),
    )(meta, *by_m(queries), *by_m(keys_values))

    direct = dp <= 8
    half_width = width // 2
    if direct:
        piece_shapes = [shape((share, half_width), F32), shape((share, half_width), BF16)]
    else:
        piece_shapes = [shape((share, width), BF16)]
    pieces = pl.pallas_call(
        functools.partial(backward_kernel, sizes, tm, width // dp, head_size),
        out_shape=piece_shapes,
        in_specs=[smem] + [vmem] * (4 + 2 * tm),
        out_specs=[vmem] * len(piece_shapes),
        scratch_shapes=[
            pltpu.VMEM((padded, share), F32),
            pltpu.VMEM((padded, share), F32),
            pltpu.VMEM((share, width), F32),
        ],
        compiler_params=pltpu.CompilerParams(vmem_limit_bytes=32 << 20),
        name="key_value_terms",
    )(meta, q4, v4, probs, slopes, *by_m(normed), *got)

    if direct:
        kept, away = pieces
        arrived = swap(away, "dp", dp, 1)
        chips = dp // 2
        part = width // dp
        summed = pl.pallas_call(
            pair_kernel,
            out_shape=[shape((share, part), BF16)] * chips,
            in_specs=[vmem] * 2,
            out_specs=[vmem] * chips,
            compiler_params=pltpu.CompilerParams(vmem_limit_bytes=4 << 20),
            name="sum_pair",
        )(kept, arrived)
        terms = [summed[0]] + [swap(summed[q], "dp", dp, 2 * q) for q in range(1, chips)]
    else:
        terms = [lax.psum_scatter(pieces[0], "dp", scatter_dimension=1, tiled=True)]
    kv_grad = pl.pallas_call(
        sum_kernel,
        out_shape=shape((width // dp, share), F32),
        in_specs=[vmem] * len(terms),
        out_specs=vmem,
        compiler_params=pltpu.CompilerParams(vmem_limit_bytes=4 << 20),
        name="sum_groups",
    )(*terms)
    return layer_out, kv_grad


def solution(mesh):
    return jax.shard_map(
        on_device,
        mesh=mesh,
        in_specs=(
            P(("dp", "tm"), None),
            P(("dp", "tm"), None),
            P(),
            P(),
            P(),
            P(),
            P(),
            P(),
            P(),
            P("dp", None),
            P("dp", None),
            P("dp", None),
        ),
        out_specs=(P(("dp", "tm"), None), P("dp", "tm")),
        check_vma=False,
    )
```

```python
import functools
import math

import jax
import jax.numpy as jnp
from jax import lax
from jax.experimental import pallas as pl
from jax.experimental.pallas import tpu as pltpu
from jax.sharding import PartitionSpec as P

HEADS = 8
KERNEL = 31
BLOCK = 64
LC = 2
SPAN = (LC + 1) * BLOCK
HALO = 32
ROWS = HALO + BLOCK
PAD = LC + 1
EPSILON = 1e-05
SOFT_CAP = 4.0
LANES = 128
SUB = 8

BF16 = jnp.bfloat16
F32 = jnp.float32


def dot_nn(a, b):
    return lax.dot_general(a, b, (((1,), (0,)), ((), ())), preferred_element_type=F32)


def dot_nt(a, b):
    return lax.dot_general(a, b, (((1,), (1,)), ((), ())), preferred_element_type=F32)


def dot_tn(a, b):
    return lax.dot_general(a, b, (((0,), (0,)), ((), ())), preferred_element_type=F32)


def norm_stats(values):
    row_mean = jnp.mean(values, axis=-1, keepdims=True)
    centred = values - row_mean
    scale_inv = lax.rsqrt(jnp.mean(centred * centred, axis=-1, keepdims=True) + EPSILON)
    return centred * scale_inv, scale_inv


class Layout:
    def __init__(self, meta_ref, utts, blocks):
        self.ref, self.utts, self.blocks = meta_ref, utts, blocks

    def me(self):
        return self.ref[0, 0]

    def dp(self):
        return self.ref[0, 1]

    def block_of(self, slot):
        found = jnp.int32(0)
        for b in range(self.blocks):
            found = jnp.where(self.ref[0, 2 + self.utts + b] == slot, jnp.int32(b), found)
        return found

    def position(self, block):
        start = jnp.int32(0)
        first = jnp.int32(0)
        for u in range(self.utts):
            first = jnp.where(block >= start, start, first)
            start = start + self.ref[0, 2 + u]
        return block - first

    def reach(self, block):
        safe = jnp.maximum(block, 0)
        left = self.ref[0, 2 + self.utts + self.blocks + safe]
        return jnp.minimum(left, self.position(safe))


def row_at(block, count=BLOCK, shift=0):
    return pl.ds(pl.multiple_of((block + PAD) * BLOCK + shift, math.gcd(BLOCK, shift)), count)


def diag_mask(heads, rows, head_size):
    shape = (heads * rows, heads * head_size)
    row_head = lax.broadcasted_iota(jnp.int32, shape, 0) // rows
    col_head = lax.broadcasted_iota(jnp.int32, shape, 1) // head_size
    return jnp.where(row_head == col_head, 1.0, 0.0).astype(F32)


def spread(rows, mask_b):
    copies = mask_b.shape[0] // rows.shape[0]
    return jnp.concatenate([rows] * copies, axis=0) * mask_b


def fold_heads(full, mask_f, rows):
    kept = full * mask_f
    total = kept[:rows]
    for h in range(1, full.shape[0] // rows):
        total = total + kept[h * rows : (h + 1) * rows]
    return total


def window_probs(diag_q, k_win, reach, head_size):
    raw = dot_nt(k_win, diag_q)
    unit = jnp.tanh(raw * (1.0 / (SOFT_CAP * math.sqrt(head_size))))
    exped = jnp.exp(SOFT_CAP * unit)
    parts = []
    for w in range(LC):
        ok = jnp.where(reach >= LC - w, 1.0, 0.0).astype(F32)
        parts.append(exped[w * BLOCK : (w + 1) * BLOCK] * ok)
    parts.append(exped[LC * BLOCK :])
    exped = jnp.concatenate(parts, axis=0)
    total = jnp.sum(exped, axis=0, keepdims=True)
    return exped * (1.0 / total), unit


def taps_kernel(small_ref, taps_ref):
    for j in range(KERNEL):
        rows = jnp.broadcast_to(small_ref[j : j + 1], (SUB, small_ref.shape[1]))
        taps_ref[j * SUB : (j + 1) * SUB] = rows


def project_kernel(crossed_at, count, *refs):
    me_ref, g1_ref, wq_ref, wkv_ref = refs[:4]
    parts = refs[4 : 4 + count]
    x_ref, n_ref, q_ref, kv_ref = refs[4 + count :]
    if crossed_at:
        me = me_ref[0, 0]
        middle = functools.reduce(jnp.logical_or, [me == t for t in crossed_at])
        handed = jnp.concatenate([ref[...] for ref in parts[1:]], axis=0)
        rows = jnp.where(middle, parts[0][...], handed)
    else:
        rows = jnp.concatenate([ref[...] for ref in parts], axis=0)
    x_ref[...] = rows
    unit, _ = norm_stats(rows.astype(F32))
    normed = (unit * g1_ref[...]).astype(BF16)
    n_ref[...] = normed
    q_ref[...] = dot_nn(normed, wq_ref[...]).astype(BF16)
    kv_ref[...] = dot_nn(normed, wkv_ref[...]).astype(BF16)


def forward_kernel(sizes, tm, head_size, *refs):
    meta_ref, grad_ref, wo_ref, small_ref, taps_ref = refs[:5]
    x_refs, q_refs, kv_refs = (refs[5 + k * tm : 5 + (k + 1) * tm] for k in range(3))
    refs = refs[5 + 3 * tm :]
    out_ref = refs[0]
    half = tm // 2
    send_refs = refs[1 : 1 + half]
    q_ref, kv_ref, tail_s, ctx_s, e_s, h_s, u_s, gr_s, gc_s = refs[1 + half :]

    table = Layout(meta_ref, *sizes)
    me = table.me()
    local = table.blocks // tm
    width = out_ref.shape[1]
    hq = q_ref.shape[1]
    share = send_refs[0].shape[1]

    for ref in (q_ref, kv_ref):
        ref[: PAD * BLOCK] = jnp.zeros((PAD * BLOCK, ref.shape[1]), BF16)
    tail_s[:HALO] = jnp.zeros((HALO, width), BF16)
    for m in range(tm):
        for j in range(local):
            b = table.block_of((me ^ m) * local + j)
            here = slice(j * BLOCK, (j + 1) * BLOCK)
            q_ref[row_at(b)] = q_refs[m][here]
            kv_ref[row_at(b)] = kv_refs[m][here]
            after = pl.ds(pl.multiple_of((b + 1) * HALO, HALO), HALO)
            tail_s[after] = x_refs[m][(j + 1) * BLOCK - HALO : (j + 1) * BLOCK]

    mid_heads = 256 // BLOCK
    mid_f = diag_mask(mid_heads, BLOCK, head_size)
    mid_b = mid_f.astype(BF16)
    side_f = diag_mask(HEADS, HALO, head_size)
    side_b = side_f.astype(BF16)

    own = [table.block_of(me * local + i) for i in range(local)]
    keep = [jnp.where(table.position(c) >= 1, 1.0, 0.0).astype(F32) for c in own]
    for i, c in enumerate(own):
        for blk, shift, count, put in ((c - 1, HALO, HALO, 0), (c, 0, BLOCK, HALO)):
            reach = table.reach(blk)
            win = row_at(blk - LC, SPAN)
            at = row_at(blk, count, shift)
            if count == BLOCK:
                groups, mask_f, mask_b = HEADS // mid_heads, mid_f, mid_b
            else:
                groups, mask_f, mask_b = 1, side_f, side_b
            wide = hq // groups
            for g in range(groups):
                cols = slice(g * wide, (g + 1) * wide)
                vcols = slice(hq + g * wide, hq + (g + 1) * wide)
                probs, _ = window_probs(
                    spread(q_ref[at, cols], mask_b), kv_ref[win, cols], reach, head_size
                )
                full = dot_tn(probs.astype(BF16), kv_ref[win, vcols])
                ctx_s[i * ROWS + put : i * ROWS + put + count, cols] = fold_heads(
                    full, mask_f, count
                ).astype(BF16)

    gain = small_ref[KERNEL + 1 : KERNEL + 2]
    product = dot_nn(ctx_s[...], wo_ref[...])
    scales = []
    for i, c in enumerate(own):
        here = slice(i * ROWS, (i + 1) * ROWS)
        tail = tail_s[pl.ds(pl.multiple_of(c * HALO, HALO), HALO)]
        rows = jnp.concatenate([tail, x_refs[0][i * BLOCK : (i + 1) * BLOCK]], axis=0)
        hidden = rows.astype(F32) + product[here]
        unit, inv = norm_stats(hidden)
        conv_in = (unit * gain).astype(BF16).astype(F32)
        e_s[i * ROWS : i * ROWS + HALO] = conv_in[:HALO] * keep[i]
        e_s[i * ROWS + HALO : (i + 1) * ROWS] = conv_in[HALO:]
        h_s[i * BLOCK : (i + 1) * BLOCK] = hidden[HALO:]
        u_s[here] = unit
        scales.append(inv)

    groups = BLOCK // SUB

    def conv(k, carry):
        cols = pl.ds(pl.multiple_of(k * LANES, LANES), LANES)
        bias = jnp.broadcast_to(small_ref[KERNEL : KERNEL + 1, cols], (SUB, LANES))
        taps = lambda j: taps_ref[j * SUB : (j + 1) * SUB, cols]
        for i in range(local):
            ext = e_s[i * ROWS : (i + 1) * ROWS, cols]
            acc = [bias] * groups
            for s in range(SUB):
                reps = (KERNEL - s + SUB - 1) // SUB
                moved = ext[s + 2 : s + 2 + BLOCK + SUB * (reps - 1)]
                for a in range(reps):
                    tap = taps(SUB * a + s)
                    for r in range(groups):
                        piece = moved[(a + r) * SUB : (a + r + 1) * SUB]
                        acc[r] = acc[r] + tap * piece
            mixed = jnp.concatenate(acc, axis=0)
            gate = 0.5 * jnp.tanh(0.5 * mixed) + 0.5
            rows = slice(i * BLOCK, (i + 1) * BLOCK)
            out_ref[rows, cols] = (h_s[rows, cols] + mixed * gate).astype(BF16)
            slope = gate * (1.0 + mixed * (1.0 - gate))
            gm = grad_ref[rows, cols].astype(F32) * slope
            zeros = jnp.zeros((HALO, LANES), F32)
            padded = jnp.concatenate([zeros, gm, zeros], axis=0)
            back = [None] * (ROWS // SUB)
            low = HALO // SUB - 1
            for s in range(SUB):
                reps = (KERNEL - s + SUB - 1) // SUB
                start = low if s else low + 1
                moved = padded[start * SUB + s : ROWS + s]
                for a in range(reps):
                    tap = taps(KERNEL - 1 - SUB * a - s)
                    for g in range(start, ROWS // SUB):
                        r = g - a
                        piece = tap * moved[(g - start) * SUB : (g - start + 1) * SUB]
                        back[r] = piece if back[r] is None else back[r] + piece
            for r in range(ROWS // SUB):
                scale = keep[i] if r < HALO // SUB else 1.0
                gr_s[i * ROWS + r * SUB : i * ROWS + (r + 1) * SUB, cols] = back[r] * scale
        return carry

    lax.fori_loop(0, width // LANES, conv, 0)

    for i in range(local):
        here = slice(i * ROWS, (i + 1) * ROWS)
        scaled = gr_s[here] * gain
        unit = u_s[here]
        first = jnp.mean(scaled, axis=-1, keepdims=True)
        second = jnp.mean(scaled * unit, axis=-1, keepdims=True)
        back = scales[i] * (scaled - first - unit * second)
        own_grad = grad_ref[i * BLOCK : (i + 1) * BLOCK].astype(F32) + back[HALO:]
        gc_s[i * ROWS : i * ROWS + HALO] = back[:HALO].astype(BF16)
        gc_s[i * ROWS + HALO : (i + 1) * ROWS] = own_grad.astype(BF16)
    for m in range(half):
        at = pl.ds(pl.multiple_of(((me ^ m) % half) * share, share), share)
        send_refs[m][...] = dot_nt(gc_s[...], wo_ref[at]).astype(BF16)


def probs_kernel(sizes, tm, head_size, meta_ref, *refs):
    q_refs, kv_refs = refs[:tm], refs[tm : 2 * tm]
    q4_ref, v4_ref, p_ref, d_ref, k4_ref = refs[2 * tm :]
    table = Layout(meta_ref, *sizes)
    me = table.me()
    local = table.blocks // tm
    hq = q_refs[0].shape[1]
    share = q4_ref.shape[1]
    lead = pl.multiple_of((me % (tm // 2)) * share, share)
    for ref in (k4_ref, v4_ref):
        ref[: PAD * BLOCK] = jnp.zeros((PAD * BLOCK, share), BF16)
    for m in range(tm):
        for j in range(local):
            at = row_at(table.block_of((me ^ m) * local + j))
            here = slice(j * BLOCK, (j + 1) * BLOCK)
            q4_ref[at] = q_refs[m][here, pl.ds(lead, share)]
            k4_ref[at] = kv_refs[m][here, pl.ds(lead, share)]
            v4_ref[at] = kv_refs[m][here, pl.ds(pl.multiple_of(hq + lead, share), share)]
    heads = share // head_size
    mask_b = diag_mask(heads, BLOCK, head_size).astype(BF16)
    for c in range(table.blocks):
        own = slice((c + PAD) * BLOCK, (c + PAD + 1) * BLOCK)
        win = slice((c + PAD - LC) * BLOCK, (c + PAD + 1) * BLOCK)
        diag_q = spread(q4_ref[own], mask_b)
        probs, unit = window_probs(diag_q, k4_ref[win], table.reach(c), head_size)
        p_ref[c] = probs
        d_ref[c] = (1.0 - unit * unit) * (1.0 / math.sqrt(head_size))


def backward_kernel(sizes, tm, part, head_size, *refs):
    meta_ref, q4_ref, v4_ref, p_ref, d_ref = refs[:5]
    n_refs = refs[5 : 5 + tm]
    g_refs = refs[5 + tm : 5 + 2 * tm]
    out_refs = refs[5 + 2 * tm : -3]
    gt_s, t_s, full_s = refs[-3:]
    table = Layout(meta_ref, *sizes)
    me = table.me()
    blocks = table.blocks
    local = blocks // tm
    share = q4_ref.shape[1]
    mask_b = diag_mask(share // head_size, BLOCK, head_size).astype(BF16)

    places = [(m, j, table.block_of((me ^ m) * local + j)) for m in range(tm) for j in range(local)]
    for m, j, b in places:
        gt_s[row_at(b)] = g_refs[m][j * ROWS + HALO : (j + 1) * ROWS].astype(F32)
    gt_s[(PAD - 1) * BLOCK : PAD * BLOCK] = jnp.zeros((BLOCK, share), F32)
    for m, j, b in places:
        at = row_at(b, HALO, -HALO)
        gt_s[at] = gt_s[at] + g_refs[m][j * ROWS : j * ROWS + HALO].astype(F32)
    t_s[...] = jnp.zeros(t_s.shape, F32)

    def spans(c):
        own = slice((c + PAD) * BLOCK, (c + PAD + 1) * BLOCK)
        win = slice((c + PAD - LC) * BLOCK, (c + PAD + 1) * BLOCK)
        return own, win, spread(gt_s[own].astype(BF16), mask_b)

    @pl.when(me >= tm // 2)
    def _():
        for c in range(blocks):
            own, win, diag_g = spans(c)
            t_s[win] = t_s[win] + dot_nn(p_ref[c].astype(BF16), diag_g)

    @pl.when(me < tm // 2)
    def _():
        for c in range(blocks):
            own, win, diag_g = spans(c)
            grad_probs = dot_nt(v4_ref[win], diag_g)
            probs = p_ref[c]
            delta = jnp.sum(probs * grad_probs, axis=0, keepdims=True)
            grad_raw = probs * (grad_probs - delta) * d_ref[c]
            t_s[win] = t_s[win] + dot_nn(grad_raw.astype(BF16), spread(q4_ref[own], mask_b))

    terms = jnp.concatenate([t_s[row_at(b)].astype(BF16) for _, _, b in places], axis=0)
    full = dot_tn(terms, jnp.concatenate([ref[...] for ref in n_refs], axis=0))
    if len(out_refs) == 1:
        out_refs[0][...] = full.astype(BF16)
        return
    full_s[...] = full
    chip, core = table.dp() // 2, table.dp() % 2
    for q in range(out_refs[0].shape[1] // part):
        for ref, side in zip(out_refs, (core, 1 - core)):
            at = pl.ds(pl.multiple_of(((chip ^ q) * 2 + side) * part, part), part)
            ref[:, q * part : (q + 1) * part] = full_s[:, at].astype(ref.dtype)


def pair_kernel(kept_ref, got_ref, *out_refs):
    part = out_refs[0].shape[1]
    for q, ref in enumerate(out_refs):
        cols = slice(q * part, (q + 1) * part)
        ref[...] = (kept_ref[:, cols] + got_ref[:, cols].astype(F32)).astype(ref.dtype)


def sum_kernel(*refs):
    total = refs[0][...].astype(F32)
    for ref in refs[1:-1]:
        total = total + ref[...].astype(F32)
    refs[-1][...] = total.T


def on_device(
    frames,
    out_grad,
    norm1_gain,
    w_query,
    w_kv,
    w_out,
    norm2_gain,
    conv_kernel,
    conv_bias,
    utt_blocks,
    block_slot,
    left_count,
):
    tm = lax.axis_size("tm")
    dp = lax.axis_size("dp")
    rows, width = frames.shape
    blocks = block_slot.shape[1]
    utts = utt_blocks.shape[1]
    sizes = (utts, blocks)
    local = rows // BLOCK
    hq = w_query.shape[1]
    head_size = hq // HEADS
    kv_width = w_kv.shape[1]
    share = kv_width // tm
    padded = (blocks + PAD) * BLOCK

    def swap(value, axis, size, m):
        return lax.ppermute(value, axis, [(i, i ^ m) for i in range(size)])

    me = lax.axis_index("tm").astype(jnp.int32).reshape(1, 1)
    meta = jnp.concatenate(
        [
            me,
            lax.axis_index("dp").astype(jnp.int32).reshape(1, 1),
            utt_blocks,
            block_slot,
            left_count,
        ],
        axis=1,
    )
    small = jnp.concatenate(
        [conv_kernel, conv_bias.reshape(1, -1), norm2_gain.reshape(1, -1)], axis=0
    )

    smem = pl.BlockSpec(memory_space=pltpu.SMEM)
    vmem = pl.BlockSpec(memory_space=pltpu.VMEM)
    shape = jax.ShapeDtypeStruct

    taps = pl.pallas_call(
        taps_kernel,
        out_shape=shape((KERNEL * SUB, width), F32),
        in_specs=[vmem],
        out_specs=vmem,
        compiler_params=pltpu.CompilerParams(vmem_limit_bytes=8 << 20),
        cost_estimate=pl.CostEstimate(flops=1, bytes_accessed=1, transcendentals=0),
        name="spread_taps",
    )(small)

    x, normed, queries, keys_values = {}, {}, {}, {}
    made = [shape((rows, w), BF16) for w in (width, width, hq, kv_width)]

    def project(m, parts, crossed_at=()):
        outs = pl.pallas_call(
            functools.partial(project_kernel, crossed_at, len(parts)),
            out_shape=made,
            in_specs=[smem] + [vmem] * (3 + len(parts)),
            out_specs=[vmem] * 4,
            compiler_params=pltpu.CompilerParams(vmem_limit_bytes=32 << 20),
            cost_estimate=pl.CostEstimate(flops=1, bytes_accessed=1, transcendentals=0),
            name=f"project_rows_{m}",
        )(me, norm1_gain.reshape(1, -1), w_query, w_kv, *parts)
        x[m], normed[m], queries[m], keys_values[m] = outs

    if tm == 4:
        inward = [(1, 0), (2, 3)]
        first, second = frames[: rows // 2], frames[rows // 2 :]
        far_a = swap(first, "tm", tm, 2)
        whole, first = lax.optimization_barrier((frames, first))
        beside = swap(whole, "tm", tm, 1)
        second, small = lax.optimization_barrier((second, small))
        far_b = swap(second, "tm", tm, 2)
        project(0, (frames,))
        far_a, normed[0] = lax.optimization_barrier((far_a, normed[0]))
        later, beside = lax.optimization_barrier((frames, beside))
        handed_a = lax.ppermute(far_a, "tm", inward)
        crossed = lax.ppermute(later, "tm", [(1, 2), (2, 1)])
        project(1, (beside,))
        far_b, handed_a, taps, meta = lax.optimization_barrier((far_b, handed_a, taps, meta))
        handed_b = lax.ppermute(far_b, "tm", inward)
        project(2, (far_a, far_b))
        project(3, (crossed, handed_a, handed_b), (1, 2))
    else:
        project(0, (frames,))
        for m in range(1, tm):
            project(m, (swap(frames, "tm", tm, m),))

    def by_m(arrays):
        return [arrays[m] for m in range(tm)]

    own_rows = local * ROWS
    results = pl.pallas_call(
        functools.partial(forward_kernel, sizes, tm, head_size),
        out_shape=[shape((rows, width), BF16)]
        + [shape((own_rows, share), BF16)] * (tm // 2),
        in_specs=[smem] + [vmem] * (4 + 3 * tm),
        out_specs=[vmem] * (tm // 2 + 1),
        scratch_shapes=[
            pltpu.VMEM((padded, hq), BF16),
            pltpu.VMEM((padded, kv_width), BF16),
            pltpu.VMEM(((blocks + 1) * HALO, width), BF16),
            pltpu.VMEM((own_rows, hq), BF16),
            pltpu.VMEM((own_rows, width), F32),
            pltpu.VMEM((rows, width), F32),
            pltpu.VMEM((own_rows, width), F32),
            pltpu.VMEM((own_rows, width), F32),
            pltpu.VMEM((own_rows, width), BF16),
        ],
        compiler_params=pltpu.CompilerParams(vmem_limit_bytes=32 << 20),
        name="forward_pass",
    )(meta, out_grad, w_out, small, taps, *by_m(x), *by_m(queries), *by_m(keys_values))
    layer_out = results[0]
    sends = results[1:]
    got = {0: sends[0]}
    for m in range(tm - 1, 0, -1):
        got[m] = swap(sends[m % (tm // 2)], "tm", tm, m)

    pair_width = share // head_size * BLOCK
    q4, v4, probs, slopes = pl.pallas_call(
        functools.partial(probs_kernel, sizes, tm, head_size),
        out_shape=[shape((padded, share), BF16)] * 2
        + [shape((blocks, SPAN, pair_width), F32)] * 2,
        in_specs=[smem] + [vmem] * (2 * tm),
        out_specs=[vmem] * 4,
        scratch_shapes=[pltpu.VMEM((padded, share), BF16)],
        compiler_params=pltpu.CompilerParams(vmem_limit_bytes=24 << 20),
        name="window_probs",
        cost_estimate=pl.CostEstimate(
            flops=2 * 10**9, bytes_accessed=4 * 10**6, transcendentals=800000
        ),
    )(meta, *by_m(queries), *by_m(keys_values))

    direct = dp <= 8
    half_width = width // 2
    if direct:
        piece_shapes = [shape((share, half_width), F32), shape((share, half_width), BF16)]
    else:
        piece_shapes = [shape((share, width), BF16)]
    pieces = pl.pallas_call(
        functools.partial(backward_kernel, sizes, tm, width // dp, head_size),
        out_shape=piece_shapes,
        in_specs=[smem] + [vmem] * (4 + 2 * tm),
        out_specs=[vmem] * len(piece_shapes),
        scratch_shapes=[
            pltpu.VMEM((padded, share), F32),
            pltpu.VMEM((padded, share), F32),
            pltpu.VMEM((share, width), F32),
        ],
        compiler_params=pltpu.CompilerParams(vmem_limit_bytes=32 << 20),
        name="key_value_terms",
    )(meta, q4, v4, probs, slopes, *by_m(normed), *by_m(got))

    if direct:
        kept, away = pieces
        arrived = swap(away, "dp", dp, 1)
        chips = dp // 2
        part = width // dp
        summed = pl.pallas_call(
            pair_kernel,
            out_shape=[shape((share, part), BF16)] * chips,
            in_specs=[vmem] * 2,
            out_specs=[vmem] * chips,
            compiler_params=pltpu.CompilerParams(vmem_limit_bytes=4 << 20),
            name="sum_pair",
        )(kept, arrived)
        terms = [swap(summed[q], "dp", dp, 2 * q) for q in range(chips - 1, 0, -1)]
        terms.append(summed[0])
    else:
        terms = [lax.psum_scatter(pieces[0], "dp", scatter_dimension=1, tiled=True)]
    kv_grad = pl.pallas_call(
        sum_kernel,
        out_shape=shape((width // dp, share), F32),
        in_specs=[vmem] * len(terms),
        out_specs=vmem,
        compiler_params=pltpu.CompilerParams(vmem_limit_bytes=4 << 20),
        name="sum_groups",
    )(*terms)
    return layer_out, kv_grad


def solution(mesh):
    return jax.shard_map(
        on_device,
        mesh=mesh,
        in_specs=(
            P(("dp", "tm"), None),
            P(("dp", "tm"), None),
            P(),
            P(),
            P(),
            P(),
            P(),
            P(),
            P(),
            P("dp", None),
            P("dp", None),
            P("dp", None),
        ),
        out_specs=(P(("dp", "tm"), None), P("dp", "tm")),
        check_vma=False,
    )
```

```python
import functools
import math

import jax
import jax.numpy as jnp
from jax import lax
from jax.experimental import pallas as pl
from jax.experimental.pallas import tpu as pltpu
from jax.sharding import PartitionSpec as P

HEADS = 8
KERNEL = 31
BLOCK = 64
LC = 2
SPAN = (LC + 1) * BLOCK
HALO = 32
ROWS = HALO + BLOCK
PAD = LC + 1
EPSILON = 1e-05
SOFT_CAP = 4.0
LANES = 128
SUB = 8

BF16 = jnp.bfloat16
F32 = jnp.float32


def dot_nn(a, b):
    return lax.dot_general(a, b, (((1,), (0,)), ((), ())), preferred_element_type=F32)


def dot_nt(a, b):
    return lax.dot_general(a, b, (((1,), (1,)), ((), ())), preferred_element_type=F32)


def dot_tn(a, b):
    return lax.dot_general(a, b, (((0,), (0,)), ((), ())), preferred_element_type=F32)


def norm_stats(values):
    row_mean = jnp.mean(values, axis=-1, keepdims=True)
    centred = values - row_mean
    scale_inv = lax.rsqrt(jnp.mean(centred * centred, axis=-1, keepdims=True) + EPSILON)
    return centred * scale_inv, scale_inv


class Layout:
    def __init__(self, meta_ref, utts, blocks):
        self.ref, self.utts, self.blocks = meta_ref, utts, blocks

    def me(self):
        return self.ref[0, 0]

    def dp(self):
        return self.ref[0, 1]

    def block_of(self, slot):
        found = jnp.int32(0)
        for b in range(self.blocks):
            found = jnp.where(self.ref[0, 2 + self.utts + b] == slot, jnp.int32(b), found)
        return found

    def position(self, block):
        start = jnp.int32(0)
        first = jnp.int32(0)
        for u in range(self.utts):
            first = jnp.where(block >= start, start, first)
            start = start + self.ref[0, 2 + u]
        return block - first

    def reach(self, block):
        safe = jnp.maximum(block, 0)
        left = self.ref[0, 2 + self.utts + self.blocks + safe]
        return jnp.minimum(left, self.position(safe))


def row_at(block, count=BLOCK, shift=0):
    return pl.ds(pl.multiple_of((block + PAD) * BLOCK + shift, math.gcd(BLOCK, shift)), count)


def diag_mask(heads, rows, head_size):
    shape = (heads * rows, heads * head_size)
    row_head = lax.broadcasted_iota(jnp.int32, shape, 0) // rows
    col_head = lax.broadcasted_iota(jnp.int32, shape, 1) // head_size
    return jnp.where(row_head == col_head, 1.0, 0.0).astype(F32)


def spread(rows, mask_b):
    copies = mask_b.shape[0] // rows.shape[0]
    return jnp.concatenate([rows] * copies, axis=0) * mask_b


def fold_heads(full, mask_f, rows):
    kept = full * mask_f
    total = kept[:rows]
    for h in range(1, full.shape[0] // rows):
        total = total + kept[h * rows : (h + 1) * rows]
    return total


def window_probs(diag_q, k_win, reach, head_size):
    raw = dot_nt(k_win, diag_q)
    unit = jnp.tanh(raw * (1.0 / (SOFT_CAP * math.sqrt(head_size))))
    exped = jnp.exp(SOFT_CAP * unit)
    parts = []
    for w in range(LC):
        ok = jnp.where(reach >= LC - w, 1.0, 0.0).astype(F32)
        parts.append(exped[w * BLOCK : (w + 1) * BLOCK] * ok)
    parts.append(exped[LC * BLOCK :])
    exped = jnp.concatenate(parts, axis=0)
    total = jnp.sum(exped, axis=0, keepdims=True)
    return exped * (1.0 / total), unit


def taps_kernel(small_ref, taps_ref):
    for j in range(KERNEL):
        rows = jnp.broadcast_to(small_ref[j : j + 1], (SUB, small_ref.shape[1]))
        taps_ref[j * SUB : (j + 1) * SUB] = rows


def project_kernel(x_ref, g1_ref, wq_ref, wkv_ref, n_ref, q_ref, kv_ref):
    unit, _ = norm_stats(x_ref[...].astype(F32))
    normed = (unit * g1_ref[...]).astype(BF16)
    n_ref[...] = normed
    q_ref[...] = dot_nn(normed, wq_ref[...]).astype(BF16)
    kv_ref[...] = dot_nn(normed, wkv_ref[...]).astype(BF16)


def forward_kernel(sizes, tm, head_size, *refs):
    meta_ref, grad_ref, wo_ref, small_ref, taps_ref = refs[:5]
    x_refs, q_refs, kv_refs = (refs[5 + k * tm : 5 + (k + 1) * tm] for k in range(3))
    refs = refs[5 + 3 * tm :]
    out_ref = refs[0]
    half = tm // 2
    send_refs = refs[1 : 1 + half]
    q_ref, kv_ref, tail_s, ctx_s, e_s, h_s, u_s, gr_s, gc_s = refs[1 + half :]

    table = Layout(meta_ref, *sizes)
    me = table.me()
    local = table.blocks // tm
    width = out_ref.shape[1]
    hq = q_ref.shape[1]
    share = send_refs[0].shape[1]

    for ref in (q_ref, kv_ref):
        ref[: PAD * BLOCK] = jnp.zeros((PAD * BLOCK, ref.shape[1]), BF16)
    tail_s[:HALO] = jnp.zeros((HALO, width), BF16)
    for m in range(tm):
        for j in range(local):
            b = table.block_of((me ^ m) * local + j)
            here = slice(j * BLOCK, (j + 1) * BLOCK)
            q_ref[row_at(b)] = q_refs[m][here]
            kv_ref[row_at(b)] = kv_refs[m][here]
            after = pl.ds(pl.multiple_of((b + 1) * HALO, HALO), HALO)
            tail_s[after] = x_refs[m][(j + 1) * BLOCK - HALO : (j + 1) * BLOCK]

    mid_heads = 256 // BLOCK
    mid_f = diag_mask(mid_heads, BLOCK, head_size)
    mid_b = mid_f.astype(BF16)
    side_f = diag_mask(HEADS, HALO, head_size)
    side_b = side_f.astype(BF16)

    own = [table.block_of(me * local + i) for i in range(local)]
    keep = [jnp.where(table.position(c) >= 1, 1.0, 0.0).astype(F32) for c in own]
    for i, c in enumerate(own):
        for blk, shift, count, put in ((c - 1, HALO, HALO, 0), (c, 0, BLOCK, HALO)):
            reach = table.reach(blk)
            win = row_at(blk - LC, SPAN)
            at = row_at(blk, count, shift)
            if count == BLOCK:
                groups, mask_f, mask_b = HEADS // mid_heads, mid_f, mid_b
            else:
                groups, mask_f, mask_b = 1, side_f, side_b
            wide = hq // groups
            for g in range(groups):
                cols = slice(g * wide, (g + 1) * wide)
                vcols = slice(hq + g * wide, hq + (g + 1) * wide)
                probs, _ = window_probs(
                    spread(q_ref[at, cols], mask_b), kv_ref[win, cols], reach, head_size
                )
                full = dot_tn(probs.astype(BF16), kv_ref[win, vcols])
                ctx_s[i * ROWS + put : i * ROWS + put + count, cols] = fold_heads(
                    full, mask_f, count
                ).astype(BF16)

    gain = small_ref[KERNEL + 1 : KERNEL + 2]
    product = dot_nn(ctx_s[...], wo_ref[...])
    scales = []
    for i, c in enumerate(own):
        here = slice(i * ROWS, (i + 1) * ROWS)
        tail = tail_s[pl.ds(pl.multiple_of(c * HALO, HALO), HALO)]
        rows = jnp.concatenate([tail, x_refs[0][i * BLOCK : (i + 1) * BLOCK]], axis=0)
        hidden = rows.astype(F32) + product[here]
        unit, inv = norm_stats(hidden)
        conv_in = (unit * gain).astype(BF16).astype(F32)
        e_s[i * ROWS : i * ROWS + HALO] = conv_in[:HALO] * keep[i]
        e_s[i * ROWS + HALO : (i + 1) * ROWS] = conv_in[HALO:]
        h_s[i * BLOCK : (i + 1) * BLOCK] = hidden[HALO:]
        u_s[here] = unit
        scales.append(inv)

    groups = BLOCK // SUB

    def conv(k, carry):
        cols = pl.ds(pl.multiple_of(k * LANES, LANES), LANES)
        bias = jnp.broadcast_to(small_ref[KERNEL : KERNEL + 1, cols], (SUB, LANES))
        taps = lambda j: taps_ref[j * SUB : (j + 1) * SUB, cols]
        for i in range(local):
            ext = e_s[i * ROWS : (i + 1) * ROWS, cols]
            acc = [bias] * groups
            for s in range(SUB):
                reps = (KERNEL - s + SUB - 1) // SUB
                moved = ext[s + 2 : s + 2 + BLOCK + SUB * (reps - 1)]
                for a in range(reps):
                    tap = taps(SUB * a + s)
                    for r in range(groups):
                        piece = moved[(a + r) * SUB : (a + r + 1) * SUB]
                        acc[r] = acc[r] + tap * piece
            mixed = jnp.concatenate(acc, axis=0)
            gate = 0.5 * jnp.tanh(0.5 * mixed) + 0.5
            rows = slice(i * BLOCK, (i + 1) * BLOCK)
            out_ref[rows, cols] = (h_s[rows, cols] + mixed * gate).astype(BF16)
            slope = gate * (1.0 + mixed * (1.0 - gate))
            gm = grad_ref[rows, cols].astype(F32) * slope
            zeros = jnp.zeros((HALO, LANES), F32)
            padded = jnp.concatenate([zeros, gm, zeros], axis=0)
            back = [None] * (ROWS // SUB)
            low = HALO // SUB - 1
            for s in range(SUB):
                reps = (KERNEL - s + SUB - 1) // SUB
                start = low if s else low + 1
                moved = padded[start * SUB + s : ROWS + s]
                for a in range(reps):
                    tap = taps(KERNEL - 1 - SUB * a - s)
                    for g in range(start, ROWS // SUB):
                        r = g - a
                        piece = tap * moved[(g - start) * SUB : (g - start + 1) * SUB]
                        back[r] = piece if back[r] is None else back[r] + piece
            for r in range(ROWS // SUB):
                scale = keep[i] if r < HALO // SUB else 1.0
                gr_s[i * ROWS + r * SUB : i * ROWS + (r + 1) * SUB, cols] = back[r] * scale
        return carry

    lax.fori_loop(0, width // LANES, conv, 0)

    for i in range(local):
        here = slice(i * ROWS, (i + 1) * ROWS)
        scaled = gr_s[here] * gain
        unit = u_s[here]
        first = jnp.mean(scaled, axis=-1, keepdims=True)
        second = jnp.mean(scaled * unit, axis=-1, keepdims=True)
        back = scales[i] * (scaled - first - unit * second)
        own_grad = grad_ref[i * BLOCK : (i + 1) * BLOCK].astype(F32) + back[HALO:]
        gc_s[i * ROWS : i * ROWS + HALO] = back[:HALO].astype(BF16)
        gc_s[i * ROWS + HALO : (i + 1) * ROWS] = own_grad.astype(BF16)
    for m in range(half):
        at = pl.ds(pl.multiple_of(((me ^ m) % half) * share, share), share)
        send_refs[m][...] = dot_nt(gc_s[...], wo_ref[at]).astype(BF16)


def probs_kernel(sizes, tm, head_size, meta_ref, *refs):
    q_refs, kv_refs = refs[:tm], refs[tm : 2 * tm]
    q4_ref, v4_ref, p_ref, d_ref, k4_ref = refs[2 * tm :]
    table = Layout(meta_ref, *sizes)
    me = table.me()
    local = table.blocks // tm
    hq = q_refs[0].shape[1]
    share = q4_ref.shape[1]
    lead = pl.multiple_of((me % (tm // 2)) * share, share)
    for ref in (k4_ref, v4_ref):
        ref[: PAD * BLOCK] = jnp.zeros((PAD * BLOCK, share), BF16)
    for m in range(tm):
        for j in range(local):
            at = row_at(table.block_of((me ^ m) * local + j))
            here = slice(j * BLOCK, (j + 1) * BLOCK)
            q4_ref[at] = q_refs[m][here, pl.ds(lead, share)]
            k4_ref[at] = kv_refs[m][here, pl.ds(lead, share)]
            v4_ref[at] = kv_refs[m][here, pl.ds(pl.multiple_of(hq + lead, share), share)]
    heads = share // head_size
    mask_b = diag_mask(heads, BLOCK, head_size).astype(BF16)
    for c in range(table.blocks):
        own = slice((c + PAD) * BLOCK, (c + PAD + 1) * BLOCK)
        win = slice((c + PAD - LC) * BLOCK, (c + PAD + 1) * BLOCK)
        diag_q = spread(q4_ref[own], mask_b)
        probs, unit = window_probs(diag_q, k4_ref[win], table.reach(c), head_size)
        p_ref[c] = probs
        d_ref[c] = (1.0 - unit * unit) * (1.0 / math.sqrt(head_size))


def backward_kernel(sizes, tm, part, head_size, *refs):
    meta_ref, q4_ref, v4_ref, p_ref, d_ref = refs[:5]
    n_refs = refs[5 : 5 + tm]
    g_refs = refs[5 + tm : 5 + 2 * tm]
    out_refs = refs[5 + 2 * tm : -3]
    gt_s, t_s, full_s = refs[-3:]
    table = Layout(meta_ref, *sizes)
    me = table.me()
    blocks = table.blocks
    local = blocks // tm
    share = q4_ref.shape[1]
    mask_b = diag_mask(share // head_size, BLOCK, head_size).astype(BF16)

    places = [(m, j, table.block_of((me ^ m) * local + j)) for m in range(tm) for j in range(local)]
    for m, j, b in places:
        gt_s[row_at(b)] = g_refs[m][j * ROWS + HALO : (j + 1) * ROWS].astype(F32)
    gt_s[(PAD - 1) * BLOCK : PAD * BLOCK] = jnp.zeros((BLOCK, share), F32)
    for m, j, b in places:
        at = row_at(b, HALO, -HALO)
        gt_s[at] = gt_s[at] + g_refs[m][j * ROWS : j * ROWS + HALO].astype(F32)
    t_s[...] = jnp.zeros(t_s.shape, F32)

    def spans(c):
        own = slice((c + PAD) * BLOCK, (c + PAD + 1) * BLOCK)
        win = slice((c + PAD - LC) * BLOCK, (c + PAD + 1) * BLOCK)
        return own, win, spread(gt_s[own].astype(BF16), mask_b)

    @pl.when(me >= tm // 2)
    def _():
        for c in range(blocks):
            own, win, diag_g = spans(c)
            t_s[win] = t_s[win] + dot_nn(p_ref[c].astype(BF16), diag_g)

    @pl.when(me < tm // 2)
    def _():
        for c in range(blocks):
            own, win, diag_g = spans(c)
            grad_probs = dot_nt(v4_ref[win], diag_g)
            probs = p_ref[c]
            delta = jnp.sum(probs * grad_probs, axis=0, keepdims=True)
            grad_raw = probs * (grad_probs - delta) * d_ref[c]
            t_s[win] = t_s[win] + dot_nn(grad_raw.astype(BF16), spread(q4_ref[own], mask_b))

    terms = jnp.concatenate([t_s[row_at(b)].astype(BF16) for _, _, b in places], axis=0)
    full = dot_tn(terms, jnp.concatenate([ref[...] for ref in n_refs], axis=0))
    if len(out_refs) == 1:
        out_refs[0][...] = full.astype(BF16)
        return
    full_s[...] = full
    chip, core = table.dp() // 2, table.dp() % 2
    for q in range(out_refs[0].shape[1] // part):
        for ref, side in zip(out_refs, (core, 1 - core)):
            at = pl.ds(pl.multiple_of(((chip ^ q) * 2 + side) * part, part), part)
            ref[:, q * part : (q + 1) * part] = full_s[:, at].astype(ref.dtype)


def pair_kernel(kept_ref, got_ref, *out_refs):
    part = out_refs[0].shape[1]
    for q, ref in enumerate(out_refs):
        cols = slice(q * part, (q + 1) * part)
        ref[...] = (kept_ref[:, cols] + got_ref[:, cols].astype(F32)).astype(ref.dtype)


def sum_kernel(*refs):
    total = refs[0][...].astype(F32)
    for ref in refs[1:-1]:
        total = total + ref[...].astype(F32)
    refs[-1][...] = total.T


def on_device(
    frames,
    out_grad,
    norm1_gain,
    w_query,
    w_kv,
    w_out,
    norm2_gain,
    conv_kernel,
    conv_bias,
    utt_blocks,
    block_slot,
    left_count,
):
    tm = lax.axis_size("tm")
    dp = lax.axis_size("dp")
    rows, width = frames.shape
    blocks = block_slot.shape[1]
    utts = utt_blocks.shape[1]
    sizes = (utts, blocks)
    local = rows // BLOCK
    hq = w_query.shape[1]
    head_size = hq // HEADS
    kv_width = w_kv.shape[1]
    share = kv_width // tm
    padded = (blocks + PAD) * BLOCK

    def swap(value, axis, size, m):
        return lax.ppermute(value, axis, [(i, i ^ m) for i in range(size)])

    meta = jnp.concatenate(
        [
            lax.axis_index("tm").astype(jnp.int32).reshape(1, 1),
            lax.axis_index("dp").astype(jnp.int32).reshape(1, 1),
            utt_blocks,
            block_slot,
            left_count,
        ],
        axis=1,
    )
    small = jnp.concatenate(
        [conv_kernel, conv_bias.reshape(1, -1), norm2_gain.reshape(1, -1)], axis=0
    )

    smem = pl.BlockSpec(memory_space=pltpu.SMEM)
    vmem = pl.BlockSpec(memory_space=pltpu.VMEM)
    shape = jax.ShapeDtypeStruct

    taps = pl.pallas_call(
        taps_kernel,
        out_shape=shape((KERNEL * SUB, width), F32),
        in_specs=[vmem],
        out_specs=vmem,
        compiler_params=pltpu.CompilerParams(vmem_limit_bytes=8 << 20),
        cost_estimate=pl.CostEstimate(flops=10**6, bytes_accessed=1 << 20, transcendentals=0),
        name="spread_taps",
    )(small)

    x, normed, queries, keys_values = {}, {}, {}, {}
    made = [shape((rows, w), BF16) for w in (width, hq, kv_width)]

    def project(m, part):
        x[m] = part
        normed[m], queries[m], keys_values[m] = pl.pallas_call(
            project_kernel,
            out_shape=made,
            in_specs=[vmem] * 4,
            out_specs=[vmem] * 3,
            compiler_params=pltpu.CompilerParams(vmem_limit_bytes=16 << 20),
            cost_estimate=pl.CostEstimate(
                flops=2 * rows * width * (hq + kv_width), bytes_accessed=4 << 20, transcendentals=0
            ),
            name=f"project_rows_{m}",
        )(part, norm1_gain.reshape(1, -1), w_query, w_kv)

    project(0, frames)
    if tm == 4:
        facing = swap(frames, "tm", tm, 2)
        beside = swap(frames, "tm", tm, 1)
        facing, normed[0], taps, meta = lax.optimization_barrier(
            (facing, normed[0], taps, meta)
        )
        across = swap(facing, "tm", tm, 1)
        project(2, facing)
        project(1, beside)
        project(3, across)
    else:
        for m in range(1, tm):
            project(m, swap(frames, "tm", tm, m))

    def by_m(arrays):
        return [arrays[m] for m in range(tm)]

    own_rows = local * ROWS
    results = pl.pallas_call(
        functools.partial(forward_kernel, sizes, tm, head_size),
        out_shape=[shape((rows, width), BF16)]
        + [shape((own_rows, share), BF16)] * (tm // 2),
        in_specs=[smem] + [vmem] * (4 + 3 * tm),
        out_specs=[vmem] * (tm // 2 + 1),
        scratch_shapes=[
            pltpu.VMEM((padded, hq), BF16),
            pltpu.VMEM((padded, kv_width), BF16),
            pltpu.VMEM(((blocks + 1) * HALO, width), BF16),
            pltpu.VMEM((own_rows, hq), BF16),
            pltpu.VMEM((own_rows, width), F32),
            pltpu.VMEM((rows, width), F32),
            pltpu.VMEM((own_rows, width), F32),
            pltpu.VMEM((own_rows, width), F32),
            pltpu.VMEM((own_rows, width), BF16),
        ],
        compiler_params=pltpu.CompilerParams(vmem_limit_bytes=32 << 20),
        name="forward_pass",
    )(meta, out_grad, w_out, small, taps, *by_m(x), *by_m(queries), *by_m(keys_values))
    layer_out = results[0]
    sends = results[1:]
    got = {0: sends[0]}
    for m in range(tm - 1, 0, -1):
        got[m] = swap(sends[m % (tm // 2)], "tm", tm, m)

    pair_width = share // head_size * BLOCK
    q4, v4, probs, slopes = pl.pallas_call(
        functools.partial(probs_kernel, sizes, tm, head_size),
        out_shape=[shape((padded, share), BF16)] * 2
        + [shape((blocks, SPAN, pair_width), F32)] * 2,
        in_specs=[smem] + [vmem] * (2 * tm),
        out_specs=[vmem] * 4,
        scratch_shapes=[pltpu.VMEM((padded, share), BF16)],
        compiler_params=pltpu.CompilerParams(vmem_limit_bytes=24 << 20),
        name="window_probs",
        cost_estimate=pl.CostEstimate(
            flops=2 * 10**9, bytes_accessed=4 * 10**6, transcendentals=800000
        ),
    )(meta, *by_m(queries), *by_m(keys_values))

    direct = dp <= 8
    half_width = width // 2
    if direct:
        piece_shapes = [shape((share, half_width), F32), shape((share, half_width), BF16)]
    else:
        piece_shapes = [shape((share, width), BF16)]
    pieces = pl.pallas_call(
        functools.partial(backward_kernel, sizes, tm, width // dp, head_size),
        out_shape=piece_shapes,
        in_specs=[smem] + [vmem] * (4 + 2 * tm),
        out_specs=[vmem] * len(piece_shapes),
        scratch_shapes=[
            pltpu.VMEM((padded, share), F32),
            pltpu.VMEM((padded, share), F32),
            pltpu.VMEM((share, width), F32),
        ],
        compiler_params=pltpu.CompilerParams(vmem_limit_bytes=32 << 20),
        name="key_value_terms",
    )(meta, q4, v4, probs, slopes, *by_m(normed), *by_m(got))

    if direct:
        kept, away = pieces
        arrived = swap(away, "dp", dp, 1)
        chips = dp // 2
        part = width // dp
        summed = pl.pallas_call(
            pair_kernel,
            out_shape=[shape((share, part), BF16)] * chips,
            in_specs=[vmem] * 2,
            out_specs=[vmem] * chips,
            compiler_params=pltpu.CompilerParams(vmem_limit_bytes=4 << 20),
            name="sum_pair",
        )(kept, arrived)
        terms = [swap(summed[q], "dp", dp, 2 * q) for q in range(chips - 1, 0, -1)]
        terms.append(summed[0])
    else:
        terms = [lax.psum_scatter(pieces[0], "dp", scatter_dimension=1, tiled=True)]
    kv_grad = pl.pallas_call(
        sum_kernel,
        out_shape=shape((width // dp, share), F32),
        in_specs=[vmem] * len(terms),
        out_specs=vmem,
        compiler_params=pltpu.CompilerParams(vmem_limit_bytes=4 << 20),
        name="sum_groups",
    )(*terms)
    return layer_out, kv_grad


def solution(mesh):
    return jax.shard_map(
        on_device,
        mesh=mesh,
        in_specs=(
            P(("dp", "tm"), None),
            P(("dp", "tm"), None),
            P(),
            P(),
            P(),
            P(),
            P(),
            P(),
            P(),
            P("dp", None),
            P("dp", None),
            P("dp", None),
        ),
        out_specs=(P(("dp", "tm"), None), P("dp", "tm")),
        check_vma=False,
    )
```

```python
import functools
import math

import jax
import jax.numpy as jnp
from jax import lax
from jax.experimental import pallas as pl
from jax.experimental.pallas import tpu as pltpu
from jax.sharding import PartitionSpec as P

HEADS = 8
KERNEL = 31
BLOCK = 64
LC = 2
SPAN = (LC + 1) * BLOCK
HALO = 32
ROWS = HALO + BLOCK
PAD = LC + 1
EPSILON = 1e-05
SOFT_CAP = 4.0
LANES = 128
SUB = 8

BF16 = jnp.bfloat16
F32 = jnp.float32


def dot_nn(a, b):
    return lax.dot_general(a, b, (((1,), (0,)), ((), ())), preferred_element_type=F32)


def dot_nt(a, b):
    return lax.dot_general(a, b, (((1,), (1,)), ((), ())), preferred_element_type=F32)


def dot_tn(a, b):
    return lax.dot_general(a, b, (((0,), (0,)), ((), ())), preferred_element_type=F32)


def norm_stats(values):
    row_mean = jnp.mean(values, axis=-1, keepdims=True)
    centred = values - row_mean
    scale_inv = lax.rsqrt(jnp.mean(centred * centred, axis=-1, keepdims=True) + EPSILON)
    return centred * scale_inv, scale_inv


class Layout:
    def __init__(self, meta_ref, utts, blocks):
        self.ref, self.utts, self.blocks = meta_ref, utts, blocks

    def me(self):
        return self.ref[0, 0]

    def dp(self):
        return self.ref[0, 1]

    def block_of(self, slot):
        found = jnp.int32(0)
        for b in range(self.blocks):
            found = jnp.where(self.ref[0, 2 + self.utts + b] == slot, jnp.int32(b), found)
        return found

    def position(self, block):
        start = jnp.int32(0)
        first = jnp.int32(0)
        for u in range(self.utts):
            first = jnp.where(block >= start, start, first)
            start = start + self.ref[0, 2 + u]
        return block - first

    def reach(self, block):
        safe = jnp.maximum(block, 0)
        left = self.ref[0, 2 + self.utts + self.blocks + safe]
        return jnp.minimum(left, self.position(safe))


def row_at(block, count=BLOCK, shift=0):
    return pl.ds(pl.multiple_of((block + PAD) * BLOCK + shift, math.gcd(BLOCK, shift)), count)


def diag_mask(heads, rows, head_size):
    shape = (heads * rows, heads * head_size)
    row_head = lax.broadcasted_iota(jnp.int32, shape, 0) // rows
    col_head = lax.broadcasted_iota(jnp.int32, shape, 1) // head_size
    return jnp.where(row_head == col_head, 1.0, 0.0).astype(F32)


def spread(rows, mask_b):
    copies = mask_b.shape[0] // rows.shape[0]
    return jnp.concatenate([rows] * copies, axis=0) * mask_b


def fold_heads(full, mask_f, rows):
    kept = full * mask_f
    total = kept[:rows]
    for h in range(1, full.shape[0] // rows):
        total = total + kept[h * rows : (h + 1) * rows]
    return total


def window_probs(diag_q, k_win, reach, head_size):
    raw = dot_nt(k_win, diag_q)
    unit = jnp.tanh(raw * (1.0 / (SOFT_CAP * math.sqrt(head_size))))
    exped = jnp.exp(SOFT_CAP * unit)
    parts = []
    for w in range(LC):
        ok = jnp.where(reach >= LC - w, 1.0, 0.0).astype(F32)
        parts.append(exped[w * BLOCK : (w + 1) * BLOCK] * ok)
    parts.append(exped[LC * BLOCK :])
    exped = jnp.concatenate(parts, axis=0)
    total = jnp.sum(exped, axis=0, keepdims=True)
    return exped * (1.0 / total), unit


def taps_kernel(small_ref, taps_ref):
    for j in range(KERNEL):
        rows = jnp.broadcast_to(small_ref[j : j + 1], (SUB, small_ref.shape[1]))
        taps_ref[j * SUB : (j + 1) * SUB] = rows


def project_kernel(x_ref, g1_ref, wq_ref, wkv_ref, n_ref, q_ref, kv_ref):
    project(x_ref, g1_ref, wq_ref, wkv_ref, n_ref, q_ref, kv_ref)


def project(x_ref, g1_ref, wq_ref, wkv_ref, n_ref, q_ref, kv_ref):
    unit, _ = norm_stats(x_ref[...].astype(F32))
    normed = (unit * g1_ref[...]).astype(BF16)
    n_ref[...] = normed
    q_ref[...] = dot_nn(normed, wq_ref[...]).astype(BF16)
    kv_ref[...] = dot_nn(normed, wkv_ref[...]).astype(BF16)


def forward_kernel(sizes, tm, head_size, *refs):
    tables_ref, grad_ref, wo_ref, small_ref, taps_ref, g1_ref, wq_ref, wkv_ref = refs[:8]
    refs = refs[8:]
    x_refs = refs[:tm]
    q_refs, kv_refs = (refs[tm + k * (tm - 1) : tm + (k + 1) * (tm - 1)] for k in range(2))
    refs = refs[3 * tm - 2 :]
    half = tm // 2
    out_ref, n_last, q_last, kv_last = refs[:4]
    send_refs = refs[4 : 4 + tm][::-1]
    q_ref, kv_ref, tail_s, ctx_s, e_s, h_s, u_s, gr_s, gc_s, meta_ref, sem = refs[4 + tm :]
    fetch = pltpu.make_async_copy(tables_ref, meta_ref, sem)
    fetch.start()
    project(x_refs[-1], g1_ref, wq_ref, wkv_ref, n_last, q_last, kv_last)
    q_refs, kv_refs = (*q_refs, q_last), (*kv_refs, kv_last)
    fetch.wait()

    table = Layout(meta_ref, *sizes)
    me = table.me()
    local = table.blocks // tm
    width = out_ref.shape[1]
    hq = q_ref.shape[1]
    share = send_refs[0].shape[1]

    for ref in (q_ref, kv_ref):
        ref[: PAD * BLOCK] = jnp.zeros((PAD * BLOCK, ref.shape[1]), BF16)
    tail_s[:HALO] = jnp.zeros((HALO, width), BF16)
    for m in range(tm):
        for j in range(local):
            b = table.block_of((me ^ m) * local + j)
            here = slice(j * BLOCK, (j + 1) * BLOCK)
            q_ref[row_at(b)] = q_refs[m][here]
            kv_ref[row_at(b)] = kv_refs[m][here]
            after = pl.ds(pl.multiple_of((b + 1) * HALO, HALO), HALO)
            tail_s[after] = x_refs[m][(j + 1) * BLOCK - HALO : (j + 1) * BLOCK]

    mid_heads = 256 // BLOCK
    mid_f = diag_mask(mid_heads, BLOCK, head_size)
    mid_b = mid_f.astype(BF16)
    side_f = diag_mask(HEADS, HALO, head_size)
    side_b = side_f.astype(BF16)

    own = [table.block_of(me * local + i) for i in range(local)]
    keep = [jnp.where(table.position(c) >= 1, 1.0, 0.0).astype(F32) for c in own]
    for i, c in enumerate(own):
        for blk, shift, count, put in ((c - 1, HALO, HALO, 0), (c, 0, BLOCK, HALO)):
            reach = table.reach(blk)
            win = row_at(blk - LC, SPAN)
            at = row_at(blk, count, shift)
            if count == BLOCK:
                groups, mask_f, mask_b = HEADS // mid_heads, mid_f, mid_b
            else:
                groups, mask_f, mask_b = 1, side_f, side_b
            wide = hq // groups
            for g in range(groups):
                cols = slice(g * wide, (g + 1) * wide)
                vcols = slice(hq + g * wide, hq + (g + 1) * wide)
                probs, _ = window_probs(
                    spread(q_ref[at, cols], mask_b), kv_ref[win, cols], reach, head_size
                )
                full = dot_tn(probs.astype(BF16), kv_ref[win, vcols])
                ctx_s[i * ROWS + put : i * ROWS + put + count, cols] = fold_heads(
                    full, mask_f, count
                ).astype(BF16)

    gain = small_ref[KERNEL + 1 : KERNEL + 2]
    product = dot_nn(ctx_s[...], wo_ref[...])
    scales = []
    for i, c in enumerate(own):
        here = slice(i * ROWS, (i + 1) * ROWS)
        tail = tail_s[pl.ds(pl.multiple_of(c * HALO, HALO), HALO)]
        rows = jnp.concatenate([tail, x_refs[0][i * BLOCK : (i + 1) * BLOCK]], axis=0)
        hidden = rows.astype(F32) + product[here]
        unit, inv = norm_stats(hidden)
        conv_in = (unit * gain).astype(BF16).astype(F32)
        e_s[i * ROWS : i * ROWS + HALO] = conv_in[:HALO] * keep[i]
        e_s[i * ROWS + HALO : (i + 1) * ROWS] = conv_in[HALO:]
        h_s[i * BLOCK : (i + 1) * BLOCK] = hidden[HALO:]
        u_s[here] = unit
        scales.append(inv)

    groups = BLOCK // SUB

    def conv(k, carry):
        cols = pl.ds(pl.multiple_of(k * LANES, LANES), LANES)
        bias = jnp.broadcast_to(small_ref[KERNEL : KERNEL + 1, cols], (SUB, LANES))
        taps = lambda j: taps_ref[j * SUB : (j + 1) * SUB, cols]
        for i in range(local):
            ext = e_s[i * ROWS : (i + 1) * ROWS, cols]
            acc = [bias] * groups
            for s in range(SUB):
                reps = (KERNEL - s + SUB - 1) // SUB
                moved = ext[s + 2 : s + 2 + BLOCK + SUB * (reps - 1)]
                for a in range(reps):
                    tap = taps(SUB * a + s)
                    for r in range(groups):
                        piece = moved[(a + r) * SUB : (a + r + 1) * SUB]
                        acc[r] = acc[r] + tap * piece
            mixed = jnp.concatenate(acc, axis=0)
            gate = 0.5 * jnp.tanh(0.5 * mixed) + 0.5
            rows = slice(i * BLOCK, (i + 1) * BLOCK)
            out_ref[rows, cols] = (h_s[rows, cols] + mixed * gate).astype(BF16)
            slope = gate * (1.0 + mixed * (1.0 - gate))
            gm = grad_ref[rows, cols].astype(F32) * slope
            zeros = jnp.zeros((HALO, LANES), F32)
            padded = jnp.concatenate([zeros, gm, zeros], axis=0)
            back = [None] * (ROWS // SUB)
            low = HALO // SUB - 1
            for s in range(SUB):
                reps = (KERNEL - s + SUB - 1) // SUB
                start = low if s else low + 1
                moved = padded[start * SUB + s : ROWS + s]
                for a in range(reps):
                    tap = taps(KERNEL - 1 - SUB * a - s)
                    for g in range(start, ROWS // SUB):
                        r = g - a
                        piece = tap * moved[(g - start) * SUB : (g - start + 1) * SUB]
                        back[r] = piece if back[r] is None else back[r] + piece
            for r in range(ROWS // SUB):
                scale = keep[i] if r < HALO // SUB else 1.0
                gr_s[i * ROWS + r * SUB : i * ROWS + (r + 1) * SUB, cols] = back[r] * scale
        return carry

    lax.fori_loop(0, width // LANES, conv, 0)

    for i in range(local):
        here = slice(i * ROWS, (i + 1) * ROWS)
        scaled = gr_s[here] * gain
        unit = u_s[here]
        first = jnp.mean(scaled, axis=-1, keepdims=True)
        second = jnp.mean(scaled * unit, axis=-1, keepdims=True)
        back = scales[i] * (scaled - first - unit * second)
        own_grad = grad_ref[i * BLOCK : (i + 1) * BLOCK].astype(F32) + back[HALO:]
        gc_s[i * ROWS : i * ROWS + HALO] = back[:HALO].astype(BF16)
        gc_s[i * ROWS + HALO : (i + 1) * ROWS] = own_grad.astype(BF16)
    for m in range(half):
        at = pl.ds(pl.multiple_of(((me ^ m) % half) * share, share), share)
        grad_context = dot_nt(gc_s[...], wo_ref[at]).astype(BF16)
        send_refs[m][...] = grad_context
        send_refs[m + half][...] = grad_context


def probs_kernel(sizes, tm, head_size, meta_ref, *refs):
    q_refs, kv_refs = refs[:tm], refs[tm : 2 * tm]
    q4_ref, v4_ref, p_ref, d_ref, k4_ref = refs[2 * tm :]
    table = Layout(meta_ref, *sizes)
    me = table.me()
    local = table.blocks // tm
    hq = q_refs[0].shape[1]
    share = q4_ref.shape[1]
    lead = pl.multiple_of((me % (tm // 2)) * share, share)
    for ref in (k4_ref, v4_ref):
        ref[: PAD * BLOCK] = jnp.zeros((PAD * BLOCK, share), BF16)
    for m in range(tm):
        for j in range(local):
            at = row_at(table.block_of((me ^ m) * local + j))
            here = slice(j * BLOCK, (j + 1) * BLOCK)
            q4_ref[at] = q_refs[m][here, pl.ds(lead, share)]
            k4_ref[at] = kv_refs[m][here, pl.ds(lead, share)]
            v4_ref[at] = kv_refs[m][here, pl.ds(pl.multiple_of(hq + lead, share), share)]
    heads = share // head_size
    mask_b = diag_mask(heads, BLOCK, head_size).astype(BF16)
    for c in range(table.blocks):
        own = slice((c + PAD) * BLOCK, (c + PAD + 1) * BLOCK)
        win = slice((c + PAD - LC) * BLOCK, (c + PAD + 1) * BLOCK)
        diag_q = spread(q4_ref[own], mask_b)
        probs, unit = window_probs(diag_q, k4_ref[win], table.reach(c), head_size)
        p_ref[c] = probs
        d_ref[c] = (1.0 - unit * unit) * (1.0 / math.sqrt(head_size))


def backward_kernel(sizes, tm, part, head_size, *refs):
    meta_ref, q4_ref, v4_ref, p_ref, d_ref = refs[:5]
    n_refs = refs[5 : 5 + tm]
    g_refs = refs[5 + tm : 5 + 2 * tm][::-1]
    out_refs = refs[5 + 2 * tm : -3]
    gt_s, t_s, full_s = refs[-3:]
    table = Layout(meta_ref, *sizes)
    me = table.me()
    blocks = table.blocks
    local = blocks // tm
    share = q4_ref.shape[1]
    mask_b = diag_mask(share // head_size, BLOCK, head_size).astype(BF16)

    places = [(m, j, table.block_of((me ^ m) * local + j)) for m in range(tm) for j in range(local)]
    for m, j, b in places:
        gt_s[row_at(b)] = g_refs[m][j * ROWS + HALO : (j + 1) * ROWS].astype(F32)
    gt_s[(PAD - 1) * BLOCK : PAD * BLOCK] = jnp.zeros((BLOCK, share), F32)
    for m, j, b in places:
        at = row_at(b, HALO, -HALO)
        gt_s[at] = gt_s[at] + g_refs[m][j * ROWS : j * ROWS + HALO].astype(F32)
    t_s[...] = jnp.zeros(t_s.shape, F32)

    def spans(c):
        own = slice((c + PAD) * BLOCK, (c + PAD + 1) * BLOCK)
        win = slice((c + PAD - LC) * BLOCK, (c + PAD + 1) * BLOCK)
        return own, win, spread(gt_s[own].astype(BF16), mask_b)

    @pl.when(me >= tm // 2)
    def _():
        for c in range(blocks):
            own, win, diag_g = spans(c)
            t_s[win] = t_s[win] + dot_nn(p_ref[c].astype(BF16), diag_g)

    @pl.when(me < tm // 2)
    def _():
        for c in range(blocks):
            own, win, diag_g = spans(c)
            grad_probs = dot_nt(v4_ref[win], diag_g)
            probs = p_ref[c]
            delta = jnp.sum(probs * grad_probs, axis=0, keepdims=True)
            grad_raw = probs * (grad_probs - delta) * d_ref[c]
            t_s[win] = t_s[win] + dot_nn(grad_raw.astype(BF16), spread(q4_ref[own], mask_b))

    terms = jnp.concatenate([t_s[row_at(b)].astype(BF16) for _, _, b in places], axis=0)
    full = dot_tn(terms, jnp.concatenate([ref[...] for ref in n_refs], axis=0))
    if len(out_refs) == 1:
        out_refs[0][...] = full.astype(BF16)
        return
    full_s[...] = full
    chip, core = table.dp() // 2, table.dp() % 2
    for q in range(out_refs[0].shape[1] // part):
        for ref, side in zip(out_refs, (core, 1 - core)):
            at = pl.ds(pl.multiple_of(((chip ^ q) * 2 + side) * part, part), part)
            ref[:, q * part : (q + 1) * part] = full_s[:, at].astype(ref.dtype)


def pair_kernel(kept_ref, got_ref, *out_refs):
    part = out_refs[0].shape[1]
    for q, ref in enumerate(out_refs):
        cols = slice(q * part, (q + 1) * part)
        ref[...] = (kept_ref[:, cols] + got_ref[:, cols].astype(F32)).astype(ref.dtype)


def sum_kernel(*refs):
    total = refs[0][...].astype(F32)
    for ref in refs[1:-1]:
        total = total + ref[...].astype(F32)
    refs[-1][...] = total.T


def on_device(
    frames,
    out_grad,
    norm1_gain,
    w_query,
    w_kv,
    w_out,
    norm2_gain,
    conv_kernel,
    conv_bias,
    utt_blocks,
    block_slot,
    left_count,
):
    tm = lax.axis_size("tm")
    dp = lax.axis_size("dp")
    rows, width = frames.shape
    blocks = block_slot.shape[1]
    utts = utt_blocks.shape[1]
    sizes = (utts, blocks)
    local = rows // BLOCK
    hq = w_query.shape[1]
    head_size = hq // HEADS
    kv_width = w_kv.shape[1]
    share = kv_width // tm
    padded = (blocks + PAD) * BLOCK

    def swap(value, axis, size, m):
        return lax.ppermute(value, axis, [(i, i ^ m) for i in range(size)])

    meta = jnp.concatenate(
        [
            lax.axis_index("tm").astype(jnp.int32).reshape(1, 1),
            lax.axis_index("dp").astype(jnp.int32).reshape(1, 1),
            utt_blocks,
            block_slot,
            left_count,
        ],
        axis=1,
    )
    small = jnp.concatenate(
        [conv_kernel, conv_bias.reshape(1, -1), norm2_gain.reshape(1, -1)], axis=0
    )

    smem = pl.BlockSpec(memory_space=pltpu.SMEM)
    vmem = pl.BlockSpec(memory_space=pltpu.VMEM)
    shape = jax.ShapeDtypeStruct

    taps = pl.pallas_call(
        taps_kernel,
        out_shape=shape((KERNEL * SUB, width), F32),
        in_specs=[vmem],
        out_specs=vmem,
        compiler_params=pltpu.CompilerParams(vmem_limit_bytes=8 << 20),
        cost_estimate=pl.CostEstimate(flops=10**6, bytes_accessed=1 << 20, transcendentals=0),
        name="spread_taps",
    )(small)

    x, normed, queries, keys_values = {}, {}, {}, {}
    made = [shape((rows, w), BF16) for w in (width, hq, kv_width)]

    def project_shard(m, part):
        normed[m], queries[m], keys_values[m] = pl.pallas_call(
            project_kernel,
            out_shape=made,
            in_specs=[vmem] * 4,
            out_specs=[vmem] * 3,
            compiler_params=pltpu.CompilerParams(vmem_limit_bytes=16 << 20),
            cost_estimate=pl.CostEstimate(
                flops=2 * rows * width * (hq + kv_width), bytes_accessed=4 << 20, transcendentals=0
            ),
            name=f"project_rows_{m}",
        )(part, norm1_gain.reshape(1, -1), w_query, w_kv)

    project_shard(0, frames)
    x[0] = frames
    if tm == 4:
        x[2] = swap(frames, "tm", tm, 2)
        own, small = lax.optimization_barrier((frames, small))
        x[1] = swap(own, "tm", tm, 1)
        facing, normed[0], taps, meta = lax.optimization_barrier((x[2], normed[0], taps, meta))
        x[3] = swap(facing, "tm", tm, 1)
        project_shard(2, facing)
        project_shard(1, x[1])
    else:
        for m in range(1, tm):
            x[m] = swap(frames, "tm", tm, m)
            if m < tm - 1:
                project_shard(m, x[m])

    def by_m(arrays):
        return [arrays[m] for m in sorted(arrays)]

    own_rows = local * ROWS
    results = pl.pallas_call(
        functools.partial(forward_kernel, sizes, tm, head_size),
        out_shape=[shape((rows, width), BF16)]
        + made
        + [shape((own_rows, share), BF16)] * tm,
        in_specs=[pl.BlockSpec(memory_space=pl.ANY)] + [vmem] * (5 + 3 * tm),
        out_specs=[vmem] * (tm + 4),
        scratch_shapes=[
            pltpu.VMEM((padded, hq), BF16),
            pltpu.VMEM((padded, kv_width), BF16),
            pltpu.VMEM(((blocks + 1) * HALO, width), BF16),
            pltpu.VMEM((own_rows, hq), BF16),
            pltpu.VMEM((own_rows, width), F32),
            pltpu.VMEM((rows, width), F32),
            pltpu.VMEM((own_rows, width), F32),
            pltpu.VMEM((own_rows, width), F32),
            pltpu.VMEM((own_rows, width), BF16),
            pltpu.SMEM(meta.shape, jnp.int32),
            pltpu.SemaphoreType.DMA,
        ],
        compiler_params=pltpu.CompilerParams(vmem_limit_bytes=32 << 20),
        name="forward_pass",
    )(
        meta,
        out_grad,
        w_out,
        small,
        taps,
        norm1_gain.reshape(1, -1),
        w_query,
        w_kv,
        *by_m(x),
        *by_m(queries),
        *by_m(keys_values),
    )
    layer_out, normed[tm - 1], queries[tm - 1], keys_values[tm - 1] = results[:4]
    sends = results[:3:-1]
    got = {0: sends[0]}
    for m in range(tm - 1, 0, -1):
        got[m] = swap(sends[m], "tm", tm, m)

    pair_width = share // head_size * BLOCK
    q4, v4, probs, slopes = pl.pallas_call(
        functools.partial(probs_kernel, sizes, tm, head_size),
        out_shape=[shape((padded, share), BF16)] * 2
        + [shape((blocks, SPAN, pair_width), F32)] * 2,
        in_specs=[smem] + [vmem] * (2 * tm),
        out_specs=[vmem] * 4,
        scratch_shapes=[pltpu.VMEM((padded, share), BF16)],
        compiler_params=pltpu.CompilerParams(vmem_limit_bytes=24 << 20),
        name="window_probs",
        cost_estimate=pl.CostEstimate(
            flops=2 * 10**9, bytes_accessed=4 * 10**6, transcendentals=800000
        ),
    )(meta, *by_m(queries), *by_m(keys_values))

    direct = dp <= 8
    half_width = width // 2
    if direct:
        piece_shapes = [shape((share, half_width), F32), shape((share, half_width), BF16)]
    else:
        piece_shapes = [shape((share, width), BF16)]
    pieces = pl.pallas_call(
        functools.partial(backward_kernel, sizes, tm, width // dp, head_size),
        out_shape=piece_shapes,
        in_specs=[smem] + [vmem] * (4 + 2 * tm),
        out_specs=[vmem] * len(piece_shapes),
        scratch_shapes=[
            pltpu.VMEM((padded, share), F32),
            pltpu.VMEM((padded, share), F32),
            pltpu.VMEM((share, width), F32),
        ],
        compiler_params=pltpu.CompilerParams(vmem_limit_bytes=32 << 20),
        name="key_value_terms",
    )(meta, q4, v4, probs, slopes, *by_m(normed), *by_m(got)[::-1])

    if direct:
        kept, away = pieces
        arrived = swap(away, "dp", dp, 1)
        chips = dp // 2
        part = width // dp
        summed = pl.pallas_call(
            pair_kernel,
            out_shape=[shape((share, part), BF16)] * chips,
            in_specs=[vmem] * 2,
            out_specs=[vmem] * chips,
            compiler_params=pltpu.CompilerParams(vmem_limit_bytes=4 << 20),
            name="sum_pair",
        )(kept, arrived)
        terms = [swap(summed[q], "dp", dp, 2 * q) for q in range(chips - 1, 0, -1)]
        terms.append(summed[0])
    else:
        terms = [lax.psum_scatter(pieces[0], "dp", scatter_dimension=1, tiled=True)]
    kv_grad = pl.pallas_call(
        sum_kernel,
        out_shape=shape((width // dp, share), F32),
        in_specs=[vmem] * len(terms),
        out_specs=vmem,
        compiler_params=pltpu.CompilerParams(vmem_limit_bytes=4 << 20),
        name="sum_groups",
    )(*terms)
    return layer_out, kv_grad


def solution(mesh):
    return jax.shard_map(
        on_device,
        mesh=mesh,
        in_specs=(
            P(("dp", "tm"), None),
            P(("dp", "tm"), None),
            P(),
            P(),
            P(),
            P(),
            P(),
            P(),
            P(),
            P("dp", None),
            P("dp", None),
            P("dp", None),
        ),
        out_specs=(P(("dp", "tm"), None), P("dp", "tm")),
        check_vma=False,
    )
```

```python
import functools
import math

import jax
import jax.numpy as jnp
from jax import lax
from jax.experimental import pallas as pl
from jax.experimental.pallas import tpu as pltpu
from jax.sharding import PartitionSpec as P

HEADS = 8
KERNEL = 31
BLOCK = 64
LC = 2
SPAN = (LC + 1) * BLOCK
HALO = 32
ROWS = HALO + BLOCK
PAD = LC + 1
EPSILON = 1e-05
SOFT_CAP = 4.0
LANES = 128
SUB = 8

BF16 = jnp.bfloat16
F32 = jnp.float32


def dot_nn(a, b):
    return lax.dot_general(a, b, (((1,), (0,)), ((), ())), preferred_element_type=F32)


def dot_nt(a, b):
    return lax.dot_general(a, b, (((1,), (1,)), ((), ())), preferred_element_type=F32)


def dot_tn(a, b):
    return lax.dot_general(a, b, (((0,), (0,)), ((), ())), preferred_element_type=F32)


def norm_stats(values):
    row_mean = jnp.mean(values, axis=-1, keepdims=True)
    centred = values - row_mean
    scale_inv = lax.rsqrt(jnp.mean(centred * centred, axis=-1, keepdims=True) + EPSILON)
    return centred * scale_inv, scale_inv


class Layout:
    def __init__(self, meta_ref, utts, blocks):
        self.ref, self.utts, self.blocks = meta_ref, utts, blocks

    def me(self):
        return self.ref[0, 0]

    def dp(self):
        return self.ref[0, 1]

    def block_of(self, slot):
        found = jnp.int32(0)
        for b in range(self.blocks):
            found = jnp.where(self.ref[0, 2 + self.utts + b] == slot, jnp.int32(b), found)
        return found

    def position(self, block):
        start = jnp.int32(0)
        first = jnp.int32(0)
        for u in range(self.utts):
            first = jnp.where(block >= start, start, first)
            start = start + self.ref[0, 2 + u]
        return block - first

    def reach(self, block):
        safe = jnp.maximum(block, 0)
        left = self.ref[0, 2 + self.utts + self.blocks + safe]
        return jnp.minimum(left, self.position(safe))


def row_at(block, count=BLOCK, shift=0):
    return pl.ds(pl.multiple_of((block + PAD) * BLOCK + shift, math.gcd(BLOCK, shift)), count)


def diag_mask(heads, rows, head_size):
    shape = (heads * rows, heads * head_size)
    row_head = lax.broadcasted_iota(jnp.int32, shape, 0) // rows
    col_head = lax.broadcasted_iota(jnp.int32, shape, 1) // head_size
    return jnp.where(row_head == col_head, 1.0, 0.0).astype(F32)


def spread(rows, mask_b):
    copies = mask_b.shape[0] // rows.shape[0]
    return jnp.concatenate([rows] * copies, axis=0) * mask_b


def fold_heads(full, mask_f, rows):
    kept = full * mask_f
    total = kept[:rows]
    for h in range(1, full.shape[0] // rows):
        total = total + kept[h * rows : (h + 1) * rows]
    return total


def window_probs(diag_q, k_win, flags, head_size):
    raw = dot_nt(k_win, diag_q)
    unit = jnp.tanh(raw * (1.0 / (SOFT_CAP * math.sqrt(head_size))))
    exped = jnp.exp(SOFT_CAP * unit)
    parts = [exped[w * BLOCK : (w + 1) * BLOCK] * flags[w] for w in range(LC)]
    parts.append(exped[LC * BLOCK :])
    exped = jnp.concatenate(parts, axis=0)
    total = jnp.sum(exped, axis=0, keepdims=True)
    return exped * (1.0 / total), unit


def taps_kernel(small_ref, taps_ref):
    for j in range(KERNEL):
        rows = jnp.broadcast_to(small_ref[j : j + 1], (SUB, small_ref.shape[1]))
        taps_ref[j * SUB : (j + 1) * SUB] = rows


def project_kernel(x_ref, g1_ref, wq_ref, wkv_ref, n_ref, q_ref, kv_ref):
    project(x_ref, g1_ref, wq_ref, wkv_ref, n_ref, q_ref, kv_ref)


def project(x_ref, g1_ref, wq_ref, wkv_ref, n_ref, q_ref, kv_ref):
    unit, _ = norm_stats(x_ref[...].astype(F32))
    normed = (unit * g1_ref[...]).astype(BF16)
    n_ref[...] = normed
    q_ref[...] = dot_nn(normed, wq_ref[...]).astype(BF16)
    kv_ref[...] = dot_nn(normed, wkv_ref[...]).astype(BF16)


def forward_block(head_size, refs, windows, keep, scratch, out_rows):
    q_ref, kv_ref, x_tail, x_own, grad_ref, wo_ref, small_ref, taps_ref, out_ref = refs
    ctx_s, e_s, h_s, u_s, gr_s, gc_s = scratch
    hq = q_ref.shape[1]
    width = out_ref.shape[1]
    mid_heads = 256 // BLOCK
    mid_f = diag_mask(mid_heads, BLOCK, head_size)
    side_f = diag_mask(HEADS, HALO, head_size)
    for flags, first, rows, groups, mask_f in (
        (windows[0], 0, slice(0, HALO), 1, side_f),
        (windows[1], BLOCK, slice(HALO, ROWS), HEADS // mid_heads, mid_f),
    ):
        mask_b = mask_f.astype(BF16)
        win = slice(first, first + SPAN)
        wide = hq // groups
        for g in range(groups):
            cols = slice(g * wide, (g + 1) * wide)
            vcols = slice(hq + g * wide, hq + (g + 1) * wide)
            diag_q = spread(q_ref[rows, cols], mask_b)
            probs, _ = window_probs(diag_q, kv_ref[win, cols], flags, head_size)
            full = dot_tn(probs.astype(BF16), kv_ref[win, vcols])
            ctx_s[rows, cols] = fold_heads(full, mask_f, rows.stop - rows.start).astype(BF16)

    gain = small_ref[KERNEL + 1 : KERNEL + 2]
    hidden = jnp.concatenate([x_tail[...], x_own[...]], axis=0).astype(F32)
    hidden = hidden + dot_nn(ctx_s[...], wo_ref[...])
    unit, inv = norm_stats(hidden)
    conv_in = (unit * gain).astype(BF16).astype(F32)
    e_s[:HALO] = conv_in[:HALO] * keep
    e_s[HALO:] = conv_in[HALO:]
    h_s[...] = hidden[HALO:]
    u_s[...] = unit

    groups = BLOCK // SUB
    keep_lanes = keep[:, :LANES] if hasattr(keep, "shape") and keep.ndim else keep

    def conv(k, carry):
        cols = pl.ds(pl.multiple_of(k * LANES, LANES), LANES)
        bias = jnp.broadcast_to(small_ref[KERNEL : KERNEL + 1, cols], (SUB, LANES))
        taps = lambda j: taps_ref[j * SUB : (j + 1) * SUB, cols]
        ext = e_s[:, cols]
        acc = [bias] * groups
        for s in range(SUB):
            reps = (KERNEL - s + SUB - 1) // SUB
            moved = ext[s + 2 : s + 2 + BLOCK + SUB * (reps - 1)]
            for a in range(reps):
                tap = taps(SUB * a + s)
                for r in range(groups):
                    piece = moved[(a + r) * SUB : (a + r + 1) * SUB]
                    acc[r] = acc[r] + tap * piece
        mixed = jnp.concatenate(acc, axis=0)
        gate = 0.5 * jnp.tanh(0.5 * mixed) + 0.5
        out_ref[out_rows, cols] = (h_s[:, cols] + mixed * gate).astype(BF16)
        slope = gate * (1.0 + mixed * (1.0 - gate))
        gm = grad_ref[out_rows, cols].astype(F32) * slope
        zeros = jnp.zeros((HALO, LANES), F32)
        padded = jnp.concatenate([zeros, gm, zeros], axis=0)
        back = [None] * (ROWS // SUB)
        low = HALO // SUB - 1
        for s in range(SUB):
            reps = (KERNEL - s + SUB - 1) // SUB
            start = low if s else low + 1
            moved = padded[start * SUB + s : ROWS + s]
            for a in range(reps):
                tap = taps(KERNEL - 1 - SUB * a - s)
                for g in range(start, ROWS // SUB):
                    r = g - a
                    piece = tap * moved[(g - start) * SUB : (g - start + 1) * SUB]
                    back[r] = piece if back[r] is None else back[r] + piece
        for r in range(ROWS // SUB):
            value = back[r] * keep_lanes if r < HALO // SUB else back[r]
            gr_s[r * SUB : (r + 1) * SUB, cols] = value
        return carry

    lax.fori_loop(0, width // LANES, conv, 0)

    scaled = gr_s[...] * gain
    unit = u_s[...]
    first = jnp.mean(scaled, axis=-1, keepdims=True)
    second = jnp.mean(scaled * unit, axis=-1, keepdims=True)
    back = inv * (scaled - first - unit * second)
    own_grad = grad_ref[out_rows].astype(F32) + back[HALO:]
    gc_s[:HALO] = back[:HALO].astype(BF16)
    gc_s[HALO:] = own_grad.astype(BF16)


def grad_contexts(tm, picks, gc_s, wo_ref, share):
    half = tm // 2
    parts = [dot_nt(gc_s[...], wo_ref[h * share : (h + 1) * share]) for h in range(half)]
    made = []
    for m in range(half):
        total = parts[0] * picks[m]
        for h in range(1, half):
            total = total + parts[h] * picks[h ^ m]
        made.append(total.astype(BF16))
    return made * 2


def first_kernel(sizes, tm, head_size, *refs):
    tables_ref, grad_ref, wo_ref, small_ref, taps_ref, g1_ref, wq_ref, wkv_ref = refs[:8]
    refs = refs[8:]
    x_refs = refs[:tm]
    q_refs, kv_refs = (refs[tm + k * (tm - 1) : tm + (k + 1) * (tm - 1)] for k in range(2))
    refs = refs[3 * tm - 2 :]
    out_ref, n_last, q_last, kv_last, q_next, kv_next, tail_next, flags_next = refs[:8]
    send_refs = refs[8 : 8 + tm]
    q_ref, kv_ref, tail_s, *scratch = refs[8 + tm : -2]
    meta_ref, sem = refs[-2:]
    fetch = pltpu.make_async_copy(tables_ref, meta_ref, sem)
    fetch.start()
    project(x_refs[-1], g1_ref, wq_ref, wkv_ref, n_last, q_last, kv_last)
    q_refs, kv_refs = (*q_refs, q_last), (*kv_refs, kv_last)
    fetch.wait()

    table = Layout(meta_ref, *sizes)
    me = table.me()
    local = table.blocks // tm
    width = out_ref.shape[1]
    share = send_refs[0].shape[1]
    for ref in (q_ref, kv_ref):
        ref[: PAD * BLOCK] = jnp.zeros((PAD * BLOCK, ref.shape[1]), BF16)
    tail_s[:HALO] = jnp.zeros((HALO, width), BF16)
    for m in range(tm):
        for j in range(local):
            b = table.block_of((me ^ m) * local + j)
            here = slice(j * BLOCK, (j + 1) * BLOCK)
            q_ref[row_at(b)] = q_refs[m][here]
            kv_ref[row_at(b)] = kv_refs[m][here]
            after = pl.ds(pl.multiple_of((b + 1) * HALO, HALO), HALO)
            tail_s[after] = x_refs[m][(j + 1) * BLOCK - HALO : (j + 1) * BLOCK]

    def one(flag):
        return jnp.where(flag, 1.0, 0.0).astype(F32)

    def places(c):
        tail = pl.ds(pl.multiple_of(c * HALO, HALO), HALO)
        return row_at(c, ROWS, -HALO), row_at(c - PAD, SPAN + BLOCK), tail

    def flags_of(c):
        windows = [[one(table.reach(b) >= LC - w) for w in range(LC)] for b in (c - 1, c)]
        return windows, one(table.position(c) >= 1)

    c = table.block_of(me * local + 1)
    q_at, kv_at, tail_at = places(c)
    q_next[...] = q_ref[q_at]
    kv_next[...] = kv_ref[kv_at]
    tail_next[...] = tail_s[tail_at]
    windows, keep = flags_of(c)
    picks = [one(me % (tm // 2) == h) for h in range(tm // 2)]
    for k, flag in enumerate([*windows[0], *windows[1], keep, *picks]):
        flags_next[k : k + 1] = jnp.full((1, width), 1.0, F32) * flag

    c = table.block_of(me * local)
    q_at, kv_at, tail_at = places(c)
    windows, keep = flags_of(c)
    block_refs = (
        q_ref.at[q_at],
        kv_ref.at[kv_at],
        tail_s.at[tail_at],
        x_refs[0].at[pl.ds(0, BLOCK)],
        grad_ref,
        wo_ref,
        small_ref,
        taps_ref,
        out_ref,
    )
    forward_block(head_size, block_refs, windows, keep, scratch, slice(0, BLOCK))
    for ref, value in zip(send_refs, grad_contexts(tm, picks, scratch[-1], wo_ref, share)):
        ref[...] = value


def second_kernel(tm, head_size, *refs):
    grad_ref, wo_ref, small_ref, taps_ref, x_ref = refs[:5]
    q_ref, kv_ref, tail_ref, flags_ref, out_first, own_first, near_first = refs[5:12]
    out_ref = refs[12]
    send_refs = refs[13 : 13 + tm]
    scratch = refs[13 + tm :]
    windows = [[flags_ref[k * LC + w : k * LC + w + 1, :256] for w in range(LC)] for k in range(2)]
    keep = flags_ref[2 * LC : 2 * LC + 1]
    block_refs = (
        q_ref,
        kv_ref,
        tail_ref,
        x_ref.at[pl.ds(BLOCK, BLOCK)],
        grad_ref,
        wo_ref,
        small_ref,
        taps_ref,
        out_ref,
    )
    out_ref[:BLOCK] = out_first[...]
    forward_block(head_size, block_refs, windows, keep, scratch, slice(BLOCK, 2 * BLOCK))
    share = send_refs[0].shape[1]
    place = 2 * LC + 1
    picks = [flags_ref[place + h : place + h + 1, :share] for h in range(tm // 2)]
    made = grad_contexts(tm, picks, scratch[-1], wo_ref, share)
    for m, (ref, value) in enumerate(zip(send_refs, made)):
        if m < 2:
            ref[:ROWS] = (own_first, near_first)[m][...]
            ref[ROWS:] = value
        else:
            ref[...] = value


def probs_kernel(sizes, tm, head_size, meta_ref, *refs):
    q_refs, kv_refs = refs[:tm], refs[tm : 2 * tm]
    q4_ref, v4_ref, p_ref, d_ref, k4_ref = refs[2 * tm :]
    table = Layout(meta_ref, *sizes)
    me = table.me()
    local = table.blocks // tm
    hq = q_refs[0].shape[1]
    share = q4_ref.shape[1]
    lead = pl.multiple_of((me % (tm // 2)) * share, share)
    for ref in (k4_ref, v4_ref):
        ref[: PAD * BLOCK] = jnp.zeros((PAD * BLOCK, share), BF16)
    for m in range(tm):
        for j in range(local):
            at = row_at(table.block_of((me ^ m) * local + j))
            here = slice(j * BLOCK, (j + 1) * BLOCK)
            q4_ref[at] = q_refs[m][here, pl.ds(lead, share)]
            k4_ref[at] = kv_refs[m][here, pl.ds(lead, share)]
            v4_ref[at] = kv_refs[m][here, pl.ds(pl.multiple_of(hq + lead, share), share)]
    heads = share // head_size
    mask_b = diag_mask(heads, BLOCK, head_size).astype(BF16)
    for c in range(table.blocks):
        own = slice((c + PAD) * BLOCK, (c + PAD + 1) * BLOCK)
        win = slice((c + PAD - LC) * BLOCK, (c + PAD + 1) * BLOCK)
        diag_q = spread(q4_ref[own], mask_b)
        reach = table.reach(c)
        flags = [jnp.where(reach >= LC - w, 1.0, 0.0).astype(F32) for w in range(LC)]
        probs, unit = window_probs(diag_q, k4_ref[win], flags, head_size)
        p_ref[c] = probs
        d_ref[c] = (1.0 - unit * unit) * (1.0 / math.sqrt(head_size))


def backward_kernel(sizes, tm, part, head_size, *refs):
    meta_ref, q4_ref, v4_ref, p_ref, d_ref = refs[:5]
    n_refs = refs[5 : 5 + tm]
    far = 2 * (tm - 2)
    g_far = refs[5 + tm : 5 + tm + far]
    g_refs = [((ref, 0), (ref, ROWS)) for ref in refs[5 + tm + far : 7 + tm + far][::-1]]
    g_refs += [((g_far[2 * k], 0), (g_far[2 * k + 1], 0)) for k in range(tm - 2)]
    out_refs = refs[7 + tm + far : -3]
    gt_s, t_s, full_s = refs[-3:]
    table = Layout(meta_ref, *sizes)
    me = table.me()
    blocks = table.blocks
    local = blocks // tm
    share = q4_ref.shape[1]
    mask_b = diag_mask(share // head_size, BLOCK, head_size).astype(BF16)

    places = [(m, j, table.block_of((me ^ m) * local + j)) for m in range(tm) for j in range(local)]
    for m, j, b in places:
        ref, top = g_refs[m][j]
        gt_s[row_at(b)] = ref[top + HALO : top + ROWS].astype(F32)
    gt_s[(PAD - 1) * BLOCK : PAD * BLOCK] = jnp.zeros((BLOCK, share), F32)
    for m, j, b in places:
        at = row_at(b, HALO, -HALO)
        ref, top = g_refs[m][j]
        gt_s[at] = gt_s[at] + ref[top : top + HALO].astype(F32)
    t_s[...] = jnp.zeros(t_s.shape, F32)

    def spans(c):
        own = slice((c + PAD) * BLOCK, (c + PAD + 1) * BLOCK)
        win = slice((c + PAD - LC) * BLOCK, (c + PAD + 1) * BLOCK)
        return own, win, spread(gt_s[own].astype(BF16), mask_b)

    @pl.when(me >= tm // 2)
    def _():
        for c in range(blocks):
            own, win, diag_g = spans(c)
            t_s[win] = t_s[win] + dot_nn(p_ref[c].astype(BF16), diag_g)

    @pl.when(me < tm // 2)
    def _():
        for c in range(blocks):
            own, win, diag_g = spans(c)
            grad_probs = dot_nt(v4_ref[win], diag_g)
            probs = p_ref[c]
            delta = jnp.sum(probs * grad_probs, axis=0, keepdims=True)
            grad_raw = probs * (grad_probs - delta) * d_ref[c]
            t_s[win] = t_s[win] + dot_nn(grad_raw.astype(BF16), spread(q4_ref[own], mask_b))

    terms = jnp.concatenate([t_s[row_at(b)].astype(BF16) for _, _, b in places], axis=0)
    full = dot_tn(terms, jnp.concatenate([ref[...] for ref in n_refs], axis=0))
    if len(out_refs) == 1:
        out_refs[0][...] = full.astype(BF16)
        return
    full_s[...] = full
    chip, core = table.dp() // 2, table.dp() % 2
    for q in range(out_refs[0].shape[1] // part):
        for ref, side in zip(out_refs, (core, 1 - core)):
            at = pl.ds(pl.multiple_of(((chip ^ q) * 2 + side) * part, part), part)
            ref[:, q * part : (q + 1) * part] = full_s[:, at].astype(ref.dtype)


def pair_kernel(kept_ref, got_ref, *out_refs):
    part = out_refs[0].shape[1]
    for q, ref in enumerate(out_refs):
        cols = slice(q * part, (q + 1) * part)
        ref[...] = (kept_ref[:, cols] + got_ref[:, cols].astype(F32)).astype(ref.dtype)


def sum_kernel(*refs):
    total = refs[0][...].astype(F32)
    for ref in refs[1:-1]:
        total = total + ref[...].astype(F32)
    refs[-1][...] = total.T


def on_device(
    frames,
    out_grad,
    norm1_gain,
    w_query,
    w_kv,
    w_out,
    norm2_gain,
    conv_kernel,
    conv_bias,
    utt_blocks,
    block_slot,
    left_count,
):
    tm = lax.axis_size("tm")
    dp = lax.axis_size("dp")
    rows, width = frames.shape
    blocks = block_slot.shape[1]
    utts = utt_blocks.shape[1]
    sizes = (utts, blocks)
    local = rows // BLOCK
    hq = w_query.shape[1]
    head_size = hq // HEADS
    kv_width = w_kv.shape[1]
    share = kv_width // tm
    padded = (blocks + PAD) * BLOCK

    def swap(value, axis, size, m):
        return lax.ppermute(value, axis, [(i, i ^ m) for i in range(size)])

    meta = jnp.concatenate(
        [
            lax.axis_index("tm").astype(jnp.int32).reshape(1, 1),
            lax.axis_index("dp").astype(jnp.int32).reshape(1, 1),
            utt_blocks,
            block_slot,
            left_count,
        ],
        axis=1,
    )
    small = jnp.concatenate(
        [conv_kernel, conv_bias.reshape(1, -1), norm2_gain.reshape(1, -1)], axis=0
    )

    smem = pl.BlockSpec(memory_space=pltpu.SMEM)
    vmem = pl.BlockSpec(memory_space=pltpu.VMEM)
    shape = jax.ShapeDtypeStruct

    taps = pl.pallas_call(
        taps_kernel,
        out_shape=shape((KERNEL * SUB, width), F32),
        in_specs=[vmem],
        out_specs=vmem,
        compiler_params=pltpu.CompilerParams(vmem_limit_bytes=8 << 20),
        cost_estimate=pl.CostEstimate(flops=10**6, bytes_accessed=1 << 20, transcendentals=0),
        name="spread_taps",
    )(small)

    x, normed, queries, keys_values = {}, {}, {}, {}
    made = [shape((rows, w), BF16) for w in (width, hq, kv_width)]

    def project_shard(m, part):
        normed[m], queries[m], keys_values[m] = pl.pallas_call(
            project_kernel,
            out_shape=made,
            in_specs=[vmem] * 4,
            out_specs=[vmem] * 3,
            compiler_params=pltpu.CompilerParams(vmem_limit_bytes=16 << 20),
            cost_estimate=pl.CostEstimate(
                flops=2 * rows * width * (hq + kv_width), bytes_accessed=4 << 20, transcendentals=0
            ),
            name=f"project_rows_{m}",
        )(part, norm1_gain.reshape(1, -1), w_query, w_kv)

    project_shard(0, frames)
    x[0] = frames
    if tm == 4:
        x[2] = swap(frames, "tm", tm, 2)
        own, normed[0] = lax.optimization_barrier((frames, normed[0]))
        x[1] = swap(own, "tm", tm, 1)
        facing, normed[0], taps, meta = lax.optimization_barrier((x[2], normed[0], taps, meta))
        x[3] = swap(facing, "tm", tm, 1)
        project_shard(2, facing)
        project_shard(1, x[1])
    else:
        for m in range(1, tm):
            x[m] = swap(frames, "tm", tm, m)
            if m < tm - 1:
                project_shard(m, x[m])

    def by_m(arrays):
        return [arrays[m] for m in sorted(arrays)]

    scratch = [
        pltpu.VMEM((ROWS, hq), BF16),
        pltpu.VMEM((ROWS, width), F32),
        pltpu.VMEM((BLOCK, width), F32),
        pltpu.VMEM((ROWS, width), F32),
        pltpu.VMEM((ROWS, width), F32),
        pltpu.VMEM((ROWS, width), BF16),
    ]
    sent = shape((ROWS, share), BF16)
    results = pl.pallas_call(
        functools.partial(first_kernel, sizes, tm, head_size),
        out_shape=[shape((BLOCK, width), BF16)]
        + made
        + [
            shape((ROWS, hq), BF16),
            shape((SPAN + BLOCK, kv_width), BF16),
            shape((HALO, width), BF16),
            shape((2 * SUB, width), F32),
        ]
        + [sent] * tm,
        in_specs=[pl.BlockSpec(memory_space=pl.ANY)] + [vmem] * (5 + 3 * tm),
        out_specs=[vmem] * (tm + 8),
        scratch_shapes=[
            pltpu.VMEM((padded, hq), BF16),
            pltpu.VMEM((padded, kv_width), BF16),
            pltpu.VMEM(((blocks + 1) * HALO, width), BF16),
            *scratch,
            pltpu.SMEM(meta.shape, jnp.int32),
            pltpu.SemaphoreType.DMA,
        ],
        compiler_params=pltpu.CompilerParams(vmem_limit_bytes=28 << 20),
        name="first_block",
    )(
        meta,
        out_grad,
        w_out,
        small,
        taps,
        norm1_gain.reshape(1, -1),
        w_query,
        w_kv,
        *by_m(x),
        *by_m(queries),
        *by_m(keys_values),
    )
    out_first, normed[tm - 1], queries[tm - 1], keys_values[tm - 1] = results[:4]
    laid_out, early = results[4:8], results[8:]
    both = shape((local * ROWS, share), BF16)
    results = pl.pallas_call(
        functools.partial(second_kernel, tm, head_size),
        out_shape=[shape((rows, width), BF16)] + [both] * 2 + [sent] * (tm - 2),
        in_specs=[vmem] * 12,
        out_specs=[vmem] * (tm + 1),
        scratch_shapes=scratch,
        compiler_params=pltpu.CompilerParams(vmem_limit_bytes=16 << 20),
        cost_estimate=pl.CostEstimate(flops=1, bytes_accessed=1, transcendentals=0),
        name="second_block",
    )(out_grad, w_out, small, taps, frames, *laid_out, out_first, early[0], early[1])
    layer_out, late = results[0], results[1:]
    got_early = [swap(early[m], "tm", tm, m) for m in range(2, tm)]
    *late, got_early = lax.optimization_barrier((*late, got_early))
    got_far = []
    for m in range(2, tm):
        got_far += [got_early[m - 2], swap(late[m], "tm", tm, m)]
    got_near = [swap(late[1], "tm", tm, 1), late[0]]

    pair_width = share // head_size * BLOCK
    q4, v4, probs, slopes = pl.pallas_call(
        functools.partial(probs_kernel, sizes, tm, head_size),
        out_shape=[shape((padded, share), BF16)] * 2
        + [shape((blocks, SPAN, pair_width), F32)] * 2,
        in_specs=[smem] + [vmem] * (2 * tm),
        out_specs=[vmem] * 4,
        scratch_shapes=[pltpu.VMEM((padded, share), BF16)],
        compiler_params=pltpu.CompilerParams(vmem_limit_bytes=24 << 20),
        name="window_probs",
        cost_estimate=pl.CostEstimate(flops=1, bytes_accessed=1, transcendentals=0),
    )(meta, *by_m(queries), *by_m(keys_values))

    direct = dp <= 8
    half_width = width // 2
    if direct:
        piece_shapes = [shape((share, half_width), F32), shape((share, half_width), BF16)]
    else:
        piece_shapes = [shape((share, width), BF16)]
    pieces = pl.pallas_call(
        functools.partial(backward_kernel, sizes, tm, width // dp, head_size),
        out_shape=piece_shapes,
        in_specs=[smem] + [vmem] * (6 + tm + len(got_far)),
        out_specs=[vmem] * len(piece_shapes),
        scratch_shapes=[
            pltpu.VMEM((padded, share), F32),
            pltpu.VMEM((padded, share), F32),
            pltpu.VMEM((share, width), F32),
        ],
        compiler_params=pltpu.CompilerParams(vmem_limit_bytes=32 << 20),
        name="key_value_terms",
    )(meta, q4, v4, probs, slopes, *by_m(normed), *got_far, *got_near)

    if direct:
        kept, away = pieces
        arrived = swap(away, "dp", dp, 1)
        chips = dp // 2
        part = width // dp
        summed = pl.pallas_call(
            pair_kernel,
            out_shape=[shape((share, part), BF16)] * chips,
            in_specs=[vmem] * 2,
            out_specs=[vmem] * chips,
            compiler_params=pltpu.CompilerParams(vmem_limit_bytes=4 << 20),
            name="sum_pair",
        )(kept, arrived)
        terms = [swap(summed[q], "dp", dp, 2 * q) for q in range(chips - 1, 0, -1)]
        terms.append(summed[0])
    else:
        terms = [lax.psum_scatter(pieces[0], "dp", scatter_dimension=1, tiled=True)]
    kv_grad = pl.pallas_call(
        sum_kernel,
        out_shape=shape((width // dp, share), F32),
        in_specs=[vmem] * len(terms),
        out_specs=vmem,
        compiler_params=pltpu.CompilerParams(vmem_limit_bytes=4 << 20),
        name="sum_groups",
    )(*terms)
    return layer_out, kv_grad


def solution(mesh):
    return jax.shard_map(
        on_device,
        mesh=mesh,
        in_specs=(
            P(("dp", "tm"), None),
            P(("dp", "tm"), None),
            P(),
            P(),
            P(),
            P(),
            P(),
            P(),
            P(),
            P("dp", None),
            P("dp", None),
            P("dp", None),
        ),
        out_specs=(P(("dp", "tm"), None), P("dp", "tm")),
        check_vma=False,
    )
```

```python
import functools
import math

import jax
import jax.numpy as jnp
from jax import lax
from jax.experimental import pallas as pl
from jax.experimental.pallas import tpu as pltpu
from jax.sharding import PartitionSpec as P

HEADS = 8
KERNEL = 31
BLOCK = 64
LC = 2
SPAN = (LC + 1) * BLOCK
HALO = 32
ROWS = HALO + BLOCK
PAD = LC + 1
EPSILON = 1e-05
SOFT_CAP = 4.0
LANES = 128
SUB = 8

BF16 = jnp.bfloat16
F32 = jnp.float32


def dot_nn(a, b):
    return lax.dot_general(a, b, (((1,), (0,)), ((), ())), preferred_element_type=F32)


def dot_nt(a, b):
    return lax.dot_general(a, b, (((1,), (1,)), ((), ())), preferred_element_type=F32)


def dot_tn(a, b):
    return lax.dot_general(a, b, (((0,), (0,)), ((), ())), preferred_element_type=F32)


def norm_stats(values):
    row_mean = jnp.mean(values, axis=-1, keepdims=True)
    centred = values - row_mean
    scale_inv = lax.rsqrt(jnp.mean(centred * centred, axis=-1, keepdims=True) + EPSILON)
    return centred * scale_inv, scale_inv


class Layout:
    def __init__(self, meta_ref, utts, blocks):
        self.ref, self.utts, self.blocks = meta_ref, utts, blocks

    def me(self):
        return self.ref[0, 0]

    def dp(self):
        return self.ref[0, 1]

    def block_of(self, slot):
        found = jnp.int32(0)
        for b in range(self.blocks):
            found = jnp.where(self.ref[0, 2 + self.utts + b] == slot, jnp.int32(b), found)
        return found

    def position(self, block):
        start = jnp.int32(0)
        first = jnp.int32(0)
        for u in range(self.utts):
            first = jnp.where(block >= start, start, first)
            start = start + self.ref[0, 2 + u]
        return block - first

    def reach(self, block):
        safe = jnp.maximum(block, 0)
        left = self.ref[0, 2 + self.utts + self.blocks + safe]
        return jnp.minimum(left, self.position(safe))


def row_at(block, count=BLOCK, shift=0):
    return pl.ds(pl.multiple_of((block + PAD) * BLOCK + shift, math.gcd(BLOCK, shift)), count)


def diag_mask(heads, rows, head_size):
    shape = (heads * rows, heads * head_size)
    row_head = lax.broadcasted_iota(jnp.int32, shape, 0) // rows
    col_head = lax.broadcasted_iota(jnp.int32, shape, 1) // head_size
    return jnp.where(row_head == col_head, 1.0, 0.0).astype(F32)


def spread(rows, mask_b):
    copies = mask_b.shape[0] // rows.shape[0]
    return jnp.concatenate([rows] * copies, axis=0) * mask_b


def fold_heads(full, mask_f, rows):
    kept = full * mask_f
    total = kept[:rows]
    for h in range(1, full.shape[0] // rows):
        total = total + kept[h * rows : (h + 1) * rows]
    return total


def window_probs(diag_q, k_win, reach, head_size):
    raw = dot_nt(k_win, diag_q)
    unit = jnp.tanh(raw * (1.0 / (SOFT_CAP * math.sqrt(head_size))))
    exped = jnp.exp(SOFT_CAP * unit)
    parts = []
    for w in range(LC):
        ok = jnp.where(reach >= LC - w, 1.0, 0.0).astype(F32)
        parts.append(exped[w * BLOCK : (w + 1) * BLOCK] * ok)
    parts.append(exped[LC * BLOCK :])
    exped = jnp.concatenate(parts, axis=0)
    total = jnp.sum(exped, axis=0, keepdims=True)
    return exped * (1.0 / total), unit


def taps_kernel(small_ref, taps_ref):
    for j in range(KERNEL):
        rows = jnp.broadcast_to(small_ref[j : j + 1], (SUB, small_ref.shape[1]))
        taps_ref[j * SUB : (j + 1) * SUB] = rows


def project_kernel(x_ref, g1_ref, wq_ref, wkv_ref, n_ref, q_ref, kv_ref):
    project(x_ref, g1_ref, wq_ref, wkv_ref, n_ref, q_ref, kv_ref)


def project(x_ref, g1_ref, wq_ref, wkv_ref, n_ref, q_ref, kv_ref):
    unit, _ = norm_stats(x_ref[...].astype(F32))
    normed = (unit * g1_ref[...]).astype(BF16)
    n_ref[...] = normed
    q_ref[...] = dot_nn(normed, wq_ref[...]).astype(BF16)
    kv_ref[...] = dot_nn(normed, wkv_ref[...]).astype(BF16)


def forward_kernel(sizes, tm, head_size, *refs):
    tables_ref, grad_ref, wo_ref, small_ref, taps_ref, g1_ref, wq_ref, wkv_ref = refs[:8]
    refs = refs[8:]
    x_refs = refs[:tm]
    q_refs, kv_refs = (refs[tm + k * (tm - 1) : tm + (k + 1) * (tm - 1)] for k in range(2))
    refs = refs[3 * tm - 2 :]
    half = tm // 2
    out_ref, n_last, q_last, kv_last = refs[:4]
    send_refs = refs[4 : 4 + tm][::-1]
    q_ref, kv_ref, tail_s, ctx_s, e_s, h_s, u_s, gr_s, gc_s, meta_ref, sem = refs[4 + tm :]
    fetch = pltpu.make_async_copy(tables_ref, meta_ref, sem)
    fetch.start()
    project(x_refs[-1], g1_ref, wq_ref, wkv_ref, n_last, q_last, kv_last)
    q_refs, kv_refs = (*q_refs, q_last), (*kv_refs, kv_last)
    fetch.wait()

    table = Layout(meta_ref, *sizes)
    me = table.me()
    local = table.blocks // tm
    width = out_ref.shape[1]
    hq = q_ref.shape[1]
    share = send_refs[0].shape[1]

    for ref in (q_ref, kv_ref):
        ref[: PAD * BLOCK] = jnp.zeros((PAD * BLOCK, ref.shape[1]), BF16)
    tail_s[:HALO] = jnp.zeros((HALO, width), BF16)
    for m in range(tm):
        for j in range(local):
            b = table.block_of((me ^ m) * local + j)
            here = slice(j * BLOCK, (j + 1) * BLOCK)
            q_ref[row_at(b)] = q_refs[m][here]
            kv_ref[row_at(b)] = kv_refs[m][here]
            after = pl.ds(pl.multiple_of((b + 1) * HALO, HALO), HALO)
            tail_s[after] = x_refs[m][(j + 1) * BLOCK - HALO : (j + 1) * BLOCK]

    mid_heads = 256 // BLOCK
    mid_f = diag_mask(mid_heads, BLOCK, head_size)
    mid_b = mid_f.astype(BF16)
    side_f = diag_mask(HEADS, HALO, head_size)
    side_b = side_f.astype(BF16)

    own = [table.block_of(me * local + i) for i in range(local)]
    keep = [jnp.where(table.position(c) >= 1, 1.0, 0.0).astype(F32) for c in own]
    for i, c in enumerate(own):
        for blk, shift, count, put in ((c - 1, HALO, HALO, 0), (c, 0, BLOCK, HALO)):
            reach = table.reach(blk)
            win = row_at(blk - LC, SPAN)
            at = row_at(blk, count, shift)
            if count == BLOCK:
                groups, mask_f, mask_b = HEADS // mid_heads, mid_f, mid_b
            else:
                groups, mask_f, mask_b = 1, side_f, side_b
            wide = hq // groups
            for g in range(groups):
                cols = slice(g * wide, (g + 1) * wide)
                vcols = slice(hq + g * wide, hq + (g + 1) * wide)
                probs, _ = window_probs(
                    spread(q_ref[at, cols], mask_b), kv_ref[win, cols], reach, head_size
                )
                full = dot_tn(probs.astype(BF16), kv_ref[win, vcols])
                ctx_s[i * ROWS + put : i * ROWS + put + count, cols] = fold_heads(
                    full, mask_f, count
                ).astype(BF16)

    gain = small_ref[KERNEL + 1 : KERNEL + 2]
    product = dot_nn(ctx_s[...], wo_ref[...])
    scales = []
    for i, c in enumerate(own):
        here = slice(i * ROWS, (i + 1) * ROWS)
        tail = tail_s[pl.ds(pl.multiple_of(c * HALO, HALO), HALO)]
        rows = jnp.concatenate([tail, x_refs[0][i * BLOCK : (i + 1) * BLOCK]], axis=0)
        hidden = rows.astype(F32) + product[here]
        unit, inv = norm_stats(hidden)
        conv_in = (unit * gain).astype(BF16).astype(F32)
        e_s[i * ROWS : i * ROWS + HALO] = conv_in[:HALO] * keep[i]
        e_s[i * ROWS + HALO : (i + 1) * ROWS] = conv_in[HALO:]
        h_s[i * BLOCK : (i + 1) * BLOCK] = hidden[HALO:]
        u_s[here] = unit
        scales.append(inv)

    groups = BLOCK // SUB

    def conv(cols):
        bias = jnp.broadcast_to(small_ref[KERNEL : KERNEL + 1, cols], (SUB, LANES))
        taps = lambda j: taps_ref[j * SUB : (j + 1) * SUB, cols]
        for i in range(local):
            ext = e_s[i * ROWS : (i + 1) * ROWS, cols]
            acc = [bias] * groups
            for s in range(SUB):
                reps = (KERNEL - s + SUB - 1) // SUB
                moved = ext[s + 2 : s + 2 + BLOCK + SUB * (reps - 1)]
                for a in range(reps):
                    tap = taps(SUB * a + s)
                    for r in range(groups):
                        piece = moved[(a + r) * SUB : (a + r + 1) * SUB]
                        acc[r] = acc[r] + tap * piece
            mixed = jnp.concatenate(acc, axis=0)
            gate = 0.5 * jnp.tanh(0.5 * mixed) + 0.5
            rows = slice(i * BLOCK, (i + 1) * BLOCK)
            out_ref[rows, cols] = (h_s[rows, cols] + mixed * gate).astype(BF16)
            slope = gate * (1.0 + mixed * (1.0 - gate))
            gm = grad_ref[rows, cols].astype(F32) * slope
            zeros = jnp.zeros((HALO, LANES), F32)
            padded = jnp.concatenate([zeros, gm, zeros], axis=0)
            back = [None] * (ROWS // SUB)
            low = HALO // SUB - 1
            for s in range(SUB):
                reps = (KERNEL - s + SUB - 1) // SUB
                start = low if s else low + 1
                moved = padded[start * SUB + s : ROWS + s]
                for a in range(reps):
                    tap = taps(KERNEL - 1 - SUB * a - s)
                    for g in range(start, ROWS // SUB):
                        r = g - a
                        piece = tap * moved[(g - start) * SUB : (g - start + 1) * SUB]
                        back[r] = piece if back[r] is None else back[r] + piece
            for r in range(ROWS // SUB):
                scale = keep[i] if r < HALO // SUB else 1.0
                gr_s[i * ROWS + r * SUB : i * ROWS + (r + 1) * SUB, cols] = back[r] * scale

    for k in range(0, width, LANES):
        conv(slice(k, k + LANES))

    for i in range(local):
        here = slice(i * ROWS, (i + 1) * ROWS)
        scaled = gr_s[here] * gain
        unit = u_s[here]
        first = jnp.mean(scaled, axis=-1, keepdims=True)
        second = jnp.mean(scaled * unit, axis=-1, keepdims=True)
        back = scales[i] * (scaled - first - unit * second)
        own_grad = grad_ref[i * BLOCK : (i + 1) * BLOCK].astype(F32) + back[HALO:]
        gc_s[i * ROWS : i * ROWS + HALO] = back[:HALO].astype(BF16)
        gc_s[i * ROWS + HALO : (i + 1) * ROWS] = own_grad.astype(BF16)
    for m in range(half):
        at = pl.ds(pl.multiple_of(((me ^ m) % half) * share, share), share)
        grad_context = dot_nt(gc_s[...], wo_ref[at]).astype(BF16)
        send_refs[m][...] = grad_context
        send_refs[m + half][...] = grad_context


def probs_kernel(sizes, tm, head_size, meta_ref, *refs):
    q_refs, kv_refs = refs[:tm], refs[tm : 2 * tm]
    q4_ref, v4_ref, p_ref, d_ref, k4_ref = refs[2 * tm :]
    table = Layout(meta_ref, *sizes)
    me = table.me()
    local = table.blocks // tm
    hq = q_refs[0].shape[1]
    share = q4_ref.shape[1]
    lead = pl.multiple_of((me % (tm // 2)) * share, share)
    for ref in (k4_ref, v4_ref):
        ref[: PAD * BLOCK] = jnp.zeros((PAD * BLOCK, share), BF16)
    for m in range(tm):
        for j in range(local):
            at = row_at(table.block_of((me ^ m) * local + j))
            here = slice(j * BLOCK, (j + 1) * BLOCK)
            q4_ref[at] = q_refs[m][here, pl.ds(lead, share)]
            k4_ref[at] = kv_refs[m][here, pl.ds(lead, share)]
            v4_ref[at] = kv_refs[m][here, pl.ds(pl.multiple_of(hq + lead, share), share)]
    heads = share // head_size
    mask_b = diag_mask(heads, BLOCK, head_size).astype(BF16)
    for c in range(table.blocks):
        own = slice((c + PAD) * BLOCK, (c + PAD + 1) * BLOCK)
        win = slice((c + PAD - LC) * BLOCK, (c + PAD + 1) * BLOCK)
        diag_q = spread(q4_ref[own], mask_b)
        probs, unit = window_probs(diag_q, k4_ref[win], table.reach(c), head_size)
        p_ref[c] = probs
        d_ref[c] = (1.0 - unit * unit) * (1.0 / math.sqrt(head_size))


def backward_kernel(sizes, tm, part, head_size, *refs):
    meta_ref, q4_ref, v4_ref, p_ref, d_ref = refs[:5]
    n_refs = refs[5 : 5 + tm]
    g_refs = refs[5 + tm : 5 + 2 * tm][::-1]
    out_refs = refs[5 + 2 * tm : -3]
    gt_s, t_s, full_s = refs[-3:]
    table = Layout(meta_ref, *sizes)
    me = table.me()
    blocks = table.blocks
    local = blocks // tm
    share = q4_ref.shape[1]
    mask_b = diag_mask(share // head_size, BLOCK, head_size).astype(BF16)

    places = [(m, j, table.block_of((me ^ m) * local + j)) for m in range(tm) for j in range(local)]
    for m, j, b in places:
        gt_s[row_at(b)] = g_refs[m][j * ROWS + HALO : (j + 1) * ROWS].astype(F32)
    gt_s[(PAD - 1) * BLOCK : PAD * BLOCK] = jnp.zeros((BLOCK, share), F32)
    for m, j, b in places:
        at = row_at(b, HALO, -HALO)
        gt_s[at] = gt_s[at] + g_refs[m][j * ROWS : j * ROWS + HALO].astype(F32)
    t_s[...] = jnp.zeros(t_s.shape, F32)

    def spans(c):
        own = slice((c + PAD) * BLOCK, (c + PAD + 1) * BLOCK)
        win = slice((c + PAD - LC) * BLOCK, (c + PAD + 1) * BLOCK)
        return own, win, spread(gt_s[own].astype(BF16), mask_b)

    @pl.when(me >= tm // 2)
    def _():
        for c in range(blocks):
            own, win, diag_g = spans(c)
            t_s[win] = t_s[win] + dot_nn(p_ref[c].astype(BF16), diag_g)

    @pl.when(me < tm // 2)
    def _():
        for c in range(blocks):
            own, win, diag_g = spans(c)
            grad_probs = dot_nt(v4_ref[win], diag_g)
            probs = p_ref[c]
            delta = jnp.sum(probs * grad_probs, axis=0, keepdims=True)
            grad_raw = probs * (grad_probs - delta) * d_ref[c]
            t_s[win] = t_s[win] + dot_nn(grad_raw.astype(BF16), spread(q4_ref[own], mask_b))

    terms = jnp.concatenate([t_s[row_at(b)].astype(BF16) for _, _, b in places], axis=0)
    full = dot_tn(terms, jnp.concatenate([ref[...] for ref in n_refs], axis=0))
    if len(out_refs) == 1:
        out_refs[0][...] = full.astype(BF16)
        return
    full_s[...] = full
    chip, core = table.dp() // 2, table.dp() % 2
    for q in range(out_refs[0].shape[1] // part):
        for ref, side in zip(out_refs, (core, 1 - core)):
            at = pl.ds(pl.multiple_of(((chip ^ q) * 2 + side) * part, part), part)
            ref[:, q * part : (q + 1) * part] = full_s[:, at].astype(ref.dtype)


def pair_kernel(kept_ref, got_ref, *out_refs):
    part = out_refs[0].shape[1]
    for q, ref in enumerate(out_refs):
        cols = slice(q * part, (q + 1) * part)
        ref[...] = (kept_ref[:, cols] + got_ref[:, cols].astype(F32)).astype(ref.dtype)


def sum_kernel(*refs):
    total = refs[0][...].astype(F32)
    for ref in refs[1:-1]:
        total = total + ref[...].astype(F32)
    refs[-1][...] = total.T


def on_device(
    frames,
    out_grad,
    norm1_gain,
    w_query,
    w_kv,
    w_out,
    norm2_gain,
    conv_kernel,
    conv_bias,
    utt_blocks,
    block_slot,
    left_count,
):
    tm = lax.axis_size("tm")
    dp = lax.axis_size("dp")
    rows, width = frames.shape
    blocks = block_slot.shape[1]
    utts = utt_blocks.shape[1]
    sizes = (utts, blocks)
    local = rows // BLOCK
    hq = w_query.shape[1]
    head_size = hq // HEADS
    kv_width = w_kv.shape[1]
    share = kv_width // tm
    padded = (blocks + PAD) * BLOCK

    def swap(value, axis, size, m):
        return lax.ppermute(value, axis, [(i, i ^ m) for i in range(size)])

    meta = jnp.concatenate(
        [
            lax.axis_index("tm").astype(jnp.int32).reshape(1, 1),
            lax.axis_index("dp").astype(jnp.int32).reshape(1, 1),
            utt_blocks,
            block_slot,
            left_count,
        ],
        axis=1,
    )
    small = jnp.concatenate(
        [conv_kernel, conv_bias.reshape(1, -1), norm2_gain.reshape(1, -1)], axis=0
    )

    smem = pl.BlockSpec(memory_space=pltpu.SMEM)
    vmem = pl.BlockSpec(memory_space=pltpu.VMEM)
    shape = jax.ShapeDtypeStruct

    taps = pl.pallas_call(
        taps_kernel,
        out_shape=shape((KERNEL * SUB, width), F32),
        in_specs=[vmem],
        out_specs=vmem,
        compiler_params=pltpu.CompilerParams(vmem_limit_bytes=4 << 20),
        cost_estimate=pl.CostEstimate(flops=10**6, bytes_accessed=1 << 20, transcendentals=0),
        name="spread_taps",
    )(small)

    x, normed, queries, keys_values = {}, {}, {}, {}
    made = [shape((rows, w), BF16) for w in (width, hq, kv_width)]

    def project_shard(m, part):
        normed[m], queries[m], keys_values[m] = pl.pallas_call(
            project_kernel,
            out_shape=made,
            in_specs=[vmem] * 4,
            out_specs=[vmem] * 3,
            compiler_params=pltpu.CompilerParams(vmem_limit_bytes=4 << 20),
            cost_estimate=pl.CostEstimate(
                flops=2 * rows * width * (hq + kv_width), bytes_accessed=4 << 20, transcendentals=0
            ),
            name=f"project_rows_{m}",
        )(part, norm1_gain.reshape(1, -1), w_query, w_kv)

    project_shard(0, frames)
    x[0] = frames
    if tm == 4:
        x[2] = swap(frames, "tm", tm, 2)
        x[1] = swap(frames, "tm", tm, 1)
        facing, normed[0], taps, meta = lax.optimization_barrier((x[2], normed[0], taps, meta))
        x[3] = swap(facing, "tm", tm, 1)
        project_shard(2, facing)
        project_shard(1, x[1])
    else:
        for m in range(1, tm):
            x[m] = swap(frames, "tm", tm, m)
            if m < tm - 1:
                project_shard(m, x[m])

    def by_m(arrays):
        return [arrays[m] for m in sorted(arrays)]

    own_rows = local * ROWS
    results = pl.pallas_call(
        functools.partial(forward_kernel, sizes, tm, head_size),
        out_shape=[shape((rows, width), BF16)]
        + made
        + [shape((own_rows, share), BF16)] * tm,
        in_specs=[pl.BlockSpec(memory_space=pl.ANY)] + [vmem] * (5 + 3 * tm),
        out_specs=[vmem] * (tm + 4),
        scratch_shapes=[
            pltpu.VMEM((padded, hq), BF16),
            pltpu.VMEM((padded, kv_width), BF16),
            pltpu.VMEM(((blocks + 1) * HALO, width), BF16),
            pltpu.VMEM((own_rows, hq), BF16),
            pltpu.VMEM((own_rows, width), F32),
            pltpu.VMEM((rows, width), F32),
            pltpu.VMEM((own_rows, width), F32),
            pltpu.VMEM((own_rows, width), F32),
            pltpu.VMEM((own_rows, width), BF16),
            pltpu.SMEM(meta.shape, jnp.int32),
            pltpu.SemaphoreType.DMA,
        ],
        compiler_params=pltpu.CompilerParams(vmem_limit_bytes=16 << 20),
        name="forward_pass",
    )(
        meta,
        out_grad,
        w_out,
        small,
        taps,
        norm1_gain.reshape(1, -1),
        w_query,
        w_kv,
        *by_m(x),
        *by_m(queries),
        *by_m(keys_values),
    )
    layer_out, normed[tm - 1], queries[tm - 1], keys_values[tm - 1] = results[:4]
    sends = results[:3:-1]
    got = {0: sends[0]}
    for m in range(tm - 1, 0, -1):
        got[m] = swap(sends[m], "tm", tm, m)

    pair_width = share // head_size * BLOCK
    q4, v4, probs, slopes = pl.pallas_call(
        functools.partial(probs_kernel, sizes, tm, head_size),
        out_shape=[shape((padded, share), BF16)] * 2
        + [shape((blocks, SPAN, pair_width), F32)] * 2,
        in_specs=[smem] + [vmem] * (2 * tm),
        out_specs=[vmem] * 4,
        scratch_shapes=[pltpu.VMEM((padded, share), BF16)],
        compiler_params=pltpu.CompilerParams(vmem_limit_bytes=8 << 20),
        name="window_probs",
        cost_estimate=pl.CostEstimate(
            flops=2 * 10**9, bytes_accessed=4 * 10**6, transcendentals=800000
        ),
    )(meta, *by_m(queries), *by_m(keys_values))

    direct = dp <= 8
    half_width = width // 2
    if direct:
        piece_shapes = [shape((share, half_width), F32), shape((share, half_width), BF16)]
    else:
        piece_shapes = [shape((share, width), BF16)]
    pieces = pl.pallas_call(
        functools.partial(backward_kernel, sizes, tm, width // dp, head_size),
        out_shape=piece_shapes,
        in_specs=[smem] + [vmem] * (4 + 2 * tm),
        out_specs=[vmem] * len(piece_shapes),
        scratch_shapes=[
            pltpu.VMEM((padded, share), F32),
            pltpu.VMEM((padded, share), F32),
            pltpu.VMEM((share, width), F32),
        ],
        compiler_params=pltpu.CompilerParams(vmem_limit_bytes=12 << 20),
        name="key_value_terms",
    )(meta, q4, v4, probs, slopes, *by_m(normed), *by_m(got)[::-1])

    if direct:
        kept, away = pieces
        arrived = swap(away, "dp", dp, 1)
        chips = dp // 2
        part = width // dp
        summed = pl.pallas_call(
            pair_kernel,
            out_shape=[shape((share, part), BF16)] * chips,
            in_specs=[vmem] * 2,
            out_specs=[vmem] * chips,
            compiler_params=pltpu.CompilerParams(vmem_limit_bytes=4 << 20),
            name="sum_pair",
        )(kept, arrived)
        terms = [swap(summed[q], "dp", dp, 2 * q) for q in range(chips - 1, 0, -1)]
        terms.append(summed[0])
    else:
        terms = [lax.psum_scatter(pieces[0], "dp", scatter_dimension=1, tiled=True)]
    kv_grad = pl.pallas_call(
        sum_kernel,
        out_shape=shape((width // dp, share), F32),
        in_specs=[vmem] * len(terms),
        out_specs=vmem,
        compiler_params=pltpu.CompilerParams(vmem_limit_bytes=4 << 20),
        name="sum_groups",
    )(*terms)
    return layer_out, kv_grad


def solution(mesh):
    return jax.shard_map(
        on_device,
        mesh=mesh,
        in_specs=(
            P(("dp", "tm"), None),
            P(("dp", "tm"), None),
            P(),
            P(),
            P(),
            P(),
            P(),
            P(),
            P(),
            P("dp", None),
            P("dp", None),
            P("dp", None),
        ),
        out_specs=(P(("dp", "tm"), None), P("dp", "tm")),
        check_vma=False,
    )
```

```python
import functools
import math

import jax
import jax.numpy as jnp
from jax import lax
from jax.experimental import pallas as pl
from jax.experimental.pallas import tpu as pltpu
from jax.sharding import PartitionSpec as P

HEADS = 8
KERNEL = 31
BLOCK = 64
LC = 2
SPAN = (LC + 1) * BLOCK
HALO = 32
ROWS = HALO + BLOCK
PAD = LC + 1
EPSILON = 1e-05
SOFT_CAP = 4.0
LANES = 128
SUB = 8

BF16 = jnp.bfloat16
F32 = jnp.float32


def dot_nn(a, b):
    return lax.dot_general(a, b, (((1,), (0,)), ((), ())), preferred_element_type=F32)


def dot_nt(a, b):
    return lax.dot_general(a, b, (((1,), (1,)), ((), ())), preferred_element_type=F32)


def dot_tn(a, b):
    return lax.dot_general(a, b, (((0,), (0,)), ((), ())), preferred_element_type=F32)


def norm_stats(values):
    row_mean = jnp.mean(values, axis=-1, keepdims=True)
    centred = values - row_mean
    scale_inv = lax.rsqrt(jnp.mean(centred * centred, axis=-1, keepdims=True) + EPSILON)
    return centred * scale_inv, scale_inv


class Layout:
    def __init__(self, meta_ref, utts, blocks):
        self.ref, self.utts, self.blocks = meta_ref, utts, blocks

    def me(self):
        return self.ref[0, 0]

    def dp(self):
        return self.ref[0, 1]

    def block_of(self, slot):
        found = jnp.int32(0)
        for b in range(self.blocks):
            found = jnp.where(self.ref[0, 2 + self.utts + b] == slot, jnp.int32(b), found)
        return found

    def position(self, block):
        start = jnp.int32(0)
        first = jnp.int32(0)
        for u in range(self.utts):
            first = jnp.where(block >= start, start, first)
            start = start + self.ref[0, 2 + u]
        return block - first

    def reach(self, block):
        safe = jnp.maximum(block, 0)
        left = self.ref[0, 2 + self.utts + self.blocks + safe]
        return jnp.minimum(left, self.position(safe))


def row_at(block, count=BLOCK, shift=0):
    return pl.ds(pl.multiple_of((block + PAD) * BLOCK + shift, math.gcd(BLOCK, shift)), count)


def diag_mask(heads, rows, head_size):
    shape = (heads * rows, heads * head_size)
    row_head = lax.broadcasted_iota(jnp.int32, shape, 0) // rows
    col_head = lax.broadcasted_iota(jnp.int32, shape, 1) // head_size
    return jnp.where(row_head == col_head, 1.0, 0.0).astype(F32)


def spread(rows, mask_b):
    copies = mask_b.shape[0] // rows.shape[0]
    return jnp.concatenate([rows] * copies, axis=0) * mask_b


def fold_heads(full, mask_f, rows):
    kept = full * mask_f
    total = kept[:rows]
    for h in range(1, full.shape[0] // rows):
        total = total + kept[h * rows : (h + 1) * rows]
    return total


def window_probs(diag_q, k_win, reach, head_size):
    raw = dot_nt(k_win, diag_q)
    unit = jnp.tanh(raw * (1.0 / (SOFT_CAP * math.sqrt(head_size))))
    exped = jnp.exp(SOFT_CAP * unit)
    parts = []
    for w in range(LC):
        ok = jnp.where(reach >= LC - w, 1.0, 0.0).astype(F32)
        parts.append(exped[w * BLOCK : (w + 1) * BLOCK] * ok)
    parts.append(exped[LC * BLOCK :])
    exped = jnp.concatenate(parts, axis=0)
    total = jnp.sum(exped, axis=0, keepdims=True)
    return exped * (1.0 / total), unit


def taps_kernel(small_ref, wo_ref, taps_ref, wot_ref):
    wot_ref[...] = wo_ref[...].T
    for j in range(KERNEL):
        rows = jnp.broadcast_to(small_ref[j : j + 1], (SUB, small_ref.shape[1]))
        taps_ref[j * SUB : (j + 1) * SUB] = rows


def project_kernel(x_ref, g1_ref, wq_ref, wkv_ref, n_ref, q_ref, kv_ref):
    project(x_ref, g1_ref, wq_ref, wkv_ref, n_ref, q_ref, kv_ref)


def project(x_ref, g1_ref, wq_ref, wkv_ref, n_ref, q_ref, kv_ref):
    unit, _ = norm_stats(x_ref[...].astype(F32))
    normed = (unit * g1_ref[...]).astype(BF16)
    n_ref[...] = normed
    q_ref[...] = dot_nn(normed, wq_ref[...]).astype(BF16)
    kv_ref[...] = dot_nn(normed, wkv_ref[...]).astype(BF16)


def forward_kernel(sizes, tm, head_size, *refs):
    tables_ref, grad_ref, wo_ref, wot_ref, small_ref, taps_ref = refs[:6]
    g1_ref, wq_ref, wkv_ref = refs[6:9]
    refs = refs[9:]
    x_refs = refs[:tm]
    q_refs, kv_refs = (refs[tm + k * (tm - 1) : tm + (k + 1) * (tm - 1)] for k in range(2))
    refs = refs[3 * tm - 2 :]
    half = tm // 2
    out_ref, n_last, q_last, kv_last = refs[:4]
    send_refs = refs[4 : 4 + tm][::-1]
    q_ref, kv_ref, tail_s, ctx_s, e_s, h_s, u_s, gr_s, gc_s, meta_ref, sem = refs[4 + tm :]
    fetch = pltpu.make_async_copy(tables_ref, meta_ref, sem)
    fetch.start()
    project(x_refs[-1], g1_ref, wq_ref, wkv_ref, n_last, q_last, kv_last)
    q_refs, kv_refs = (*q_refs, q_last), (*kv_refs, kv_last)
    fetch.wait()

    table = Layout(meta_ref, *sizes)
    me = table.me()
    local = table.blocks // tm
    width = out_ref.shape[1]
    hq = q_ref.shape[1]
    share = send_refs[0].shape[1]

    for ref in (q_ref, kv_ref):
        ref[: PAD * BLOCK] = jnp.zeros((PAD * BLOCK, ref.shape[1]), BF16)
    tail_s[:HALO] = jnp.zeros((HALO, width), BF16)
    for m in range(tm):
        for j in range(local):
            b = table.block_of((me ^ m) * local + j)
            here = slice(j * BLOCK, (j + 1) * BLOCK)
            q_ref[row_at(b)] = q_refs[m][here]
            kv_ref[row_at(b)] = kv_refs[m][here]
            after = pl.ds(pl.multiple_of((b + 1) * HALO, HALO), HALO)
            tail_s[after] = x_refs[m][(j + 1) * BLOCK - HALO : (j + 1) * BLOCK]

    mid_heads = 256 // BLOCK
    mid_f = diag_mask(mid_heads, BLOCK, head_size)
    mid_b = mid_f.astype(BF16)
    side_f = diag_mask(HEADS, HALO, head_size)
    side_b = side_f.astype(BF16)

    ones = jnp.ones((SPAN, LANES), BF16)
    key_block = lax.broadcasted_iota(jnp.int32, (1, SPAN), 1) // BLOCK
    own = [table.block_of(me * local + i) for i in range(local)]
    keep = [jnp.where(table.position(c) >= 1, 1.0, 0.0).astype(F32) for c in own]
    for i, c in enumerate(own):
        for blk, shift, count, put in ((c - 1, HALO, HALO, 0), (c, 0, BLOCK, HALO)):
            reach = table.reach(blk)
            allowed = jnp.ones((1, SPAN), F32)
            for w in range(LC):
                ok = jnp.where(reach >= LC - w, 1.0, 0.0).astype(F32)
                allowed = jnp.where(key_block == w, ok, allowed)
            win = row_at(blk - LC, SPAN)
            at = row_at(blk, count, shift)
            if count == BLOCK:
                groups, mask_f, mask_b = HEADS // mid_heads, mid_f, mid_b
            else:
                groups, mask_f, mask_b = 1, side_f, side_b
            wide = hq // groups
            for g in range(groups):
                cols = slice(g * wide, (g + 1) * wide)
                vcols = slice(hq + g * wide, hq + (g + 1) * wide)
                raw = dot_nt(spread(q_ref[at, cols], mask_b), kv_ref[win, cols])
                unit = jnp.tanh(raw * (1.0 / (SOFT_CAP * math.sqrt(head_size))))
                exped = (jnp.exp(SOFT_CAP * unit) * allowed).astype(BF16)
                inverse = 1.0 / dot_nn(exped, ones)
                scale = mask_f * jnp.concatenate([inverse] * (wide // LANES), axis=1)
                full = dot_nn(exped, kv_ref[win, vcols])
                ctx_s[i * ROWS + put : i * ROWS + put + count, cols] = fold_heads(
                    full, scale, count
                ).astype(BF16)

    gain = small_ref[KERNEL + 1 : KERNEL + 2]
    product = dot_nn(ctx_s[...], wo_ref[...])
    scales = []
    for i, c in enumerate(own):
        here = slice(i * ROWS, (i + 1) * ROWS)
        tail = tail_s[pl.ds(pl.multiple_of(c * HALO, HALO), HALO)]
        rows = jnp.concatenate([tail, x_refs[0][i * BLOCK : (i + 1) * BLOCK]], axis=0)
        hidden = rows.astype(F32) + product[here]
        unit, inv = norm_stats(hidden)
        conv_in = (unit * gain).astype(BF16).astype(F32)
        e_s[i * ROWS : i * ROWS + HALO] = conv_in[:HALO] * keep[i]
        e_s[i * ROWS + HALO : (i + 1) * ROWS] = conv_in[HALO:]
        h_s[i * BLOCK : (i + 1) * BLOCK] = hidden[HALO:]
        u_s[here] = unit
        scales.append(inv)

    groups = BLOCK // SUB

    def conv(cols):
        bias = jnp.broadcast_to(small_ref[KERNEL : KERNEL + 1, cols], (SUB, LANES))
        taps = lambda j: taps_ref[j * SUB : (j + 1) * SUB, cols]
        for i in range(local):
            ext = e_s[i * ROWS : (i + 1) * ROWS, cols]
            acc = [bias] * groups
            for s in range(SUB):
                reps = (KERNEL - s + SUB - 1) // SUB
                moved = ext[s + 2 : s + 2 + BLOCK + SUB * (reps - 1)]
                for a in range(reps):
                    tap = taps(SUB * a + s)
                    for r in range(groups):
                        piece = moved[(a + r) * SUB : (a + r + 1) * SUB]
                        acc[r] = acc[r] + tap * piece
            mixed = jnp.concatenate(acc, axis=0)
            gate = 0.5 * jnp.tanh(0.5 * mixed) + 0.5
            rows = slice(i * BLOCK, (i + 1) * BLOCK)
            out_ref[rows, cols] = (h_s[rows, cols] + mixed * gate).astype(BF16)
            slope = gate * (1.0 + mixed * (1.0 - gate))
            gm = grad_ref[rows, cols].astype(F32) * slope
            zeros = jnp.zeros((HALO, LANES), F32)
            padded = jnp.concatenate([zeros, gm, zeros], axis=0)
            back = [None] * (ROWS // SUB)
            low = HALO // SUB - 1
            for s in range(SUB):
                reps = (KERNEL - s + SUB - 1) // SUB
                start = low if s else low + 1
                moved = padded[start * SUB + s : ROWS + s]
                for a in range(reps):
                    tap = taps(KERNEL - 1 - SUB * a - s)
                    for g in range(start, ROWS // SUB):
                        r = g - a
                        piece = tap * moved[(g - start) * SUB : (g - start + 1) * SUB]
                        back[r] = piece if back[r] is None else back[r] + piece
            for r in range(ROWS // SUB):
                scale = keep[i] if r < HALO // SUB else 1.0
                gr_s[i * ROWS + r * SUB : i * ROWS + (r + 1) * SUB, cols] = back[r] * scale

    for k in range(0, width, LANES):
        conv(slice(k, k + LANES))

    for i in range(local):
        here = slice(i * ROWS, (i + 1) * ROWS)
        scaled = gr_s[here] * gain
        unit = u_s[here]
        first = jnp.mean(scaled, axis=-1, keepdims=True)
        second = jnp.mean(scaled * unit, axis=-1, keepdims=True)
        back = scales[i] * (scaled - first - unit * second)
        own_grad = grad_ref[i * BLOCK : (i + 1) * BLOCK].astype(F32) + back[HALO:]
        gc_s[i * ROWS : i * ROWS + HALO] = back[:HALO].astype(BF16)
        gc_s[i * ROWS + HALO : (i + 1) * ROWS] = own_grad.astype(BF16)
    for m in range(half):
        at = pl.ds(pl.multiple_of(((me ^ m) % half) * share, share), share)
        grad_context = dot_nn(gc_s[...], wot_ref[:, at]).astype(BF16)
        send_refs[m][...] = grad_context
        send_refs[m + half][...] = grad_context


def probs_kernel(sizes, tm, head_size, meta_ref, *refs):
    q_refs, kv_refs, n_refs = refs[:tm], refs[tm : 2 * tm], refs[2 * tm : 3 * tm]
    q4_ref, v4_ref, p_ref, d_ref, nt_ref, k4_ref = refs[3 * tm :]
    for m in range(tm):
        rows = n_refs[m].shape[0]
        nt_ref[:, m * rows : (m + 1) * rows] = n_refs[m][...].T
    table = Layout(meta_ref, *sizes)
    me = table.me()
    local = table.blocks // tm
    hq = q_refs[0].shape[1]
    share = q4_ref.shape[1]
    lead = pl.multiple_of((me % (tm // 2)) * share, share)
    for ref in (k4_ref, v4_ref):
        ref[: PAD * BLOCK] = jnp.zeros((PAD * BLOCK, share), BF16)
    for m in range(tm):
        for j in range(local):
            at = row_at(table.block_of((me ^ m) * local + j))
            here = slice(j * BLOCK, (j + 1) * BLOCK)
            q4_ref[at] = q_refs[m][here, pl.ds(lead, share)]
            k4_ref[at] = kv_refs[m][here, pl.ds(lead, share)]
            v4_ref[at] = kv_refs[m][here, pl.ds(pl.multiple_of(hq + lead, share), share)]
    heads = share // head_size
    mask_b = diag_mask(heads, BLOCK, head_size).astype(BF16)
    for c in range(table.blocks):
        own = slice((c + PAD) * BLOCK, (c + PAD + 1) * BLOCK)
        win = slice((c + PAD - LC) * BLOCK, (c + PAD + 1) * BLOCK)
        diag_q = spread(q4_ref[own], mask_b)
        probs, unit = window_probs(diag_q, k4_ref[win], table.reach(c), head_size)
        p_ref[c] = probs
        d_ref[c] = (1.0 - unit * unit) * (1.0 / math.sqrt(head_size))


def backward_kernel(sizes, tm, part, head_size, *refs):
    tables_ref, q4_ref, v4_ref, p_ref, d_ref, nt_ref = refs[:6]
    g_refs = refs[6 : 6 + tm][::-1]
    out_refs = refs[6 + tm : -5]
    gt_s, t_s, full_s, meta_ref, sem = refs[-5:]
    fetch = pltpu.make_async_copy(tables_ref, meta_ref, sem)
    fetch.start()
    t_s[...] = jnp.zeros(t_s.shape, F32)
    fetch.wait()
    table = Layout(meta_ref, *sizes)
    me = table.me()
    blocks = table.blocks
    local = blocks // tm
    share = q4_ref.shape[1]
    mask_b = diag_mask(share // head_size, BLOCK, head_size).astype(BF16)

    places = [(m, j, table.block_of((me ^ m) * local + j)) for m in range(tm) for j in range(local)]
    for m, j, b in places:
        gt_s[row_at(b)] = g_refs[m][j * ROWS + HALO : (j + 1) * ROWS].astype(F32)
    gt_s[(PAD - 1) * BLOCK : PAD * BLOCK] = jnp.zeros((BLOCK, share), F32)
    for m, j, b in places:
        at = row_at(b, HALO, -HALO)
        gt_s[at] = gt_s[at] + g_refs[m][j * ROWS : j * ROWS + HALO].astype(F32)

    def spans(c):
        own = slice((c + PAD) * BLOCK, (c + PAD + 1) * BLOCK)
        win = slice((c + PAD - LC) * BLOCK, (c + PAD + 1) * BLOCK)
        return own, win, spread(gt_s[own].astype(BF16), mask_b)

    @pl.when(me >= tm // 2)
    def _():
        for c in range(blocks):
            own, win, diag_g = spans(c)
            t_s[win] = t_s[win] + dot_nn(p_ref[c].astype(BF16), diag_g)

    @pl.when(me < tm // 2)
    def _():
        for c in range(blocks):
            own, win, diag_g = spans(c)
            grad_probs = dot_nt(v4_ref[win], diag_g)
            probs = p_ref[c]
            delta = jnp.sum(probs * grad_probs, axis=0, keepdims=True)
            grad_raw = probs * (grad_probs - delta) * d_ref[c]
            t_s[win] = t_s[win] + dot_nn(grad_raw.astype(BF16), spread(q4_ref[own], mask_b))

    terms = jnp.concatenate([t_s[row_at(b)].astype(BF16) for _, _, b in places], axis=0)
    full = dot_nn(nt_ref[...], terms)
    if len(out_refs) == 1:
        out_refs[0][...] = full.astype(BF16)
        return
    full_s[...] = full
    chip, core = table.dp() // 2, table.dp() % 2
    for q in range(out_refs[0].shape[0] // part):
        for ref, side in zip(out_refs, (core, 1 - core)):
            at = pl.ds(pl.multiple_of(((chip ^ q) * 2 + side) * part, part), part)
            ref[q * part : (q + 1) * part] = full_s[at].astype(ref.dtype)


def pair_kernel(kept_ref, got_ref, *out_refs):
    part = out_refs[0].shape[0]
    for q, ref in enumerate(out_refs):
        rows = slice(q * part, (q + 1) * part)
        ref[...] = (kept_ref[rows] + got_ref[rows].astype(F32)).astype(ref.dtype)


def sum_kernel(*refs):
    total = refs[0][...].astype(F32)
    for ref in refs[1:-1]:
        total = total + ref[...].astype(F32)
    refs[-1][...] = total


def on_device(
    frames,
    out_grad,
    norm1_gain,
    w_query,
    w_kv,
    w_out,
    norm2_gain,
    conv_kernel,
    conv_bias,
    utt_blocks,
    block_slot,
    left_count,
):
    tm = lax.axis_size("tm")
    dp = lax.axis_size("dp")
    rows, width = frames.shape
    blocks = block_slot.shape[1]
    utts = utt_blocks.shape[1]
    sizes = (utts, blocks)
    local = rows // BLOCK
    hq = w_query.shape[1]
    head_size = hq // HEADS
    kv_width = w_kv.shape[1]
    share = kv_width // tm
    padded = (blocks + PAD) * BLOCK

    def swap(value, axis, size, m):
        return lax.ppermute(value, axis, [(i, i ^ m) for i in range(size)])

    meta = jnp.concatenate(
        [
            lax.axis_index("tm").astype(jnp.int32).reshape(1, 1),
            lax.axis_index("dp").astype(jnp.int32).reshape(1, 1),
            utt_blocks,
            block_slot,
            left_count,
        ],
        axis=1,
    )
    small = jnp.concatenate(
        [conv_kernel, conv_bias.reshape(1, -1), norm2_gain.reshape(1, -1)], axis=0
    )

    smem = pl.BlockSpec(memory_space=pltpu.SMEM)
    vmem = pl.BlockSpec(memory_space=pltpu.VMEM)
    shape = jax.ShapeDtypeStruct

    taps, w_out_t = pl.pallas_call(
        taps_kernel,
        out_shape=[shape((KERNEL * SUB, width), F32), shape((width, hq), BF16)],
        in_specs=[vmem] * 2,
        out_specs=[vmem] * 2,
        compiler_params=pltpu.CompilerParams(vmem_limit_bytes=4 << 20),
        cost_estimate=pl.CostEstimate(flops=10**6, bytes_accessed=1 << 20, transcendentals=0),
        name="spread_taps",
    )(small, w_out)

    x, normed, queries, keys_values = {}, {}, {}, {}
    made = [shape((rows, w), BF16) for w in (width, hq, kv_width)]

    def project_shard(m, part):
        normed[m], queries[m], keys_values[m] = pl.pallas_call(
            project_kernel,
            out_shape=made,
            in_specs=[vmem] * 4,
            out_specs=[vmem] * 3,
            compiler_params=pltpu.CompilerParams(vmem_limit_bytes=4 << 20),
            cost_estimate=pl.CostEstimate(
                flops=2 * rows * width * (hq + kv_width), bytes_accessed=4 << 20, transcendentals=0
            ),
            name=f"project_rows_{m}",
        )(part, norm1_gain.reshape(1, -1), w_query, w_kv)

    project_shard(0, frames)
    x[0] = frames
    if tm == 4:
        x[2] = swap(frames, "tm", tm, 2)
        x[1] = swap(frames, "tm", tm, 1)
        facing, normed[0], taps, meta = lax.optimization_barrier((x[2], normed[0], taps, meta))
        x[3] = swap(facing, "tm", tm, 1)
        project_shard(2, facing)
        project_shard(1, x[1])
    else:
        for m in range(1, tm):
            x[m] = swap(frames, "tm", tm, m)
            if m < tm - 1:
                project_shard(m, x[m])

    def by_m(arrays):
        return [arrays[m] for m in sorted(arrays)]

    own_rows = local * ROWS
    results = pl.pallas_call(
        functools.partial(forward_kernel, sizes, tm, head_size),
        out_shape=[shape((rows, width), BF16)]
        + made
        + [shape((own_rows, share), BF16)] * tm,
        in_specs=[pl.BlockSpec(memory_space=pl.ANY)] + [vmem] * (6 + 3 * tm),
        out_specs=[vmem] * (tm + 4),
        scratch_shapes=[
            pltpu.VMEM((padded, hq), BF16),
            pltpu.VMEM((padded, kv_width), BF16),
            pltpu.VMEM(((blocks + 1) * HALO, width), BF16),
            pltpu.VMEM((own_rows, hq), BF16),
            pltpu.VMEM((own_rows, width), F32),
            pltpu.VMEM((rows, width), F32),
            pltpu.VMEM((own_rows, width), F32),
            pltpu.VMEM((own_rows, width), F32),
            pltpu.VMEM((own_rows, width), BF16),
            pltpu.SMEM(meta.shape, jnp.int32),
            pltpu.SemaphoreType.DMA,
        ],
        compiler_params=pltpu.CompilerParams(vmem_limit_bytes=16 << 20),
        name="forward_pass",
    )(
        meta,
        out_grad,
        w_out,
        w_out_t,
        small,
        taps,
        norm1_gain.reshape(1, -1),
        w_query,
        w_kv,
        *by_m(x),
        *by_m(queries),
        *by_m(keys_values),
    )
    layer_out, normed[tm - 1], queries[tm - 1], keys_values[tm - 1] = results[:4]
    sends = results[:3:-1]
    got = {0: sends[0]}
    for m in range(tm - 1, 0, -1):
        got[m] = swap(sends[m], "tm", tm, m)

    pair_width = share // head_size * BLOCK
    q4, v4, probs, slopes, normed_t = pl.pallas_call(
        functools.partial(probs_kernel, sizes, tm, head_size),
        out_shape=[shape((padded, share), BF16)] * 2
        + [shape((blocks, SPAN, pair_width), F32)] * 2
        + [shape((width, blocks * BLOCK), BF16)],
        in_specs=[smem] + [vmem] * (3 * tm),
        out_specs=[vmem] * 5,
        scratch_shapes=[pltpu.VMEM((padded, share), BF16)],
        compiler_params=pltpu.CompilerParams(vmem_limit_bytes=8 << 20),
        name="window_probs",
        cost_estimate=pl.CostEstimate(
            flops=2 * 10**9, bytes_accessed=4 * 10**6, transcendentals=800000
        ),
    )(meta, *by_m(queries), *by_m(keys_values), *by_m(normed))

    direct = dp <= 8
    half_width = width // 2
    if direct:
        piece_shapes = [shape((half_width, share), F32), shape((half_width, share), BF16)]
    else:
        piece_shapes = [shape((width, share), BF16)]
    pieces = pl.pallas_call(
        functools.partial(backward_kernel, sizes, tm, width // dp, head_size),
        out_shape=piece_shapes,
        in_specs=[pl.BlockSpec(memory_space=pl.ANY)] + [vmem] * (5 + tm),
        out_specs=[vmem] * len(piece_shapes),
        scratch_shapes=[
            pltpu.VMEM((padded, share), F32),
            pltpu.VMEM((padded, share), F32),
            pltpu.VMEM((width, share), F32),
            pltpu.SMEM(meta.shape, jnp.int32),
            pltpu.SemaphoreType.DMA,
        ],
        compiler_params=pltpu.CompilerParams(vmem_limit_bytes=12 << 20),
        name="key_value_terms",
    )(meta, q4, v4, probs, slopes, normed_t, *by_m(got)[::-1])

    if direct:
        kept, away = pieces
        arrived = swap(away, "dp", dp, 1)
        chips = dp // 2
        part = width // dp
        summed = pl.pallas_call(
            pair_kernel,
            out_shape=[shape((part, share), BF16)] * chips,
            in_specs=[vmem] * 2,
            out_specs=[vmem] * chips,
            compiler_params=pltpu.CompilerParams(vmem_limit_bytes=4 << 20),
            name="sum_pair",
        )(kept, arrived)
        terms = [swap(summed[q], "dp", dp, 2 * q) for q in range(chips - 1, 0, -1)]
        terms.append(summed[0])
    else:
        terms = [lax.psum_scatter(pieces[0], "dp", scatter_dimension=0, tiled=True)]
    kv_grad = pl.pallas_call(
        sum_kernel,
        out_shape=shape((width // dp, share), F32),
        in_specs=[vmem] * len(terms),
        out_specs=vmem,
        compiler_params=pltpu.CompilerParams(vmem_limit_bytes=4 << 20),
        name="sum_groups",
    )(*terms)
    return layer_out, kv_grad


def solution(mesh):
    return jax.shard_map(
        on_device,
        mesh=mesh,
        in_specs=(
            P(("dp", "tm"), None),
            P(("dp", "tm"), None),
            P(),
            P(),
            P(),
            P(),
            P(),
            P(),
            P(),
            P("dp", None),
            P("dp", None),
            P("dp", None),
        ),
        out_specs=(P(("dp", "tm"), None), P("dp", "tm")),
        check_vma=False,
    )
```

```python
import functools
import math

import jax
import jax.numpy as jnp
from jax import lax
from jax.experimental import pallas as pl
from jax.experimental.pallas import tpu as pltpu
from jax.sharding import PartitionSpec as P

HEADS = 8
KERNEL = 31
BLOCK = 64
LC = 2
SPAN = (LC + 1) * BLOCK
HALO = 32
ROWS = HALO + BLOCK
KERNEL_GAP = HALO - (KERNEL - 1)
PAD = LC + 1
EPSILON = 1e-05
SOFT_CAP = 4.0
LANES = 128
SUB = 8

BF16 = jnp.bfloat16
F32 = jnp.float32


def dot_nn(a, b):
    return lax.dot_general(a, b, (((1,), (0,)), ((), ())), preferred_element_type=F32)


def dot_nt(a, b):
    return lax.dot_general(a, b, (((1,), (1,)), ((), ())), preferred_element_type=F32)


def dot_tn(a, b):
    return lax.dot_general(a, b, (((0,), (0,)), ((), ())), preferred_element_type=F32)


def norm_stats(values):
    row_mean = jnp.mean(values, axis=-1, keepdims=True)
    centred = values - row_mean
    scale_inv = lax.rsqrt(jnp.mean(centred * centred, axis=-1, keepdims=True) + EPSILON)
    return centred * scale_inv, scale_inv


class Layout:
    def __init__(self, meta_ref, utts, blocks):
        self.ref, self.utts, self.blocks = meta_ref, utts, blocks

    def me(self):
        return self.ref[0, 0]

    def dp(self):
        return self.ref[0, 1]

    def block_of(self, slot):
        found = jnp.int32(0)
        for b in range(self.blocks):
            found = jnp.where(self.ref[0, 2 + self.utts + b] == slot, jnp.int32(b), found)
        return found

    def position(self, block):
        start = jnp.int32(0)
        first = jnp.int32(0)
        for u in range(self.utts):
            first = jnp.where(block >= start, start, first)
            start = start + self.ref[0, 2 + u]
        return block - first

    def reach(self, block):
        safe = jnp.maximum(block, 0)
        left = self.ref[0, 2 + self.utts + self.blocks + safe]
        return jnp.minimum(left, self.position(safe))


def row_at(block, count=BLOCK, shift=0):
    return pl.ds(pl.multiple_of((block + PAD) * BLOCK + shift, math.gcd(BLOCK, shift)), count)


def diag_mask(heads, rows, head_size):
    shape = (heads * rows, heads * head_size)
    row_head = lax.broadcasted_iota(jnp.int32, shape, 0) // rows
    col_head = lax.broadcasted_iota(jnp.int32, shape, 1) // head_size
    return jnp.where(row_head == col_head, 1.0, 0.0).astype(F32)


def spread(rows, mask_b):
    copies = mask_b.shape[0] // rows.shape[0]
    return jnp.concatenate([rows] * copies, axis=0) * mask_b


def fold_heads(full, mask_f, rows):
    kept = full * mask_f
    total = kept[:rows]
    for h in range(1, full.shape[0] // rows):
        total = total + kept[h * rows : (h + 1) * rows]
    return total


def window_probs(diag_q, k_win, reach, head_size):
    raw = dot_nt(k_win, diag_q)
    unit = jnp.tanh(raw * (1.0 / (SOFT_CAP * math.sqrt(head_size))))
    exped = jnp.exp(SOFT_CAP * unit)
    parts = []
    for w in range(LC):
        ok = jnp.where(reach >= LC - w, 1.0, 0.0).astype(F32)
        parts.append(exped[w * BLOCK : (w + 1) * BLOCK] * ok)
    parts.append(exped[LC * BLOCK :])
    exped = jnp.concatenate(parts, axis=0)
    total = jnp.sum(exped, axis=0, keepdims=True)
    return exped * (1.0 / total), unit


def taps_kernel(small_ref, wo_ref, taps_ref, wot_ref):
    wot_ref[...] = wo_ref[...].T
    for j in range(KERNEL):
        rows = jnp.broadcast_to(small_ref[j : j + 1], (SUB, small_ref.shape[1]))
        taps_ref[j * SUB : (j + 1) * SUB] = rows


def project_kernel(x_ref, g1_ref, wq_ref, wkv_ref, n_ref, q_ref, kv_ref):
    project(x_ref, g1_ref, wq_ref, wkv_ref, n_ref, q_ref, kv_ref)


def project(x_ref, g1_ref, wq_ref, wkv_ref, n_ref, q_ref, kv_ref):
    unit, _ = norm_stats(x_ref[...].astype(F32))
    normed = (unit * g1_ref[...]).astype(BF16)
    n_ref[...] = normed
    q_ref[...] = dot_nn(normed, wq_ref[...]).astype(BF16)
    kv_ref[...] = dot_nn(normed, wkv_ref[...]).astype(BF16)


def shifted_up(values, shift):
    return pltpu.roll(values, values.shape[0] - shift, axis=0) if shift else values


def forward_kernel(sizes, tm, head_size, *refs):
    tables_ref, grad_ref, wo_ref, wot_ref, small_ref, taps_ref = refs[:6]
    g1_ref, wq_ref, wkv_ref = refs[6:9]
    refs = refs[9:]
    x_refs = refs[:tm]
    q_refs, kv_refs = (refs[tm + k * (tm - 1) : tm + (k + 1) * (tm - 1)] for k in range(2))
    refs = refs[3 * tm - 2 :]
    half = tm // 2
    out_ref, n_last, q_last, kv_last = refs[:4]
    send_refs = refs[4 : 4 + tm][::-1]
    q_ref, kv_ref, tail_s, ctx_s, e_s, h_s, u_s, gr_s, gc_s, meta_ref, sem = refs[4 + tm :]
    fetch = pltpu.make_async_copy(tables_ref, meta_ref, sem)
    fetch.start()
    project(x_refs[-1], g1_ref, wq_ref, wkv_ref, n_last, q_last, kv_last)
    q_refs, kv_refs = (*q_refs, q_last), (*kv_refs, kv_last)
    fetch.wait()

    table = Layout(meta_ref, *sizes)
    me = table.me()
    local = table.blocks // tm
    width = out_ref.shape[1]
    hq = q_ref.shape[1]
    share = send_refs[0].shape[1]

    for ref in (q_ref, kv_ref):
        ref[: PAD * BLOCK] = jnp.zeros((PAD * BLOCK, ref.shape[1]), BF16)
    tail_s[:HALO] = jnp.zeros((HALO, width), BF16)
    for m in range(tm):
        for j in range(local):
            b = table.block_of((me ^ m) * local + j)
            here = slice(j * BLOCK, (j + 1) * BLOCK)
            q_ref[row_at(b)] = q_refs[m][here]
            kv_ref[row_at(b)] = kv_refs[m][here]
            after = pl.ds(pl.multiple_of((b + 1) * HALO, HALO), HALO)
            tail_s[after] = x_refs[m][(j + 1) * BLOCK - HALO : (j + 1) * BLOCK]

    mid_heads = 256 // BLOCK
    mid_f = diag_mask(mid_heads, BLOCK, head_size)
    mid_b = mid_f.astype(BF16)
    side_f = diag_mask(HEADS, HALO, head_size)
    side_b = side_f.astype(BF16)

    own = [table.block_of(me * local + i) for i in range(local)]
    keep = [jnp.where(table.position(c) >= 1, 1.0, 0.0).astype(F32) for c in own]
    for i, c in enumerate(own):
        for blk, shift, count, put in ((c - 1, HALO, HALO, 0), (c, 0, BLOCK, HALO)):
            reach = table.reach(blk)
            win = row_at(blk - LC, SPAN)
            at = row_at(blk, count, shift)
            if count == BLOCK:
                groups, mask_f, mask_b = HEADS // mid_heads, mid_f, mid_b
            else:
                groups, mask_f, mask_b = 1, side_f, side_b
            wide = hq // groups
            for g in range(groups):
                cols = slice(g * wide, (g + 1) * wide)
                vcols = slice(hq + g * wide, hq + (g + 1) * wide)
                probs, _ = window_probs(
                    spread(q_ref[at, cols], mask_b), kv_ref[win, cols], reach, head_size
                )
                full = dot_tn(probs.astype(BF16), kv_ref[win, vcols])
                ctx_s[i * ROWS + put : i * ROWS + put + count, cols] = fold_heads(
                    full, mask_f, count
                ).astype(BF16)

    gain = small_ref[KERNEL + 1 : KERNEL + 2]
    product = dot_nn(ctx_s[...], wo_ref[...])
    scales = []
    for i, c in enumerate(own):
        here = slice(i * ROWS, (i + 1) * ROWS)
        tail = tail_s[pl.ds(pl.multiple_of(c * HALO, HALO), HALO)]
        rows = jnp.concatenate([tail, x_refs[0][i * BLOCK : (i + 1) * BLOCK]], axis=0)
        hidden = rows.astype(F32) + product[here]
        unit, inv = norm_stats(hidden)
        conv_in = (unit * gain).astype(BF16).astype(F32)
        e_s[i * ROWS : i * ROWS + HALO] = conv_in[:HALO] * keep[i]
        e_s[i * ROWS + HALO : (i + 1) * ROWS] = conv_in[HALO:]
        h_s[i * BLOCK : (i + 1) * BLOCK] = hidden[HALO:]
        u_s[here] = unit
        scales.append(inv)

    groups = BLOCK // SUB

    def conv(cols):
        bias = jnp.broadcast_to(small_ref[KERNEL : KERNEL + 1, cols], (SUB, LANES))
        taps = lambda j: taps_ref[j * SUB : (j + 1) * SUB, cols]
        for i in range(local):
            ext = e_s[i * ROWS : (i + 1) * ROWS, cols]
            acc = [bias] * groups
            for s in range(SUB):
                reps = (KERNEL - s + SUB - 1) // SUB
                skip, shift = divmod(s + KERNEL_GAP, SUB)
                moved = shifted_up(ext, shift)
                for a in range(reps):
                    tap = taps(SUB * a + s)
                    for r in range(groups):
                        at = (a + r + skip) * SUB
                        acc[r] = acc[r] + tap * moved[at : at + SUB]
            mixed = jnp.concatenate(acc, axis=0)
            gate = 0.5 * jnp.tanh(0.5 * mixed) + 0.5
            rows = slice(i * BLOCK, (i + 1) * BLOCK)
            out_ref[rows, cols] = (h_s[rows, cols] + mixed * gate).astype(BF16)
            slope = gate * (1.0 + mixed * (1.0 - gate))
            gm = grad_ref[rows, cols].astype(F32) * slope
            zeros = jnp.zeros((HALO, LANES), F32)
            padded = jnp.concatenate([zeros[:SUB], gm, zeros[:SUB]], axis=0)
            back = [None] * (ROWS // SUB)
            low = HALO // SUB - 1
            for s in range(SUB):
                reps = (KERNEL - s + SUB - 1) // SUB
                start = low if s else low + 1
                moved = shifted_up(padded, s)
                for a in range(reps):
                    tap = taps(KERNEL - 1 - SUB * a - s)
                    for g in range(start, ROWS // SUB):
                        r = g - a
                        piece = tap * moved[(g - low) * SUB : (g - low + 1) * SUB]
                        back[r] = piece if back[r] is None else back[r] + piece
            for r in range(ROWS // SUB):
                scale = keep[i] if r < HALO // SUB else 1.0
                gr_s[i * ROWS + r * SUB : i * ROWS + (r + 1) * SUB, cols] = back[r] * scale

    for k in range(0, width, LANES):
        conv(slice(k, k + LANES))

    for i in range(local):
        here = slice(i * ROWS, (i + 1) * ROWS)
        scaled = gr_s[here] * gain
        unit = u_s[here]
        first = jnp.mean(scaled, axis=-1, keepdims=True)
        second = jnp.mean(scaled * unit, axis=-1, keepdims=True)
        back = scales[i] * (scaled - first - unit * second)
        own_grad = grad_ref[i * BLOCK : (i + 1) * BLOCK].astype(F32) + back[HALO:]
        gc_s[i * ROWS : i * ROWS + HALO] = back[:HALO].astype(BF16)
        gc_s[i * ROWS + HALO : (i + 1) * ROWS] = own_grad.astype(BF16)
    for m in range(half):
        at = pl.ds(pl.multiple_of(((me ^ m) % half) * share, share), share)
        grad_context = dot_nn(gc_s[...], wot_ref[:, at]).astype(BF16)
        send_refs[m][...] = grad_context
        send_refs[m + half][...] = grad_context


def probs_kernel(sizes, tm, head_size, meta_ref, *refs):
    q_refs, kv_refs, n_refs = refs[:tm], refs[tm : 2 * tm], refs[2 * tm : 3 * tm]
    q4_ref, v4_ref, p_ref, d_ref, nt_ref, k4_ref = refs[3 * tm :]
    for m in range(tm):
        rows = n_refs[m].shape[0]
        nt_ref[:, m * rows : (m + 1) * rows] = n_refs[m][...].T
    table = Layout(meta_ref, *sizes)
    me = table.me()
    local = table.blocks // tm
    hq = q_refs[0].shape[1]
    share = q4_ref.shape[1]
    lead = pl.multiple_of((me % (tm // 2)) * share, share)
    for ref in (k4_ref, v4_ref):
        ref[: PAD * BLOCK] = jnp.zeros((PAD * BLOCK, share), BF16)
    for m in range(tm):
        for j in range(local):
            at = row_at(table.block_of((me ^ m) * local + j))
            here = slice(j * BLOCK, (j + 1) * BLOCK)
            q4_ref[at] = q_refs[m][here, pl.ds(lead, share)]
            k4_ref[at] = kv_refs[m][here, pl.ds(lead, share)]
            v4_ref[at] = kv_refs[m][here, pl.ds(pl.multiple_of(hq + lead, share), share)]
    heads = share // head_size
    mask_b = diag_mask(heads, BLOCK, head_size).astype(BF16)
    for c in range(table.blocks):
        own = slice((c + PAD) * BLOCK, (c + PAD + 1) * BLOCK)
        win = slice((c + PAD - LC) * BLOCK, (c + PAD + 1) * BLOCK)
        diag_q = spread(q4_ref[own], mask_b)
        probs, unit = window_probs(diag_q, k4_ref[win], table.reach(c), head_size)
        p_ref[c] = probs
        d_ref[c] = (1.0 - unit * unit) * (1.0 / math.sqrt(head_size))


def backward_kernel(sizes, tm, part, head_size, *refs):
    tables_ref, q4_ref, v4_ref, p_ref, d_ref, nt_ref = refs[:6]
    g_refs = refs[6 : 6 + tm][::-1]
    out_refs = refs[6 + tm : -5]
    gt_s, t_s, full_s, meta_ref, sem = refs[-5:]
    fetch = pltpu.make_async_copy(tables_ref, meta_ref, sem)
    fetch.start()
    t_s[...] = jnp.zeros(t_s.shape, F32)
    fetch.wait()
    table = Layout(meta_ref, *sizes)
    me = table.me()
    blocks = table.blocks
    local = blocks // tm
    share = q4_ref.shape[1]
    mask_b = diag_mask(share // head_size, BLOCK, head_size).astype(BF16)

    places = [(m, j, table.block_of((me ^ m) * local + j)) for m in range(tm) for j in range(local)]
    for m, j, b in places:
        gt_s[row_at(b)] = g_refs[m][j * ROWS + HALO : (j + 1) * ROWS].astype(F32)
    gt_s[(PAD - 1) * BLOCK : PAD * BLOCK] = jnp.zeros((BLOCK, share), F32)
    for m, j, b in places:
        at = row_at(b, HALO, -HALO)
        gt_s[at] = gt_s[at] + g_refs[m][j * ROWS : j * ROWS + HALO].astype(F32)

    def spans(c):
        own = slice((c + PAD) * BLOCK, (c + PAD + 1) * BLOCK)
        win = slice((c + PAD - LC) * BLOCK, (c + PAD + 1) * BLOCK)
        return own, win, spread(gt_s[own].astype(BF16), mask_b)

    @pl.when(me >= tm // 2)
    def _():
        for c in range(blocks):
            own, win, diag_g = spans(c)
            t_s[win] = t_s[win] + dot_nn(p_ref[c].astype(BF16), diag_g)

    @pl.when(me < tm // 2)
    def _():
        for c in range(blocks):
            own, win, diag_g = spans(c)
            grad_probs = dot_nt(v4_ref[win], diag_g)
            probs = p_ref[c]
            delta = jnp.sum(probs * grad_probs, axis=0, keepdims=True)
            grad_raw = probs * (grad_probs - delta) * d_ref[c]
            t_s[win] = t_s[win] + dot_nn(grad_raw.astype(BF16), spread(q4_ref[own], mask_b))

    terms = jnp.concatenate([t_s[row_at(b)].astype(BF16) for _, _, b in places], axis=0)
    full = dot_nn(nt_ref[...], terms)
    if len(out_refs) == 1:
        out_refs[0][...] = full.astype(BF16)
        return
    full_s[...] = full
    chip, core = table.dp() // 2, table.dp() % 2
    for q in range(out_refs[0].shape[0] // part):
        for ref, side in zip(out_refs, (core, 1 - core)):
            at = pl.ds(pl.multiple_of(((chip ^ q) * 2 + side) * part, part), part)
            ref[q * part : (q + 1) * part] = full_s[at].astype(ref.dtype)


def pair_kernel(kept_ref, got_ref, *out_refs):
    part = out_refs[0].shape[0]
    for q, ref in enumerate(out_refs):
        rows = slice(q * part, (q + 1) * part)
        ref[...] = (kept_ref[rows] + got_ref[rows].astype(F32)).astype(ref.dtype)


def sum_kernel(*refs):
    total = refs[0][...].astype(F32)
    for ref in refs[1:-1]:
        total = total + ref[...].astype(F32)
    refs[-1][...] = total


def on_device(
    frames,
    out_grad,
    norm1_gain,
    w_query,
    w_kv,
    w_out,
    norm2_gain,
    conv_kernel,
    conv_bias,
    utt_blocks,
    block_slot,
    left_count,
):
    tm = lax.axis_size("tm")
    dp = lax.axis_size("dp")
    rows, width = frames.shape
    blocks = block_slot.shape[1]
    utts = utt_blocks.shape[1]
    sizes = (utts, blocks)
    local = rows // BLOCK
    hq = w_query.shape[1]
    head_size = hq // HEADS
    kv_width = w_kv.shape[1]
    share = kv_width // tm
    padded = (blocks + PAD) * BLOCK

    def swap(value, axis, size, m):
        return lax.ppermute(value, axis, [(i, i ^ m) for i in range(size)])

    meta = jnp.concatenate(
        [
            lax.axis_index("tm").astype(jnp.int32).reshape(1, 1),
            lax.axis_index("dp").astype(jnp.int32).reshape(1, 1),
            utt_blocks,
            block_slot,
            left_count,
        ],
        axis=1,
    )
    small = jnp.concatenate(
        [conv_kernel, conv_bias.reshape(1, -1), norm2_gain.reshape(1, -1)], axis=0
    )

    smem = pl.BlockSpec(memory_space=pltpu.SMEM)
    vmem = pl.BlockSpec(memory_space=pltpu.VMEM)
    shape = jax.ShapeDtypeStruct

    taps, w_out_t = pl.pallas_call(
        taps_kernel,
        out_shape=[shape((KERNEL * SUB, width), F32), shape((width, hq), BF16)],
        in_specs=[vmem] * 2,
        out_specs=[vmem] * 2,
        compiler_params=pltpu.CompilerParams(vmem_limit_bytes=4 << 20),
        cost_estimate=pl.CostEstimate(flops=10**6, bytes_accessed=1 << 20, transcendentals=0),
        name="spread_taps",
    )(small, w_out)

    x, normed, queries, keys_values = {}, {}, {}, {}
    made = [shape((rows, w), BF16) for w in (width, hq, kv_width)]

    def project_shard(m, part):
        normed[m], queries[m], keys_values[m] = pl.pallas_call(
            project_kernel,
            out_shape=made,
            in_specs=[vmem] * 4,
            out_specs=[vmem] * 3,
            compiler_params=pltpu.CompilerParams(vmem_limit_bytes=4 << 20),
            cost_estimate=pl.CostEstimate(
                flops=2 * rows * width * (hq + kv_width), bytes_accessed=4 << 20, transcendentals=0
            ),
            name=f"project_rows_{m}",
        )(part, norm1_gain.reshape(1, -1), w_query, w_kv)

    project_shard(0, frames)
    x[0] = frames
    if tm == 4:
        x[2] = swap(frames, "tm", tm, 2)
        x[1] = swap(frames, "tm", tm, 1)
        facing, normed[0], taps, meta = lax.optimization_barrier((x[2], normed[0], taps, meta))
        x[3] = swap(facing, "tm", tm, 1)
        project_shard(2, facing)
        project_shard(1, x[1])
    else:
        for m in range(1, tm):
            x[m] = swap(frames, "tm", tm, m)
            if m < tm - 1:
                project_shard(m, x[m])

    def by_m(arrays):
        return [arrays[m] for m in sorted(arrays)]

    own_rows = local * ROWS
    results = pl.pallas_call(
        functools.partial(forward_kernel, sizes, tm, head_size),
        out_shape=[shape((rows, width), BF16)]
        + made
        + [shape((own_rows, share), BF16)] * tm,
        in_specs=[pl.BlockSpec(memory_space=pl.ANY)] + [vmem] * (6 + 3 * tm),
        out_specs=[vmem] * (tm + 4),
        scratch_shapes=[
            pltpu.VMEM((padded, hq), BF16),
            pltpu.VMEM((padded, kv_width), BF16),
            pltpu.VMEM(((blocks + 1) * HALO, width), BF16),
            pltpu.VMEM((own_rows, hq), BF16),
            pltpu.VMEM((own_rows, width), F32),
            pltpu.VMEM((rows, width), F32),
            pltpu.VMEM((own_rows, width), F32),
            pltpu.VMEM((own_rows, width), F32),
            pltpu.VMEM((own_rows, width), BF16),
            pltpu.SMEM(meta.shape, jnp.int32),
            pltpu.SemaphoreType.DMA,
        ],
        compiler_params=pltpu.CompilerParams(vmem_limit_bytes=16 << 20),
        name="forward_pass",
    )(
        meta,
        out_grad,
        w_out,
        w_out_t,
        small,
        taps,
        norm1_gain.reshape(1, -1),
        w_query,
        w_kv,
        *by_m(x),
        *by_m(queries),
        *by_m(keys_values),
    )
    layer_out, normed[tm - 1], queries[tm - 1], keys_values[tm - 1] = results[:4]
    sends = results[:3:-1]
    got = {0: sends[0]}
    for m in range(tm - 1, 0, -1):
        got[m] = swap(sends[m], "tm", tm, m)

    pair_width = share // head_size * BLOCK
    q4, v4, probs, slopes, normed_t = pl.pallas_call(
        functools.partial(probs_kernel, sizes, tm, head_size),
        out_shape=[shape((padded, share), BF16)] * 2
        + [shape((blocks, SPAN, pair_width), F32)] * 2
        + [shape((width, blocks * BLOCK), BF16)],
        in_specs=[smem] + [vmem] * (3 * tm),
        out_specs=[vmem] * 5,
        scratch_shapes=[pltpu.VMEM((padded, share), BF16)],
        compiler_params=pltpu.CompilerParams(vmem_limit_bytes=8 << 20),
        name="window_probs",
        cost_estimate=pl.CostEstimate(
            flops=2 * 10**9, bytes_accessed=4 * 10**6, transcendentals=800000
        ),
    )(meta, *by_m(queries), *by_m(keys_values), *by_m(normed))

    direct = dp <= 8
    half_width = width // 2
    if direct:
        piece_shapes = [shape((half_width, share), F32), shape((half_width, share), BF16)]
    else:
        piece_shapes = [shape((width, share), BF16)]
    pieces = pl.pallas_call(
        functools.partial(backward_kernel, sizes, tm, width // dp, head_size),
        out_shape=piece_shapes,
        in_specs=[pl.BlockSpec(memory_space=pl.ANY)] + [vmem] * (5 + tm),
        out_specs=[vmem] * len(piece_shapes),
        scratch_shapes=[
            pltpu.VMEM((padded, share), F32),
            pltpu.VMEM((padded, share), F32),
            pltpu.VMEM((width, share), F32),
            pltpu.SMEM(meta.shape, jnp.int32),
            pltpu.SemaphoreType.DMA,
        ],
        compiler_params=pltpu.CompilerParams(vmem_limit_bytes=12 << 20),
        name="key_value_terms",
    )(meta, q4, v4, probs, slopes, normed_t, *by_m(got)[::-1])

    if direct:
        kept, away = pieces
        arrived = swap(away, "dp", dp, 1)
        chips = dp // 2
        part = width // dp
        summed = pl.pallas_call(
            pair_kernel,
            out_shape=[shape((part, share), BF16)] * chips,
            in_specs=[vmem] * 2,
            out_specs=[vmem] * chips,
            compiler_params=pltpu.CompilerParams(vmem_limit_bytes=4 << 20),
            name="sum_pair",
        )(kept, arrived)
        terms = [swap(summed[q], "dp", dp, 2 * q) for q in range(chips - 1, 0, -1)]
        terms.append(summed[0])
    else:
        terms = [lax.psum_scatter(pieces[0], "dp", scatter_dimension=0, tiled=True)]
    kv_grad = pl.pallas_call(
        sum_kernel,
        out_shape=shape((width // dp, share), F32),
        in_specs=[vmem] * len(terms),
        out_specs=vmem,
        compiler_params=pltpu.CompilerParams(vmem_limit_bytes=4 << 20),
        name="sum_groups",
    )(*terms)
    return layer_out, kv_grad


def solution(mesh):
    return jax.shard_map(
        on_device,
        mesh=mesh,
        in_specs=(
            P(("dp", "tm"), None),
            P(("dp", "tm"), None),
            P(),
            P(),
            P(),
            P(),
            P(),
            P(),
            P(),
            P("dp", None),
            P("dp", None),
            P("dp", None),
        ),
        out_specs=(P(("dp", "tm"), None), P("dp", "tm")),
        check_vma=False,
    )
```

```python
import functools
import math

import jax
import jax.numpy as jnp
from jax import lax
from jax.experimental import pallas as pl
from jax.experimental.pallas import tpu as pltpu
from jax.sharding import PartitionSpec as P

HEADS = 8
KERNEL = 31
BLOCK = 64
LC = 2
SPAN = (LC + 1) * BLOCK
HALO = 32
ROWS = HALO + BLOCK
KERNEL_GAP = HALO - (KERNEL - 1)
PAD = LC + 1
EPSILON = 1e-05
SOFT_CAP = 4.0
LANES = 128
SUB = 8

BF16 = jnp.bfloat16
F32 = jnp.float32


def dot_nn(a, b):
    return lax.dot_general(a, b, (((1,), (0,)), ((), ())), preferred_element_type=F32)


def dot_nt(a, b):
    return lax.dot_general(a, b, (((1,), (1,)), ((), ())), preferred_element_type=F32)


def dot_tn(a, b):
    return lax.dot_general(a, b, (((0,), (0,)), ((), ())), preferred_element_type=F32)


def norm_stats(values):
    row_mean = jnp.mean(values, axis=-1, keepdims=True)
    centred = values - row_mean
    scale_inv = lax.rsqrt(jnp.mean(centred * centred, axis=-1, keepdims=True) + EPSILON)
    return centred * scale_inv, scale_inv


def sending_order(tm):
    return (*range(2, tm), 1, 0)


class Layout:
    def __init__(self, meta_ref, utts, blocks):
        self.ref, self.utts, self.blocks = meta_ref, utts, blocks

    def me(self):
        return self.ref[0, 0]

    def dp(self):
        return self.ref[0, 1]

    def block_of(self, slot):
        found = jnp.int32(0)
        for b in range(self.blocks):
            found = jnp.where(self.ref[0, 2 + self.utts + b] == slot, jnp.int32(b), found)
        return found

    def position(self, block):
        start = jnp.int32(0)
        first = jnp.int32(0)
        for u in range(self.utts):
            first = jnp.where(block >= start, start, first)
            start = start + self.ref[0, 2 + u]
        return block - first

    def reach(self, block):
        safe = jnp.maximum(block, 0)
        left = self.ref[0, 2 + self.utts + self.blocks + safe]
        return jnp.minimum(left, self.position(safe))


def row_at(block, count=BLOCK, shift=0):
    return pl.ds(pl.multiple_of((block + PAD) * BLOCK + shift, math.gcd(BLOCK, shift)), count)


def diag_mask(heads, rows, head_size):
    shape = (heads * rows, heads * head_size)
    row_head = lax.broadcasted_iota(jnp.int32, shape, 0) // rows
    col_head = lax.broadcasted_iota(jnp.int32, shape, 1) // head_size
    return jnp.where(row_head == col_head, 1.0, 0.0).astype(F32)


def spread(rows, mask_b):
    copies = mask_b.shape[0] // rows.shape[0]
    return jnp.concatenate([rows] * copies, axis=0) * mask_b


def fold_heads(full, mask_f, rows):
    kept = full * mask_f
    total = kept[:rows]
    for h in range(1, full.shape[0] // rows):
        total = total + kept[h * rows : (h + 1) * rows]
    return total


def window_probs(diag_q, k_win, reach):
    unit = jnp.tanh(dot_nt(k_win, diag_q))
    exped = jnp.exp2(unit * (SOFT_CAP * math.log2(math.e)))
    parts = [exped[w * BLOCK : (w + 1) * BLOCK] for w in range(LC + 1)]
    sums = [jnp.sum(part, axis=0, keepdims=True) for part in parts]
    flags = [jnp.where(reach >= LC - w, 1.0, 0.0).astype(F32) for w in range(LC)]
    total = sums[LC]
    for w in range(LC):
        total = total + sums[w] * flags[w]
    inverse = 1.0 / total
    scaled = [parts[w] * (inverse * flags[w]) for w in range(LC)] + [parts[LC] * inverse]
    return jnp.concatenate(scaled, axis=0), unit


def taps_kernel(small_ref, wo_ref, taps_ref, wot_ref):
    wot_ref[...] = wo_ref[...].T
    for j in range(KERNEL):
        rows = jnp.broadcast_to(small_ref[j : j + 1], (SUB, small_ref.shape[1]))
        taps_ref[j * SUB : (j + 1) * SUB] = rows


def project_kernel(x_ref, g1_ref, wq_ref, wkv_ref, n_ref, q_ref, kv_ref):
    project(x_ref, g1_ref, wq_ref, wkv_ref, n_ref, q_ref, kv_ref)


def project(x_ref, g1_ref, wq_ref, wkv_ref, n_ref, q_ref, kv_ref):
    unit, _ = norm_stats(x_ref[...].astype(F32))
    normed = (unit * g1_ref[...]).astype(BF16)
    n_ref[...] = normed
    q_ref[...] = dot_nn(normed, wq_ref[...]).astype(BF16)
    kv_ref[...] = dot_nn(normed, wkv_ref[...]).astype(BF16)


def shifted_up(values, shift):
    return pltpu.roll(values, values.shape[0] - shift, axis=0) if shift else values


def forward_kernel(sizes, tm, head_size, *refs):
    tables_ref, grad_ref, wo_ref, wot_ref, small_ref, taps_ref = refs[:6]
    g1_ref, wq_ref, wkv_ref = refs[6:9]
    refs = refs[9:]
    x_refs = refs[:tm]
    q_refs, kv_refs = (refs[tm + k * (tm - 1) : tm + (k + 1) * (tm - 1)] for k in range(2))
    refs = refs[3 * tm - 2 :]
    half = tm // 2
    out_ref, n_last, q_last, kv_last = refs[:4]
    send_refs = refs[4 : 4 + tm][::-1]
    q_ref, kv_ref, tail_s, ctx_s, e_s, h_s, u_s, gr_s, gc_s, meta_ref, sem = refs[4 + tm :]
    fetch = pltpu.make_async_copy(tables_ref, meta_ref, sem)
    fetch.start()
    project(x_refs[-1], g1_ref, wq_ref, wkv_ref, n_last, q_last, kv_last)
    q_refs, kv_refs = (*q_refs, q_last), (*kv_refs, kv_last)
    fetch.wait()

    table = Layout(meta_ref, *sizes)
    me = table.me()
    local = table.blocks // tm
    width = out_ref.shape[1]
    hq = q_ref.shape[1]
    share = send_refs[0].shape[1]

    for ref in (q_ref, kv_ref):
        ref[: PAD * BLOCK] = jnp.zeros((PAD * BLOCK, ref.shape[1]), BF16)
    tail_s[:HALO] = jnp.zeros((HALO, width), BF16)
    for m in range(tm):
        for j in range(local):
            b = table.block_of((me ^ m) * local + j)
            here = slice(j * BLOCK, (j + 1) * BLOCK)
            q_ref[row_at(b)] = q_refs[m][here]
            kv_ref[row_at(b)] = kv_refs[m][here]
            after = pl.ds(pl.multiple_of((b + 1) * HALO, HALO), HALO)
            tail_s[after] = x_refs[m][(j + 1) * BLOCK - HALO : (j + 1) * BLOCK]

    mid_heads = 256 // BLOCK
    mid_f = diag_mask(mid_heads, BLOCK, head_size)
    lower = 1.0 / (SOFT_CAP * math.sqrt(head_size))
    mid_b = (mid_f * lower).astype(BF16)
    side_f = diag_mask(HEADS, HALO, head_size)
    side_b = (side_f * lower).astype(BF16)

    own = [table.block_of(me * local + i) for i in range(local)]
    keep = [jnp.where(table.position(c) >= 1, 1.0, 0.0).astype(F32) for c in own]
    for i, c in enumerate(own):
        for blk, shift, count, put in ((c - 1, HALO, HALO, 0), (c, 0, BLOCK, HALO)):
            reach = table.reach(blk)
            win = row_at(blk - LC, SPAN)
            at = row_at(blk, count, shift)
            if count == BLOCK:
                groups, mask_f, mask_b = HEADS // mid_heads, mid_f, mid_b
            else:
                groups, mask_f, mask_b = 1, side_f, side_b
            wide = hq // groups
            for g in range(groups):
                cols = slice(g * wide, (g + 1) * wide)
                vcols = slice(hq + g * wide, hq + (g + 1) * wide)
                probs, _ = window_probs(spread(q_ref[at, cols], mask_b), kv_ref[win, cols], reach)
                full = dot_tn(probs.astype(BF16), kv_ref[win, vcols])
                ctx_s[i * ROWS + put : i * ROWS + put + count, cols] = fold_heads(
                    full, mask_f, count
                ).astype(BF16)

    gain = small_ref[KERNEL + 1 : KERNEL + 2]
    product = dot_nn(ctx_s[...], wo_ref[...])
    scales = []
    for i, c in enumerate(own):
        here = slice(i * ROWS, (i + 1) * ROWS)
        tail = tail_s[pl.ds(pl.multiple_of(c * HALO, HALO), HALO)]
        rows = jnp.concatenate([tail, x_refs[0][i * BLOCK : (i + 1) * BLOCK]], axis=0)
        hidden = rows.astype(F32) + product[here]
        unit, inv = norm_stats(hidden)
        conv_in = (unit * gain).astype(BF16).astype(F32)
        e_s[i * ROWS : i * ROWS + HALO] = conv_in[:HALO] * keep[i]
        e_s[i * ROWS + HALO : (i + 1) * ROWS] = conv_in[HALO:]
        h_s[i * BLOCK : (i + 1) * BLOCK] = hidden[HALO:]
        u_s[here] = unit
        scales.append(inv)

    groups = BLOCK // SUB

    def conv(cols):
        bias = jnp.broadcast_to(small_ref[KERNEL : KERNEL + 1, cols], (SUB, LANES))
        taps = lambda j: taps_ref[j * SUB : (j + 1) * SUB, cols]
        for i in range(local):
            ext = e_s[i * ROWS : (i + 1) * ROWS, cols]
            acc = [bias] * groups
            for s in range(SUB):
                reps = (KERNEL - s + SUB - 1) // SUB
                skip, shift = divmod(s + KERNEL_GAP, SUB)
                moved = shifted_up(ext, shift)
                for a in range(reps):
                    tap = taps(SUB * a + s)
                    for r in range(groups):
                        at = (a + r + skip) * SUB
                        acc[r] = acc[r] + tap * moved[at : at + SUB]
            mixed = jnp.concatenate(acc, axis=0)
            gate = 0.5 * jnp.tanh(0.5 * mixed) + 0.5
            rows = slice(i * BLOCK, (i + 1) * BLOCK)
            out_ref[rows, cols] = (h_s[rows, cols] + mixed * gate).astype(BF16)
            slope = gate * (1.0 + mixed * (1.0 - gate))
            gm = grad_ref[rows, cols].astype(F32) * slope
            zeros = jnp.zeros((HALO, LANES), F32)
            padded = jnp.concatenate([zeros[:SUB], gm, zeros[:SUB]], axis=0)
            back = [None] * (ROWS // SUB)
            low = HALO // SUB - 1
            for s in range(SUB):
                reps = (KERNEL - s + SUB - 1) // SUB
                start = low if s else low + 1
                moved = shifted_up(padded, s)
                for a in range(reps):
                    tap = taps(KERNEL - 1 - SUB * a - s)
                    for g in range(start, ROWS // SUB):
                        r = g - a
                        piece = tap * moved[(g - low) * SUB : (g - low + 1) * SUB]
                        back[r] = piece if back[r] is None else back[r] + piece
            for r in range(ROWS // SUB):
                scale = keep[i] if r < HALO // SUB else 1.0
                gr_s[i * ROWS + r * SUB : i * ROWS + (r + 1) * SUB, cols] = back[r] * scale

    for k in range(0, width, LANES):
        conv(slice(k, k + LANES))

    for i in range(local):
        here = slice(i * ROWS, (i + 1) * ROWS)
        scaled = gr_s[here] * gain
        unit = u_s[here]
        first = jnp.mean(scaled, axis=-1, keepdims=True)
        second = jnp.mean(scaled * unit, axis=-1, keepdims=True)
        back = scales[i] * (scaled - first - unit * second)
        own_grad = grad_ref[i * BLOCK : (i + 1) * BLOCK].astype(F32) + back[HALO:]
        gc_s[i * ROWS : i * ROWS + HALO] = back[:HALO].astype(BF16)
        gc_s[i * ROWS + HALO : (i + 1) * ROWS] = own_grad.astype(BF16)
    for m in range(half):
        at = pl.ds(pl.multiple_of(((me ^ m) % half) * share, share), share)
        grad_context = dot_nn(gc_s[...], wot_ref[:, at]).astype(BF16)
        send_refs[m][...] = grad_context
        send_refs[m + half][...] = grad_context


def probs_kernel(sizes, tm, head_size, meta_ref, *refs):
    q_refs, kv_refs, n_refs = refs[:tm], refs[tm : 2 * tm], refs[2 * tm : 3 * tm]
    q4_ref, v4_ref, p_ref, d_ref, nt_ref, k4_ref = refs[3 * tm :]
    for m in range(tm):
        rows = n_refs[m].shape[0]
        nt_ref[:, m * rows : (m + 1) * rows] = n_refs[m][...].T
    table = Layout(meta_ref, *sizes)
    me = table.me()
    local = table.blocks // tm
    hq = q_refs[0].shape[1]
    share = q4_ref.shape[1]
    lead = pl.multiple_of((me % (tm // 2)) * share, share)
    for ref in (k4_ref, v4_ref):
        ref[: PAD * BLOCK] = jnp.zeros((PAD * BLOCK, share), BF16)
    for m in range(tm):
        for j in range(local):
            at = row_at(table.block_of((me ^ m) * local + j))
            here = slice(j * BLOCK, (j + 1) * BLOCK)
            q4_ref[at] = q_refs[m][here, pl.ds(lead, share)]
            k4_ref[at] = kv_refs[m][here, pl.ds(lead, share)]
            v4_ref[at] = kv_refs[m][here, pl.ds(pl.multiple_of(hq + lead, share), share)]
    heads = share // head_size
    lower = 1.0 / (SOFT_CAP * math.sqrt(head_size))
    mask_b = (diag_mask(heads, BLOCK, head_size) * lower).astype(BF16)
    for c in range(table.blocks):
        own = slice((c + PAD) * BLOCK, (c + PAD + 1) * BLOCK)
        win = slice((c + PAD - LC) * BLOCK, (c + PAD + 1) * BLOCK)
        diag_q = spread(q4_ref[own], mask_b)
        probs, unit = window_probs(diag_q, k4_ref[win], table.reach(c))
        p_ref[c] = probs
        d_ref[c] = (1.0 - unit * unit) * (1.0 / math.sqrt(head_size))


def backward_kernel(sizes, tm, part, head_size, *refs):
    tables_ref, q4_ref, v4_ref, p_ref, d_ref, nt_ref = refs[:6]
    g_refs = dict(zip(sending_order(tm), refs[6 : 6 + tm]))
    out_refs = refs[6 + tm : -5]
    gt_s, t_s, full_s, meta_ref, sem = refs[-5:]
    fetch = pltpu.make_async_copy(tables_ref, meta_ref, sem)
    fetch.start()
    t_s[...] = jnp.zeros(t_s.shape, F32)
    fetch.wait()
    table = Layout(meta_ref, *sizes)
    me = table.me()
    blocks = table.blocks
    local = blocks // tm
    share = q4_ref.shape[1]
    mask_b = diag_mask(share // head_size, BLOCK, head_size).astype(BF16)

    places = [(m, j, table.block_of((me ^ m) * local + j)) for m in range(tm) for j in range(local)]
    for m, j, b in places:
        gt_s[row_at(b)] = g_refs[m][j * ROWS + HALO : (j + 1) * ROWS].astype(F32)
    gt_s[(PAD - 1) * BLOCK : PAD * BLOCK] = jnp.zeros((BLOCK, share), F32)
    for m, j, b in places:
        at = row_at(b, HALO, -HALO)
        gt_s[at] = gt_s[at] + g_refs[m][j * ROWS : j * ROWS + HALO].astype(F32)

    def spans(c):
        own = slice((c + PAD) * BLOCK, (c + PAD + 1) * BLOCK)
        win = slice((c + PAD - LC) * BLOCK, (c + PAD + 1) * BLOCK)
        return own, win, spread(gt_s[own].astype(BF16), mask_b)

    @pl.when(me >= tm // 2)
    def _():
        for c in range(blocks):
            own, win, diag_g = spans(c)
            t_s[win] = t_s[win] + dot_nn(p_ref[c].astype(BF16), diag_g)

    @pl.when(me < tm // 2)
    def _():
        for c in range(blocks):
            own, win, diag_g = spans(c)
            grad_probs = dot_nt(v4_ref[win], diag_g)
            probs = p_ref[c]
            delta = jnp.sum(probs * grad_probs, axis=0, keepdims=True)
            grad_raw = probs * (grad_probs - delta) * d_ref[c]
            t_s[win] = t_s[win] + dot_nn(grad_raw.astype(BF16), spread(q4_ref[own], mask_b))

    terms = jnp.concatenate([t_s[row_at(b)].astype(BF16) for _, _, b in places], axis=0)
    full = dot_nn(nt_ref[...], terms)
    if len(out_refs) == 1:
        out_refs[0][...] = full.astype(BF16)
        return
    full_s[...] = full
    chip, core = table.dp() // 2, table.dp() % 2
    for q in range(out_refs[0].shape[0] // part):
        for ref, side in zip(out_refs, (core, 1 - core)):
            at = pl.ds(pl.multiple_of(((chip ^ q) * 2 + side) * part, part), part)
            ref[q * part : (q + 1) * part] = full_s[at].astype(ref.dtype)


def pair_kernel(kept_ref, got_ref, *out_refs):
    part = out_refs[0].shape[0]
    for q, ref in enumerate(out_refs):
        rows = slice(q * part, (q + 1) * part)
        ref[...] = (kept_ref[rows] + got_ref[rows].astype(F32)).astype(ref.dtype)


def sum_kernel(*refs):
    total = refs[0][...].astype(F32)
    for ref in refs[1:-1]:
        total = total + ref[...].astype(F32)
    refs[-1][...] = total


def on_device(
    frames,
    out_grad,
    norm1_gain,
    w_query,
    w_kv,
    w_out,
    norm2_gain,
    conv_kernel,
    conv_bias,
    utt_blocks,
    block_slot,
    left_count,
):
    tm = lax.axis_size("tm")
    dp = lax.axis_size("dp")
    rows, width = frames.shape
    blocks = block_slot.shape[1]
    utts = utt_blocks.shape[1]
    sizes = (utts, blocks)
    local = rows // BLOCK
    hq = w_query.shape[1]
    head_size = hq // HEADS
    kv_width = w_kv.shape[1]
    share = kv_width // tm
    padded = (blocks + PAD) * BLOCK

    def swap(value, axis, size, m):
        return lax.ppermute(value, axis, [(i, i ^ m) for i in range(size)])

    meta = jnp.concatenate(
        [
            lax.axis_index("tm").astype(jnp.int32).reshape(1, 1),
            lax.axis_index("dp").astype(jnp.int32).reshape(1, 1),
            utt_blocks,
            block_slot,
            left_count,
        ],
        axis=1,
    )
    small = jnp.concatenate(
        [conv_kernel, conv_bias.reshape(1, -1), norm2_gain.reshape(1, -1)], axis=0
    )

    smem = pl.BlockSpec(memory_space=pltpu.SMEM)
    vmem = pl.BlockSpec(memory_space=pltpu.VMEM)
    shape = jax.ShapeDtypeStruct

    taps, w_out_t = pl.pallas_call(
        taps_kernel,
        out_shape=[shape((KERNEL * SUB, width), F32), shape((width, hq), BF16)],
        in_specs=[vmem] * 2,
        out_specs=[vmem] * 2,
        compiler_params=pltpu.CompilerParams(vmem_limit_bytes=4 << 20),
        cost_estimate=pl.CostEstimate(flops=10**6, bytes_accessed=1 << 20, transcendentals=0),
        name="spread_taps",
    )(small, w_out)

    x, normed, queries, keys_values = {}, {}, {}, {}
    made = [shape((rows, w), BF16) for w in (width, hq, kv_width)]

    def project_shard(m, part):
        normed[m], queries[m], keys_values[m] = pl.pallas_call(
            project_kernel,
            out_shape=made,
            in_specs=[vmem] * 4,
            out_specs=[vmem] * 3,
            compiler_params=pltpu.CompilerParams(vmem_limit_bytes=4 << 20),
            cost_estimate=pl.CostEstimate(
                flops=2 * rows * width * (hq + kv_width), bytes_accessed=4 << 20, transcendentals=0
            ),
            name=f"project_rows_{m}",
        )(part, norm1_gain.reshape(1, -1), w_query, w_kv)

    project_shard(0, frames)
    x[0] = frames
    if tm == 4:
        x[2] = swap(frames, "tm", tm, 2)
        x[1] = swap(frames, "tm", tm, 1)
        facing, normed[0], taps, meta = lax.optimization_barrier((x[2], normed[0], taps, meta))
        x[3] = swap(facing, "tm", tm, 1)
        project_shard(2, facing)
        project_shard(1, x[1])
    else:
        for m in range(1, tm):
            x[m] = swap(frames, "tm", tm, m)
            if m < tm - 1:
                project_shard(m, x[m])

    def by_m(arrays):
        return [arrays[m] for m in sorted(arrays)]

    own_rows = local * ROWS
    results = pl.pallas_call(
        functools.partial(forward_kernel, sizes, tm, head_size),
        out_shape=[shape((rows, width), BF16)]
        + made
        + [shape((own_rows, share), BF16)] * tm,
        in_specs=[pl.BlockSpec(memory_space=pl.ANY)] + [vmem] * (6 + 3 * tm),
        out_specs=[vmem] * (tm + 4),
        scratch_shapes=[
            pltpu.VMEM((padded, hq), BF16),
            pltpu.VMEM((padded, kv_width), BF16),
            pltpu.VMEM(((blocks + 1) * HALO, width), BF16),
            pltpu.VMEM((own_rows, hq), BF16),
            pltpu.VMEM((own_rows, width), F32),
            pltpu.VMEM((rows, width), F32),
            pltpu.VMEM((own_rows, width), F32),
            pltpu.VMEM((own_rows, width), F32),
            pltpu.VMEM((own_rows, width), BF16),
            pltpu.SMEM(meta.shape, jnp.int32),
            pltpu.SemaphoreType.DMA,
        ],
        compiler_params=pltpu.CompilerParams(vmem_limit_bytes=16 << 20),
        name="forward_pass",
    )(
        meta,
        out_grad,
        w_out,
        w_out_t,
        small,
        taps,
        norm1_gain.reshape(1, -1),
        w_query,
        w_kv,
        *by_m(x),
        *by_m(queries),
        *by_m(keys_values),
    )
    layer_out, normed[tm - 1], queries[tm - 1], keys_values[tm - 1] = results[:4]
    sends = results[:3:-1]
    got = {0: sends[0]}
    for m in range(tm - 1, 0, -1):
        got[m] = swap(sends[m], "tm", tm, m)

    pair_width = share // head_size * BLOCK
    q4, v4, probs, slopes, normed_t = pl.pallas_call(
        functools.partial(probs_kernel, sizes, tm, head_size),
        out_shape=[shape((padded, share), BF16)] * 2
        + [shape((blocks, SPAN, pair_width), F32)] * 2
        + [shape((width, blocks * BLOCK), BF16)],
        in_specs=[smem] + [vmem] * (3 * tm),
        out_specs=[vmem] * 5,
        scratch_shapes=[pltpu.VMEM((padded, share), BF16)],
        compiler_params=pltpu.CompilerParams(vmem_limit_bytes=8 << 20),
        name="window_probs",
        cost_estimate=pl.CostEstimate(
            flops=2 * 10**9, bytes_accessed=4 * 10**6, transcendentals=800000
        ),
    )(meta, *by_m(queries), *by_m(keys_values), *by_m(normed))

    direct = dp <= 8
    half_width = width // 2
    if direct:
        piece_shapes = [shape((half_width, share), F32), shape((half_width, share), BF16)]
    else:
        piece_shapes = [shape((width, share), BF16)]
    pieces = pl.pallas_call(
        functools.partial(backward_kernel, sizes, tm, width // dp, head_size),
        out_shape=piece_shapes,
        in_specs=[pl.BlockSpec(memory_space=pl.ANY)] + [vmem] * (5 + tm),
        out_specs=[vmem] * len(piece_shapes),
        scratch_shapes=[
            pltpu.VMEM((padded, share), F32),
            pltpu.VMEM((padded, share), F32),
            pltpu.VMEM((width, share), F32),
            pltpu.SMEM(meta.shape, jnp.int32),
            pltpu.SemaphoreType.DMA,
        ],
        compiler_params=pltpu.CompilerParams(vmem_limit_bytes=12 << 20),
        name="key_value_terms",
    )(meta, q4, v4, probs, slopes, normed_t, *[got[m] for m in sending_order(tm)])

    if direct:
        kept, away = pieces
        arrived = swap(away, "dp", dp, 1)
        chips = dp // 2
        part = width // dp
        summed = pl.pallas_call(
            pair_kernel,
            out_shape=[shape((part, share), BF16)] * chips,
            in_specs=[vmem] * 2,
            out_specs=[vmem] * chips,
            compiler_params=pltpu.CompilerParams(vmem_limit_bytes=4 << 20),
            name="sum_pair",
        )(kept, arrived)
        terms = [swap(summed[q], "dp", dp, 2 * q) for q in range(chips - 1, 0, -1)]
        terms.append(summed[0])
    else:
        terms = [lax.psum_scatter(pieces[0], "dp", scatter_dimension=0, tiled=True)]
    kv_grad = pl.pallas_call(
        sum_kernel,
        out_shape=shape((width // dp, share), F32),
        in_specs=[vmem] * len(terms),
        out_specs=vmem,
        compiler_params=pltpu.CompilerParams(vmem_limit_bytes=4 << 20),
        name="sum_groups",
    )(*terms)
    return layer_out, kv_grad


def solution(mesh):
    return jax.shard_map(
        on_device,
        mesh=mesh,
        in_specs=(
            P(("dp", "tm"), None),
            P(("dp", "tm"), None),
            P(),
            P(),
            P(),
            P(),
            P(),
            P(),
            P(),
            P("dp", None),
            P("dp", None),
            P("dp", None),
        ),
        out_specs=(P(("dp", "tm"), None), P("dp", "tm")),
        check_vma=False,
    )
```

```python
import functools
import math

import jax
import jax.numpy as jnp
from jax import lax
from jax.experimental import pallas as pl
from jax.experimental.pallas import tpu as pltpu
from jax.sharding import PartitionSpec as P

HEADS = 8
KERNEL = 31
BLOCK = 64
LC = 2
SPAN = (LC + 1) * BLOCK
HALO = 32
ROWS = HALO + BLOCK
KERNEL_GAP = HALO - (KERNEL - 1)
PAD = LC + 1
EPSILON = 1e-05
SOFT_CAP = 4.0
LANES = 128
SUB = 8

BF16 = jnp.bfloat16
F32 = jnp.float32


def dot_nn(a, b):
    return lax.dot_general(a, b, (((1,), (0,)), ((), ())), preferred_element_type=F32)


def dot_nt(a, b):
    return lax.dot_general(a, b, (((1,), (1,)), ((), ())), preferred_element_type=F32)


def dot_tn(a, b):
    return lax.dot_general(a, b, (((0,), (0,)), ((), ())), preferred_element_type=F32)


def norm_stats(values):
    row_mean = jnp.mean(values, axis=-1, keepdims=True)
    centred = values - row_mean
    scale_inv = lax.rsqrt(jnp.mean(centred * centred, axis=-1, keepdims=True) + EPSILON)
    return centred * scale_inv, scale_inv


def sending_order(tm):
    return (*range(2, tm), 1, 0)


class Layout:
    def __init__(self, meta_ref, utts, blocks):
        self.ref, self.utts, self.blocks = meta_ref, utts, blocks

    def me(self):
        return self.ref[0, 0]

    def dp(self):
        return self.ref[0, 1]

    def block_of(self, slot):
        found = jnp.int32(0)
        for b in range(self.blocks):
            found = jnp.where(self.ref[0, 2 + self.utts + b] == slot, jnp.int32(b), found)
        return found

    def position(self, block):
        start = jnp.int32(0)
        first = jnp.int32(0)
        for u in range(self.utts):
            first = jnp.where(block >= start, start, first)
            start = start + self.ref[0, 2 + u]
        return block - first

    def reach(self, block):
        safe = jnp.maximum(block, 0)
        left = self.ref[0, 2 + self.utts + self.blocks + safe]
        return jnp.minimum(left, self.position(safe))


def row_at(block, count=BLOCK, shift=0):
    return pl.ds(pl.multiple_of((block + PAD) * BLOCK + shift, math.gcd(BLOCK, shift)), count)


def diag_mask(heads, rows, head_size):
    shape = (heads * rows, heads * head_size)
    row_head = lax.broadcasted_iota(jnp.int32, shape, 0) // rows
    col_head = lax.broadcasted_iota(jnp.int32, shape, 1) // head_size
    return jnp.where(row_head == col_head, 1.0, 0.0).astype(F32)


def spread(rows, mask_b):
    copies = mask_b.shape[0] // rows.shape[0]
    return jnp.concatenate([rows] * copies, axis=0) * mask_b


def fold_heads(full, mask_f, rows):
    kept = full * mask_f
    total = kept[:rows]
    for h in range(1, full.shape[0] // rows):
        total = total + kept[h * rows : (h + 1) * rows]
    return total


def window_probs(diag_q, k_win, reach):
    unit = jnp.tanh(dot_nt(k_win, diag_q))
    exped = jnp.exp2(unit * (SOFT_CAP * math.log2(math.e)))
    parts = [exped[w * BLOCK : (w + 1) * BLOCK] for w in range(LC + 1)]
    sums = [jnp.sum(part, axis=0, keepdims=True) for part in parts]
    flags = [jnp.where(reach >= LC - w, 1.0, 0.0).astype(F32) for w in range(LC)]
    total = sums[LC]
    for w in range(LC):
        total = total + sums[w] * flags[w]
    inverse = 1.0 / total
    scaled = [parts[w] * (inverse * flags[w]) for w in range(LC)] + [parts[LC] * inverse]
    return jnp.concatenate(scaled, axis=0), unit


def taps_kernel(small_ref, wo_ref, taps_ref, wot_ref):
    wot_ref[...] = wo_ref[...].T
    for j in range(KERNEL):
        rows = jnp.broadcast_to(small_ref[j : j + 1], (SUB, small_ref.shape[1]))
        taps_ref[j * SUB : (j + 1) * SUB] = rows


def project_kernel(x_ref, g1_ref, wq_ref, wkv_ref, n_ref, q_ref, kv_ref):
    project(x_ref, g1_ref, wq_ref, wkv_ref, n_ref, q_ref, kv_ref)


def project(x_ref, g1_ref, wq_ref, wkv_ref, n_ref, q_ref, kv_ref):
    unit, _ = norm_stats(x_ref[...].astype(F32))
    normed = (unit * g1_ref[...]).astype(BF16)
    n_ref[...] = normed
    q_ref[...] = dot_nn(normed, wq_ref[...]).astype(BF16)
    kv_ref[...] = dot_nn(normed, wkv_ref[...]).astype(BF16)


def shifted_up(values, shift):
    return pltpu.roll(values, values.shape[0] - shift, axis=0) if shift else values


def forward_kernel(sizes, tm, head_size, *refs):
    tables_ref, grad_ref, wo_ref, wot_ref, small_ref, taps_ref = refs[:6]
    g1_ref, wq_ref, wkv_ref = refs[6:9]
    refs = refs[9:]
    x_refs = refs[:tm]
    q_refs, kv_refs = (refs[tm + k * (tm - 1) : tm + (k + 1) * (tm - 1)] for k in range(2))
    refs = refs[3 * tm - 2 :]
    half = tm // 2
    out_ref, n_last, q_last, kv_last = refs[:4]
    send_refs = refs[4 : 4 + tm][::-1]
    q_ref, kv_ref, tail_s, ctx_s, e_s, h_s, u_s, gr_s, gc_s, meta_ref, sem = refs[4 + tm :]
    fetch = pltpu.make_async_copy(tables_ref, meta_ref, sem)
    fetch.start()
    project(x_refs[-1], g1_ref, wq_ref, wkv_ref, n_last, q_last, kv_last)
    q_refs, kv_refs = (*q_refs, q_last), (*kv_refs, kv_last)
    fetch.wait()

    table = Layout(meta_ref, *sizes)
    me = table.me()
    local = table.blocks // tm
    width = out_ref.shape[1]
    hq = q_ref.shape[1]
    share = send_refs[0].shape[1]

    for ref in (q_ref, kv_ref):
        ref[: PAD * BLOCK] = jnp.zeros((PAD * BLOCK, ref.shape[1]), BF16)
    tail_s[:HALO] = jnp.zeros((HALO, width), BF16)
    for m in range(tm):
        for j in range(local):
            b = table.block_of((me ^ m) * local + j)
            here = slice(j * BLOCK, (j + 1) * BLOCK)
            q_ref[row_at(b)] = q_refs[m][here]
            kv_ref[row_at(b)] = kv_refs[m][here]
            after = pl.ds(pl.multiple_of((b + 1) * HALO, HALO), HALO)
            tail_s[after] = x_refs[m][(j + 1) * BLOCK - HALO : (j + 1) * BLOCK]

    mid_heads = 256 // BLOCK
    mid_f = diag_mask(mid_heads, BLOCK, head_size)
    lower = 1.0 / (SOFT_CAP * math.sqrt(head_size))
    mid_b = (mid_f * lower).astype(BF16)
    side_f = diag_mask(HEADS, HALO, head_size)
    side_b = (side_f * lower).astype(BF16)

    own = [table.block_of(me * local + i) for i in range(local)]
    keep = [jnp.where(table.position(c) >= 1, 1.0, 0.0).astype(F32) for c in own]
    for i, c in enumerate(own):
        for blk, shift, count, put in ((c - 1, HALO, HALO, 0), (c, 0, BLOCK, HALO)):
            reach = table.reach(blk)
            win = row_at(blk - LC, SPAN)
            at = row_at(blk, count, shift)
            if count == BLOCK:
                groups, mask_f, mask_b = HEADS // mid_heads, mid_f, mid_b
            else:
                groups, mask_f, mask_b = 1, side_f, side_b
            wide = hq // groups
            for g in range(groups):
                cols = slice(g * wide, (g + 1) * wide)
                vcols = slice(hq + g * wide, hq + (g + 1) * wide)
                probs, _ = window_probs(spread(q_ref[at, cols], mask_b), kv_ref[win, cols], reach)
                full = dot_tn(probs.astype(BF16), kv_ref[win, vcols])
                ctx_s[i * ROWS + put : i * ROWS + put + count, cols] = fold_heads(
                    full, mask_f, count
                ).astype(BF16)

    gain = small_ref[KERNEL + 1 : KERNEL + 2]
    product = dot_nn(ctx_s[...], wo_ref[...])
    scales = []
    for i, c in enumerate(own):
        here = slice(i * ROWS, (i + 1) * ROWS)
        tail = tail_s[pl.ds(pl.multiple_of(c * HALO, HALO), HALO)]
        rows = jnp.concatenate([tail, x_refs[0][i * BLOCK : (i + 1) * BLOCK]], axis=0)
        hidden = rows.astype(F32) + product[here]
        unit, inv = norm_stats(hidden)
        conv_in = (unit * gain).astype(BF16).astype(F32)
        e_s[i * ROWS : i * ROWS + HALO] = conv_in[:HALO] * keep[i]
        e_s[i * ROWS + HALO : (i + 1) * ROWS] = conv_in[HALO:]
        h_s[i * BLOCK : (i + 1) * BLOCK] = hidden[HALO:]
        u_s[here] = unit
        scales.append(inv)

    groups = BLOCK // SUB

    def conv(cols):
        bias = jnp.broadcast_to(small_ref[KERNEL : KERNEL + 1, cols], (SUB, LANES))
        taps = lambda j: taps_ref[j * SUB : (j + 1) * SUB, cols]
        for i in range(local):
            ext = e_s[i * ROWS : (i + 1) * ROWS, cols]
            acc = [bias] * groups
            for s in range(SUB):
                reps = (KERNEL - s + SUB - 1) // SUB
                skip, shift = divmod(s + KERNEL_GAP, SUB)
                moved = shifted_up(ext, shift)
                for a in range(reps):
                    tap = taps(SUB * a + s)
                    for r in range(groups):
                        at = (a + r + skip) * SUB
                        acc[r] = acc[r] + tap * moved[at : at + SUB]
            mixed = jnp.concatenate(acc, axis=0)
            gate = 0.5 * jnp.tanh(0.5 * mixed) + 0.5
            rows = slice(i * BLOCK, (i + 1) * BLOCK)
            out_ref[rows, cols] = (h_s[rows, cols] + mixed * gate).astype(BF16)
            slope = gate * (1.0 + mixed * (1.0 - gate))
            gm = grad_ref[rows, cols].astype(F32) * slope
            zeros = jnp.zeros((HALO, LANES), F32)
            padded = jnp.concatenate([zeros[:SUB], gm, zeros[:SUB]], axis=0)
            back = [None] * (ROWS // SUB)
            low = HALO // SUB - 1
            for s in range(SUB):
                reps = (KERNEL - s + SUB - 1) // SUB
                start = low if s else low + 1
                moved = shifted_up(padded, s)
                for a in range(reps):
                    tap = taps(KERNEL - 1 - SUB * a - s)
                    for g in range(start, ROWS // SUB):
                        r = g - a
                        piece = tap * moved[(g - low) * SUB : (g - low + 1) * SUB]
                        back[r] = piece if back[r] is None else back[r] + piece
            for r in range(ROWS // SUB):
                scale = keep[i] if r < HALO // SUB else 1.0
                gr_s[i * ROWS + r * SUB : i * ROWS + (r + 1) * SUB, cols] = back[r] * scale

    for k in range(0, width, LANES):
        conv(slice(k, k + LANES))

    for i in range(local):
        here = slice(i * ROWS, (i + 1) * ROWS)
        scaled = gr_s[here] * gain
        unit = u_s[here]
        first = jnp.mean(scaled, axis=-1, keepdims=True)
        second = jnp.mean(scaled * unit, axis=-1, keepdims=True)
        back = scales[i] * (scaled - first - unit * second)
        own_grad = grad_ref[i * BLOCK : (i + 1) * BLOCK].astype(F32) + back[HALO:]
        gc_s[i * ROWS : i * ROWS + HALO] = back[:HALO].astype(BF16)
        gc_s[i * ROWS + HALO : (i + 1) * ROWS] = own_grad.astype(BF16)
    for m in range(half):
        at = pl.ds(pl.multiple_of(((me ^ m) % half) * share, share), share)
        grad_context = dot_nn(gc_s[...], wot_ref[:, at]).astype(BF16)
        send_refs[m][...] = grad_context
        send_refs[m + half][...] = grad_context


def probs_kernel(sizes, tm, head_size, meta_ref, *refs):
    q_refs, kv_refs, n_refs = refs[:tm], refs[tm : 2 * tm], refs[2 * tm : 3 * tm]
    made_ref, out_ref, q4_ref, v4_ref, p_ref, d_ref, nt_ref, k4_ref = refs[3 * tm :]
    out_ref[...] = made_ref[...]
    for m in range(tm):
        rows = n_refs[m].shape[0]
        nt_ref[:, m * rows : (m + 1) * rows] = n_refs[m][...].T
    table = Layout(meta_ref, *sizes)
    me = table.me()
    local = table.blocks // tm
    hq = q_refs[0].shape[1]
    share = q4_ref.shape[1]
    lead = pl.multiple_of((me % (tm // 2)) * share, share)
    for ref in (k4_ref, v4_ref):
        ref[: PAD * BLOCK] = jnp.zeros((PAD * BLOCK, share), BF16)
    for m in range(tm):
        for j in range(local):
            at = row_at(table.block_of((me ^ m) * local + j))
            here = slice(j * BLOCK, (j + 1) * BLOCK)
            q4_ref[at] = q_refs[m][here, pl.ds(lead, share)]
            k4_ref[at] = kv_refs[m][here, pl.ds(lead, share)]
            v4_ref[at] = kv_refs[m][here, pl.ds(pl.multiple_of(hq + lead, share), share)]
    heads = share // head_size
    lower = 1.0 / (SOFT_CAP * math.sqrt(head_size))
    mask_b = (diag_mask(heads, BLOCK, head_size) * lower).astype(BF16)
    for c in range(table.blocks):
        own = slice((c + PAD) * BLOCK, (c + PAD + 1) * BLOCK)
        win = slice((c + PAD - LC) * BLOCK, (c + PAD + 1) * BLOCK)
        diag_q = spread(q4_ref[own], mask_b)
        probs, unit = window_probs(diag_q, k4_ref[win], table.reach(c))
        p_ref[c] = probs
        d_ref[c] = (1.0 - unit * unit) * (1.0 / math.sqrt(head_size))


def backward_kernel(sizes, tm, part, head_size, *refs):
    tables_ref, q4_ref, v4_ref, p_ref, d_ref, nt_ref = refs[:6]
    g_refs = dict(zip(sending_order(tm), refs[6 : 6 + tm]))
    out_refs = refs[6 + tm : -5]
    gt_s, t_s, full_s, meta_ref, sem = refs[-5:]
    fetch = pltpu.make_async_copy(tables_ref, meta_ref, sem)
    fetch.start()
    t_s[...] = jnp.zeros(t_s.shape, F32)
    fetch.wait()
    table = Layout(meta_ref, *sizes)
    me = table.me()
    blocks = table.blocks
    local = blocks // tm
    share = q4_ref.shape[1]
    mask_b = diag_mask(share // head_size, BLOCK, head_size).astype(BF16)

    places = [(m, j, table.block_of((me ^ m) * local + j)) for m in range(tm) for j in range(local)]
    for m, j, b in places:
        gt_s[row_at(b)] = g_refs[m][j * ROWS + HALO : (j + 1) * ROWS].astype(F32)
    gt_s[(PAD - 1) * BLOCK : PAD * BLOCK] = jnp.zeros((BLOCK, share), F32)
    for m, j, b in places:
        at = row_at(b, HALO, -HALO)
        gt_s[at] = gt_s[at] + g_refs[m][j * ROWS : j * ROWS + HALO].astype(F32)

    def spans(c):
        own = slice((c + PAD) * BLOCK, (c + PAD + 1) * BLOCK)
        win = slice((c + PAD - LC) * BLOCK, (c + PAD + 1) * BLOCK)
        return own, win, spread(gt_s[own].astype(BF16), mask_b)

    @pl.when(me >= tm // 2)
    def _():
        for c in range(blocks):
            own, win, diag_g = spans(c)
            t_s[win] = t_s[win] + dot_nn(p_ref[c].astype(BF16), diag_g)

    @pl.when(me < tm // 2)
    def _():
        for c in range(blocks):
            own, win, diag_g = spans(c)
            grad_probs = dot_nt(v4_ref[win], diag_g)
            probs = p_ref[c]
            delta = jnp.sum(probs * grad_probs, axis=0, keepdims=True)
            grad_raw = probs * (grad_probs - delta) * d_ref[c]
            t_s[win] = t_s[win] + dot_nn(grad_raw.astype(BF16), spread(q4_ref[own], mask_b))

    terms = jnp.concatenate([t_s[row_at(b)].astype(BF16) for _, _, b in places], axis=0)
    full = dot_nn(nt_ref[...], terms)
    if len(out_refs) == 1:
        out_refs[0][...] = full.astype(BF16)
        return
    full_s[...] = full
    chip, core = table.dp() // 2, table.dp() % 2
    for q in range(out_refs[0].shape[0] // part):
        for ref, side in zip(out_refs, (core, 1 - core)):
            at = pl.ds(pl.multiple_of(((chip ^ q) * 2 + side) * part, part), part)
            ref[q * part : (q + 1) * part] = full_s[at].astype(ref.dtype)


def pair_kernel(kept_ref, got_ref, *out_refs):
    part = out_refs[0].shape[0]
    for q, ref in enumerate(out_refs):
        rows = slice(q * part, (q + 1) * part)
        ref[...] = (kept_ref[rows] + got_ref[rows].astype(F32)).astype(ref.dtype)


def sum_kernel(*refs):
    total = refs[0][...].astype(F32)
    for ref in refs[1:-1]:
        total = total + ref[...].astype(F32)
    refs[-1][...] = total


def on_device(
    frames,
    out_grad,
    norm1_gain,
    w_query,
    w_kv,
    w_out,
    norm2_gain,
    conv_kernel,
    conv_bias,
    utt_blocks,
    block_slot,
    left_count,
):
    tm = lax.axis_size("tm")
    dp = lax.axis_size("dp")
    rows, width = frames.shape
    blocks = block_slot.shape[1]
    utts = utt_blocks.shape[1]
    sizes = (utts, blocks)
    local = rows // BLOCK
    hq = w_query.shape[1]
    head_size = hq // HEADS
    kv_width = w_kv.shape[1]
    share = kv_width // tm
    padded = (blocks + PAD) * BLOCK

    def swap(value, axis, size, m):
        return lax.ppermute(value, axis, [(i, i ^ m) for i in range(size)])

    meta = jnp.concatenate(
        [
            lax.axis_index("tm").astype(jnp.int32).reshape(1, 1),
            lax.axis_index("dp").astype(jnp.int32).reshape(1, 1),
            utt_blocks,
            block_slot,
            left_count,
        ],
        axis=1,
    )
    small = jnp.concatenate(
        [conv_kernel, conv_bias.reshape(1, -1), norm2_gain.reshape(1, -1)], axis=0
    )

    smem = pl.BlockSpec(memory_space=pltpu.SMEM)
    vmem = pl.BlockSpec(memory_space=pltpu.VMEM)
    shape = jax.ShapeDtypeStruct

    taps, w_out_t = pl.pallas_call(
        taps_kernel,
        out_shape=[shape((KERNEL * SUB, width), F32), shape((width, hq), BF16)],
        in_specs=[vmem] * 2,
        out_specs=[vmem] * 2,
        compiler_params=pltpu.CompilerParams(vmem_limit_bytes=4 << 20),
        cost_estimate=pl.CostEstimate(flops=10**6, bytes_accessed=1 << 20, transcendentals=0),
        name="spread_taps",
    )(small, w_out)

    x, normed, queries, keys_values = {}, {}, {}, {}
    made = [shape((rows, w), BF16) for w in (width, hq, kv_width)]

    def project_shard(m, part):
        normed[m], queries[m], keys_values[m] = pl.pallas_call(
            project_kernel,
            out_shape=made,
            in_specs=[vmem] * 4,
            out_specs=[vmem] * 3,
            compiler_params=pltpu.CompilerParams(vmem_limit_bytes=4 << 20),
            cost_estimate=pl.CostEstimate(
                flops=2 * rows * width * (hq + kv_width), bytes_accessed=4 << 20, transcendentals=0
            ),
            name=f"project_rows_{m}",
        )(part, norm1_gain.reshape(1, -1), w_query, w_kv)

    project_shard(0, frames)
    x[0] = frames
    if tm == 4:
        x[2] = swap(frames, "tm", tm, 2)
        x[1] = swap(frames, "tm", tm, 1)
        facing, normed[0], taps, meta = lax.optimization_barrier((x[2], normed[0], taps, meta))
        x[3] = swap(facing, "tm", tm, 1)
        project_shard(2, facing)
        project_shard(1, x[1])
    else:
        for m in range(1, tm):
            x[m] = swap(frames, "tm", tm, m)
            if m < tm - 1:
                project_shard(m, x[m])

    def by_m(arrays):
        return [arrays[m] for m in sorted(arrays)]

    own_rows = local * ROWS
    results = pl.pallas_call(
        functools.partial(forward_kernel, sizes, tm, head_size),
        out_shape=[shape((rows, width), BF16)]
        + made
        + [shape((own_rows, share), BF16)] * tm,
        in_specs=[pl.BlockSpec(memory_space=pl.ANY)] + [vmem] * (6 + 3 * tm),
        out_specs=[vmem] * (tm + 4),
        scratch_shapes=[
            pltpu.VMEM((padded, hq), BF16),
            pltpu.VMEM((padded, kv_width), BF16),
            pltpu.VMEM(((blocks + 1) * HALO, width), BF16),
            pltpu.VMEM((own_rows, hq), BF16),
            pltpu.VMEM((own_rows, width), F32),
            pltpu.VMEM((rows, width), F32),
            pltpu.VMEM((own_rows, width), F32),
            pltpu.VMEM((own_rows, width), F32),
            pltpu.VMEM((own_rows, width), BF16),
            pltpu.SMEM(meta.shape, jnp.int32),
            pltpu.SemaphoreType.DMA,
        ],
        compiler_params=pltpu.CompilerParams(vmem_limit_bytes=16 << 20),
        name="forward_pass",
    )(
        meta,
        out_grad,
        w_out,
        w_out_t,
        small,
        taps,
        norm1_gain.reshape(1, -1),
        w_query,
        w_kv,
        *by_m(x),
        *by_m(queries),
        *by_m(keys_values),
    )
    made_out, normed[tm - 1], queries[tm - 1], keys_values[tm - 1] = results[:4]
    sends = results[:3:-1]
    got = {0: sends[0]}
    for m in range(tm - 1, 0, -1):
        got[m] = swap(sends[m], "tm", tm, m)

    pair_width = share // head_size * BLOCK
    layer_out, q4, v4, probs, slopes, normed_t = pl.pallas_call(
        functools.partial(probs_kernel, sizes, tm, head_size),
        out_shape=[shape((rows, width), BF16)]
        + [shape((padded, share), BF16)] * 2
        + [shape((blocks, SPAN, pair_width), F32)] * 2
        + [shape((width, blocks * BLOCK), BF16)],
        in_specs=[smem] + [vmem] * (3 * tm + 1),
        out_specs=[vmem] * 6,
        scratch_shapes=[pltpu.VMEM((padded, share), BF16)],
        compiler_params=pltpu.CompilerParams(vmem_limit_bytes=8 << 20),
        name="window_probs",
        cost_estimate=pl.CostEstimate(
            flops=2 * 10**9, bytes_accessed=4 * 10**6, transcendentals=800000
        ),
    )(meta, *by_m(queries), *by_m(keys_values), *by_m(normed), made_out)

    direct = dp <= 8
    half_width = width // 2
    if direct:
        piece_shapes = [shape((half_width, share), F32), shape((half_width, share), BF16)]
    else:
        piece_shapes = [shape((width, share), BF16)]
    pieces = pl.pallas_call(
        functools.partial(backward_kernel, sizes, tm, width // dp, head_size),
        out_shape=piece_shapes,
        in_specs=[pl.BlockSpec(memory_space=pl.ANY)] + [vmem] * (5 + tm),
        out_specs=[vmem] * len(piece_shapes),
        scratch_shapes=[
            pltpu.VMEM((padded, share), F32),
            pltpu.VMEM((padded, share), F32),
            pltpu.VMEM((width, share), F32),
            pltpu.SMEM(meta.shape, jnp.int32),
            pltpu.SemaphoreType.DMA,
        ],
        compiler_params=pltpu.CompilerParams(vmem_limit_bytes=12 << 20),
        name="key_value_terms",
    )(meta, q4, v4, probs, slopes, normed_t, *[got[m] for m in sending_order(tm)])

    if direct:
        kept, away = pieces
        arrived = swap(away, "dp", dp, 1)
        chips = dp // 2
        part = width // dp
        summed = pl.pallas_call(
            pair_kernel,
            out_shape=[shape((part, share), BF16)] * chips,
            in_specs=[vmem] * 2,
            out_specs=[vmem] * chips,
            compiler_params=pltpu.CompilerParams(vmem_limit_bytes=4 << 20),
            name="sum_pair",
        )(kept, arrived)
        terms = [swap(summed[q], "dp", dp, 2 * q) for q in range(chips - 1, 0, -1)]
        terms.append(summed[0])
    else:
        terms = [lax.psum_scatter(pieces[0], "dp", scatter_dimension=0, tiled=True)]
    kv_grad = pl.pallas_call(
        sum_kernel,
        out_shape=shape((width // dp, share), F32),
        in_specs=[vmem] * len(terms),
        out_specs=vmem,
        compiler_params=pltpu.CompilerParams(vmem_limit_bytes=4 << 20),
        name="sum_groups",
    )(*terms)
    return layer_out, kv_grad


def solution(mesh):
    return jax.shard_map(
        on_device,
        mesh=mesh,
        in_specs=(
            P(("dp", "tm"), None),
            P(("dp", "tm"), None),
            P(),
            P(),
            P(),
            P(),
            P(),
            P(),
            P(),
            P("dp", None),
            P("dp", None),
            P("dp", None),
        ),
        out_specs=(P(("dp", "tm"), None), P("dp", "tm")),
        check_vma=False,
    )
```

```python
import functools
import math

import jax
import jax.numpy as jnp
from jax import lax
from jax.experimental import pallas as pl
from jax.experimental.pallas import tpu as pltpu
from jax.sharding import PartitionSpec as P

HEADS = 8
KERNEL = 31
BLOCK = 64
LC = 2
SPAN = (LC + 1) * BLOCK
HALO = 32
ROWS = HALO + BLOCK
KERNEL_GAP = HALO - (KERNEL - 1)
PAD = LC + 1
EPSILON = 1e-05
SOFT_CAP = 4.0
LANES = 128
SUB = 8

BF16 = jnp.bfloat16
F32 = jnp.float32


def dot_nn(a, b):
    return lax.dot_general(a, b, (((1,), (0,)), ((), ())), preferred_element_type=F32)


def dot_nt(a, b):
    return lax.dot_general(a, b, (((1,), (1,)), ((), ())), preferred_element_type=F32)


def dot_tn(a, b):
    return lax.dot_general(a, b, (((0,), (0,)), ((), ())), preferred_element_type=F32)


def norm_stats(values):
    row_mean = jnp.mean(values, axis=-1, keepdims=True)
    centred = values - row_mean
    scale_inv = lax.rsqrt(jnp.mean(centred * centred, axis=-1, keepdims=True) + EPSILON)
    return centred * scale_inv, scale_inv


def sending_order(tm):
    return (*range(2, tm), 1, 0)


class Layout:
    def __init__(self, meta_ref, utts, blocks):
        self.ref, self.utts, self.blocks = meta_ref, utts, blocks

    def me(self):
        return self.ref[0, 0]

    def dp(self):
        return self.ref[0, 1]

    def block_of(self, slot):
        found = jnp.int32(0)
        for b in range(self.blocks):
            found = jnp.where(self.ref[0, 2 + self.utts + b] == slot, jnp.int32(b), found)
        return found

    def position(self, block):
        start = jnp.int32(0)
        first = jnp.int32(0)
        for u in range(self.utts):
            first = jnp.where(block >= start, start, first)
            start = start + self.ref[0, 2 + u]
        return block - first

    def reach(self, block):
        safe = jnp.maximum(block, 0)
        left = self.ref[0, 2 + self.utts + self.blocks + safe]
        return jnp.minimum(left, self.position(safe))


def row_at(block, count=BLOCK, shift=0):
    return pl.ds(pl.multiple_of((block + PAD) * BLOCK + shift, math.gcd(BLOCK, shift)), count)


def diag_mask(heads, rows, head_size):
    shape = (heads * rows, heads * head_size)
    row_head = lax.broadcasted_iota(jnp.int32, shape, 0) // rows
    col_head = lax.broadcasted_iota(jnp.int32, shape, 1) // head_size
    return jnp.where(row_head == col_head, 1.0, 0.0).astype(F32)


def spread(rows, mask_b):
    copies = mask_b.shape[0] // rows.shape[0]
    return jnp.concatenate([rows] * copies, axis=0) * mask_b


def fold_heads(full, mask_f, rows):
    kept = full * mask_f
    total = kept[:rows]
    for h in range(1, full.shape[0] // rows):
        total = total + kept[h * rows : (h + 1) * rows]
    return total


def window_probs(diag_q, k_win, reach):
    unit = jnp.tanh(dot_nt(k_win, diag_q))
    exped = jnp.exp2(unit * (SOFT_CAP * math.log2(math.e)))
    parts = [exped[w * BLOCK : (w + 1) * BLOCK] for w in range(LC + 1)]
    sums = [jnp.sum(part, axis=0, keepdims=True) for part in parts]
    flags = [jnp.where(reach >= LC - w, 1.0, 0.0).astype(F32) for w in range(LC)]
    total = sums[LC]
    for w in range(LC):
        total = total + sums[w] * flags[w]
    inverse = 1.0 / total
    scaled = [parts[w] * (inverse * flags[w]) for w in range(LC)] + [parts[LC] * inverse]
    return jnp.concatenate(scaled, axis=0), unit


def taps_kernel(small_ref, wo_ref, taps_ref, wot_ref):
    wot_ref[...] = wo_ref[...].T
    for j in range(KERNEL):
        rows = jnp.broadcast_to(small_ref[j : j + 1], (SUB, small_ref.shape[1]))
        taps_ref[j * SUB : (j + 1) * SUB] = rows


def project_kernel(x_ref, g1_ref, wq_ref, wkv_ref, n_ref, q_ref, kv_ref):
    project(x_ref, g1_ref, wq_ref, wkv_ref, n_ref, q_ref, kv_ref)


def project(x_ref, g1_ref, wq_ref, wkv_ref, n_ref, q_ref, kv_ref):
    unit, _ = norm_stats(x_ref[...].astype(F32))
    normed = (unit * g1_ref[...]).astype(BF16)
    n_ref[...] = normed
    q_ref[...] = dot_nn(normed, wq_ref[...]).astype(BF16)
    kv_ref[...] = dot_nn(normed, wkv_ref[...]).astype(BF16)


def shifted_up(values, shift):
    return pltpu.roll(values, values.shape[0] - shift, axis=0) if shift else values


def forward_kernel(sizes, tm, head_size, *refs):
    tables_ref, grad_ref, wo_ref, wot_ref, small_ref, taps_ref = refs[:6]
    g1_ref, wq_ref, wkv_ref = refs[6:9]
    refs = refs[9:]
    x_refs = refs[:tm]
    q_refs, kv_refs = (refs[tm + k * (tm - 1) : tm + (k + 1) * (tm - 1)] for k in range(2))
    refs = refs[3 * tm - 2 :]
    half = tm // 2
    out_ref, n_last, q_last, kv_last = refs[:4]
    send_refs = refs[4 : 4 + tm][::-1]
    q_ref, kv_ref, tail_s, ctx_s, e_s, h_s, u_s, gr_s, gc_s, meta_ref, sem = refs[4 + tm :]
    fetch = pltpu.make_async_copy(tables_ref, meta_ref, sem)
    fetch.start()
    project(x_refs[-1], g1_ref, wq_ref, wkv_ref, n_last, q_last, kv_last)
    q_refs, kv_refs = (*q_refs, q_last), (*kv_refs, kv_last)
    fetch.wait()

    table = Layout(meta_ref, *sizes)
    me = table.me()
    local = table.blocks // tm
    width = out_ref.shape[1]
    hq = q_ref.shape[1]
    share = send_refs[0].shape[1]

    for ref in (q_ref, kv_ref):
        ref[: PAD * BLOCK] = jnp.zeros((PAD * BLOCK, ref.shape[1]), BF16)
    tail_s[:HALO] = jnp.zeros((HALO, width), BF16)
    for m in range(tm):
        for j in range(local):
            b = table.block_of((me ^ m) * local + j)
            here = slice(j * BLOCK, (j + 1) * BLOCK)
            q_ref[row_at(b)] = q_refs[m][here]
            kv_ref[row_at(b)] = kv_refs[m][here]
            after = pl.ds(pl.multiple_of((b + 1) * HALO, HALO), HALO)
            tail_s[after] = x_refs[m][(j + 1) * BLOCK - HALO : (j + 1) * BLOCK]

    mid_heads = 256 // BLOCK
    mid_f = diag_mask(mid_heads, BLOCK, head_size)
    lower = 1.0 / (SOFT_CAP * math.sqrt(head_size))
    mid_b = (mid_f * lower).astype(BF16)
    side_f = diag_mask(HEADS, HALO, head_size)
    side_b = (side_f * lower).astype(BF16)

    own = [table.block_of(me * local + i) for i in range(local)]
    keep = [jnp.where(table.position(c) >= 1, 1.0, 0.0).astype(F32) for c in own]

    def attend(i, unit):
        blk, shift, count, put = ((own[i] - 1, HALO, HALO, 0), (own[i], 0, BLOCK, HALO))[unit > 0]
        mask_f, mask_b = (mid_f, mid_b) if unit else (side_f, side_b)
        wide = mid_heads * head_size if unit else hq
        first = max(unit - 1, 0) * wide
        cols = slice(first, first + wide)
        win = row_at(blk - LC, SPAN)
        diag_q = spread(q_ref[row_at(blk, count, shift), cols], mask_b)
        probs, _ = window_probs(diag_q, kv_ref[win, cols], table.reach(blk))
        full = dot_tn(probs.astype(BF16), kv_ref[win, hq + first : hq + first + wide])
        rows = slice(i * ROWS + put, i * ROWS + put + count)
        ctx_s[rows, cols] = fold_heads(full, mask_f, count).astype(BF16)

    gain = small_ref[KERNEL + 1 : KERNEL + 2]
    scales = {}

    def settle(i):
        here = slice(i * ROWS, (i + 1) * ROWS)
        tail = tail_s[pl.ds(pl.multiple_of(own[i] * HALO, HALO), HALO)]
        rows = jnp.concatenate([tail, x_refs[0][i * BLOCK : (i + 1) * BLOCK]], axis=0)
        hidden = rows.astype(F32) + dot_nn(ctx_s[here], wo_ref[...])
        unit, inv = norm_stats(hidden)
        conv_in = (unit * gain).astype(BF16).astype(F32)
        e_s[i * ROWS : i * ROWS + HALO] = conv_in[:HALO] * keep[i]
        e_s[i * ROWS + HALO : (i + 1) * ROWS] = conv_in[HALO:]
        h_s[i * BLOCK : (i + 1) * BLOCK] = hidden[HALO:]
        u_s[here] = unit
        scales[i] = inv

    groups = BLOCK // SUB

    def conv(i, k):
        cols = slice(k * LANES, (k + 1) * LANES)
        bias = jnp.broadcast_to(small_ref[KERNEL : KERNEL + 1, cols], (SUB, LANES))
        taps = lambda j: taps_ref[j * SUB : (j + 1) * SUB, cols]
        ext = e_s[i * ROWS : (i + 1) * ROWS, cols]
        acc = [bias] * groups
        for s in range(SUB):
            reps = (KERNEL - s + SUB - 1) // SUB
            skip, shift = divmod(s + KERNEL_GAP, SUB)
            moved = shifted_up(ext, shift)
            for a in range(reps):
                tap = taps(SUB * a + s)
                for r in range(groups):
                    at = (a + r + skip) * SUB
                    acc[r] = acc[r] + tap * moved[at : at + SUB]
        mixed = jnp.concatenate(acc, axis=0)
        gate = 0.5 * jnp.tanh(0.5 * mixed) + 0.5
        rows = slice(i * BLOCK, (i + 1) * BLOCK)
        out_ref[rows, cols] = (h_s[rows, cols] + mixed * gate).astype(BF16)
        slope = gate * (1.0 + mixed * (1.0 - gate))
        gm = grad_ref[rows, cols].astype(F32) * slope
        zeros = jnp.zeros((HALO, LANES), F32)
        padded = jnp.concatenate([zeros[:SUB], gm, zeros[:SUB]], axis=0)
        back = [None] * (ROWS // SUB)
        low = HALO // SUB - 1
        for s in range(SUB):
            reps = (KERNEL - s + SUB - 1) // SUB
            start = low if s else low + 1
            moved = shifted_up(padded, s)
            for a in range(reps):
                tap = taps(KERNEL - 1 - SUB * a - s)
                for g in range(start, ROWS // SUB):
                    r = g - a
                    piece = tap * moved[(g - low) * SUB : (g - low + 1) * SUB]
                    back[r] = piece if back[r] is None else back[r] + piece
        for r in range(ROWS // SUB):
            scale = keep[i] if r < HALO // SUB else 1.0
            gr_s[i * ROWS + r * SUB : i * ROWS + (r + 1) * SUB, cols] = back[r] * scale

    def finish(i):
        here = slice(i * ROWS, (i + 1) * ROWS)
        scaled = gr_s[here] * gain
        unit = u_s[here]
        first = jnp.mean(scaled, axis=-1, keepdims=True)
        second = jnp.mean(scaled * unit, axis=-1, keepdims=True)
        back = scales[i] * (scaled - first - unit * second)
        own_grad = grad_ref[i * BLOCK : (i + 1) * BLOCK].astype(F32) + back[HALO:]
        gc_s[i * ROWS : i * ROWS + HALO] = back[:HALO].astype(BF16)
        gc_s[i * ROWS + HALO : (i + 1) * ROWS] = own_grad.astype(BF16)
        for m in range(half):
            at = pl.ds(pl.multiple_of(((me ^ m) % half) * share, share), share)
            grad_context = dot_nn(gc_s[here], wot_ref[:, at]).astype(BF16)
            send_refs[m][here] = grad_context
            send_refs[m + half][here] = grad_context

    units = 1 + HEADS // mid_heads
    chunks = width // LANES
    for unit in range(units):
        attend(0, unit)
    settle(0)
    for i in range(local):
        done = 0
        steps = units if i + 1 < local else 1
        for unit in range(steps):
            if i + 1 < local:
                attend(i + 1, unit)
            upto = chunks * (unit + 1) // steps
            for k in range(done, upto):
                conv(i, k)
                if i > 0 and k == chunks // 2:
                    finish(i - 1)
            done = upto
        if i + 1 < local:
            settle(i + 1)
    finish(local - 1)


def probs_kernel(sizes, tm, head_size, meta_ref, *refs):
    q_refs, kv_refs, n_refs = refs[:tm], refs[tm : 2 * tm], refs[2 * tm : 3 * tm]
    made_ref, out_ref, q4_ref, v4_ref, p_ref, d_ref, nt_ref, k4_ref = refs[3 * tm :]
    out_ref[...] = made_ref[...]
    for m in range(tm):
        rows = n_refs[m].shape[0]
        nt_ref[:, m * rows : (m + 1) * rows] = n_refs[m][...].T
    table = Layout(meta_ref, *sizes)
    me = table.me()
    local = table.blocks // tm
    hq = q_refs[0].shape[1]
    share = q4_ref.shape[1]
    lead = pl.multiple_of((me % (tm // 2)) * share, share)
    for ref in (k4_ref, v4_ref):
        ref[: PAD * BLOCK] = jnp.zeros((PAD * BLOCK, share), BF16)
    for m in range(tm):
        for j in range(local):
            at = row_at(table.block_of((me ^ m) * local + j))
            here = slice(j * BLOCK, (j + 1) * BLOCK)
            q4_ref[at] = q_refs[m][here, pl.ds(lead, share)]
            k4_ref[at] = kv_refs[m][here, pl.ds(lead, share)]
            v4_ref[at] = kv_refs[m][here, pl.ds(pl.multiple_of(hq + lead, share), share)]
    heads = share // head_size
    lower = 1.0 / (SOFT_CAP * math.sqrt(head_size))
    mask_b = (diag_mask(heads, BLOCK, head_size) * lower).astype(BF16)
    for c in range(table.blocks):
        own = slice((c + PAD) * BLOCK, (c + PAD + 1) * BLOCK)
        win = slice((c + PAD - LC) * BLOCK, (c + PAD + 1) * BLOCK)
        diag_q = spread(q4_ref[own], mask_b)
        probs, unit = window_probs(diag_q, k4_ref[win], table.reach(c))
        p_ref[c] = probs
        d_ref[c] = (1.0 - unit * unit) * (1.0 / math.sqrt(head_size))


def backward_kernel(sizes, tm, part, head_size, *refs):
    tables_ref, q4_ref, v4_ref, p_ref, d_ref, nt_ref = refs[:6]
    g_refs = dict(zip(sending_order(tm), refs[6 : 6 + tm]))
    out_refs = refs[6 + tm : -5]
    gt_s, t_s, full_s, meta_ref, sem = refs[-5:]
    fetch = pltpu.make_async_copy(tables_ref, meta_ref, sem)
    fetch.start()
    t_s[...] = jnp.zeros(t_s.shape, F32)
    fetch.wait()
    table = Layout(meta_ref, *sizes)
    me = table.me()
    blocks = table.blocks
    local = blocks // tm
    share = q4_ref.shape[1]
    mask_b = diag_mask(share // head_size, BLOCK, head_size).astype(BF16)

    places = [(m, j, table.block_of((me ^ m) * local + j)) for m in range(tm) for j in range(local)]
    for m, j, b in places:
        gt_s[row_at(b)] = g_refs[m][j * ROWS + HALO : (j + 1) * ROWS].astype(F32)
    gt_s[(PAD - 1) * BLOCK : PAD * BLOCK] = jnp.zeros((BLOCK, share), F32)
    for m, j, b in places:
        at = row_at(b, HALO, -HALO)
        gt_s[at] = gt_s[at] + g_refs[m][j * ROWS : j * ROWS + HALO].astype(F32)

    def spans(c):
        own = slice((c + PAD) * BLOCK, (c + PAD + 1) * BLOCK)
        win = slice((c + PAD - LC) * BLOCK, (c + PAD + 1) * BLOCK)
        return own, win, spread(gt_s[own].astype(BF16), mask_b)

    @pl.when(me >= tm // 2)
    def _():
        for c in range(blocks):
            own, win, diag_g = spans(c)
            t_s[win] = t_s[win] + dot_nn(p_ref[c].astype(BF16), diag_g)

    @pl.when(me < tm // 2)
    def _():
        for c in range(blocks):
            own, win, diag_g = spans(c)
            grad_probs = dot_nt(v4_ref[win], diag_g)
            probs = p_ref[c]
            delta = jnp.sum(probs * grad_probs, axis=0, keepdims=True)
            grad_raw = probs * (grad_probs - delta) * d_ref[c]
            t_s[win] = t_s[win] + dot_nn(grad_raw.astype(BF16), spread(q4_ref[own], mask_b))

    terms = jnp.concatenate([t_s[row_at(b)].astype(BF16) for _, _, b in places], axis=0)
    full = dot_nn(nt_ref[...], terms)
    if len(out_refs) == 1:
        out_refs[0][...] = full.astype(BF16)
        return
    full_s[...] = full
    chip, core = table.dp() // 2, table.dp() % 2
    for q in range(out_refs[0].shape[0] // part):
        for ref, side in zip(out_refs, (core, 1 - core)):
            at = pl.ds(pl.multiple_of(((chip ^ q) * 2 + side) * part, part), part)
            ref[q * part : (q + 1) * part] = full_s[at].astype(ref.dtype)


def pair_kernel(kept_ref, got_ref, *out_refs):
    part = out_refs[0].shape[0]
    for q, ref in enumerate(out_refs):
        rows = slice(q * part, (q + 1) * part)
        ref[...] = (kept_ref[rows] + got_ref[rows].astype(F32)).astype(ref.dtype)


def sum_kernel(*refs):
    total = refs[0][...].astype(F32)
    for ref in refs[1:-1]:
        total = total + ref[...].astype(F32)
    refs[-1][...] = total


def on_device(
    frames,
    out_grad,
    norm1_gain,
    w_query,
    w_kv,
    w_out,
    norm2_gain,
    conv_kernel,
    conv_bias,
    utt_blocks,
    block_slot,
    left_count,
):
    tm = lax.axis_size("tm")
    dp = lax.axis_size("dp")
    rows, width = frames.shape
    blocks = block_slot.shape[1]
    utts = utt_blocks.shape[1]
    sizes = (utts, blocks)
    local = rows // BLOCK
    hq = w_query.shape[1]
    head_size = hq // HEADS
    kv_width = w_kv.shape[1]
    share = kv_width // tm
    padded = (blocks + PAD) * BLOCK

    def swap(value, axis, size, m):
        return lax.ppermute(value, axis, [(i, i ^ m) for i in range(size)])

    meta = jnp.concatenate(
        [
            lax.axis_index("tm").astype(jnp.int32).reshape(1, 1),
            lax.axis_index("dp").astype(jnp.int32).reshape(1, 1),
            utt_blocks,
            block_slot,
            left_count,
        ],
        axis=1,
    )
    small = jnp.concatenate(
        [conv_kernel, conv_bias.reshape(1, -1), norm2_gain.reshape(1, -1)], axis=0
    )

    smem = pl.BlockSpec(memory_space=pltpu.SMEM)
    vmem = pl.BlockSpec(memory_space=pltpu.VMEM)
    shape = jax.ShapeDtypeStruct

    taps, w_out_t = pl.pallas_call(
        taps_kernel,
        out_shape=[shape((KERNEL * SUB, width), F32), shape((width, hq), BF16)],
        in_specs=[vmem] * 2,
        out_specs=[vmem] * 2,
        compiler_params=pltpu.CompilerParams(vmem_limit_bytes=4 << 20),
        cost_estimate=pl.CostEstimate(flops=10**6, bytes_accessed=1 << 20, transcendentals=0),
        name="spread_taps",
    )(small, w_out)

    x, normed, queries, keys_values = {}, {}, {}, {}
    made = [shape((rows, w), BF16) for w in (width, hq, kv_width)]

    def project_shard(m, part):
        normed[m], queries[m], keys_values[m] = pl.pallas_call(
            project_kernel,
            out_shape=made,
            in_specs=[vmem] * 4,
            out_specs=[vmem] * 3,
            compiler_params=pltpu.CompilerParams(vmem_limit_bytes=4 << 20),
            cost_estimate=pl.CostEstimate(
                flops=2 * rows * width * (hq + kv_width), bytes_accessed=4 << 20, transcendentals=0
            ),
            name=f"project_rows_{m}",
        )(part, norm1_gain.reshape(1, -1), w_query, w_kv)

    project_shard(0, frames)
    x[0] = frames
    if tm == 4:
        x[2] = swap(frames, "tm", tm, 2)
        x[1] = swap(frames, "tm", tm, 1)
        facing, normed[0], taps, meta = lax.optimization_barrier((x[2], normed[0], taps, meta))
        x[3] = swap(facing, "tm", tm, 1)
        project_shard(2, facing)
        project_shard(1, x[1])
    else:
        for m in range(1, tm):
            x[m] = swap(frames, "tm", tm, m)
            if m < tm - 1:
                project_shard(m, x[m])

    def by_m(arrays):
        return [arrays[m] for m in sorted(arrays)]

    own_rows = local * ROWS
    results = pl.pallas_call(
        functools.partial(forward_kernel, sizes, tm, head_size),
        out_shape=[shape((rows, width), BF16)]
        + made
        + [shape((own_rows, share), BF16)] * tm,
        in_specs=[pl.BlockSpec(memory_space=pl.ANY)] + [vmem] * (6 + 3 * tm),
        out_specs=[vmem] * (tm + 4),
        scratch_shapes=[
            pltpu.VMEM((padded, hq), BF16),
            pltpu.VMEM((padded, kv_width), BF16),
            pltpu.VMEM(((blocks + 1) * HALO, width), BF16),
            pltpu.VMEM((own_rows, hq), BF16),
            pltpu.VMEM((own_rows, width), F32),
            pltpu.VMEM((rows, width), F32),
            pltpu.VMEM((own_rows, width), F32),
            pltpu.VMEM((own_rows, width), F32),
            pltpu.VMEM((own_rows, width), BF16),
            pltpu.SMEM(meta.shape, jnp.int32),
            pltpu.SemaphoreType.DMA,
        ],
        compiler_params=pltpu.CompilerParams(vmem_limit_bytes=16 << 20),
        name="forward_pass",
    )(
        meta,
        out_grad,
        w_out,
        w_out_t,
        small,
        taps,
        norm1_gain.reshape(1, -1),
        w_query,
        w_kv,
        *by_m(x),
        *by_m(queries),
        *by_m(keys_values),
    )
    made_out, normed[tm - 1], queries[tm - 1], keys_values[tm - 1] = results[:4]
    sends = results[:3:-1]
    got = {0: sends[0]}
    for m in range(tm - 1, 0, -1):
        got[m] = swap(sends[m], "tm", tm, m)

    pair_width = share // head_size * BLOCK
    layer_out, q4, v4, probs, slopes, normed_t = pl.pallas_call(
        functools.partial(probs_kernel, sizes, tm, head_size),
        out_shape=[shape((rows, width), BF16)]
        + [shape((padded, share), BF16)] * 2
        + [shape((blocks, SPAN, pair_width), F32)] * 2
        + [shape((width, blocks * BLOCK), BF16)],
        in_specs=[smem] + [vmem] * (3 * tm + 1),
        out_specs=[vmem] * 6,
        scratch_shapes=[pltpu.VMEM((padded, share), BF16)],
        compiler_params=pltpu.CompilerParams(vmem_limit_bytes=8 << 20),
        name="window_probs",
        cost_estimate=pl.CostEstimate(
            flops=2 * 10**9, bytes_accessed=4 * 10**6, transcendentals=800000
        ),
    )(meta, *by_m(queries), *by_m(keys_values), *by_m(normed), made_out)

    direct = dp <= 8
    half_width = width // 2
    if direct:
        piece_shapes = [shape((half_width, share), F32), shape((half_width, share), BF16)]
    else:
        piece_shapes = [shape((width, share), BF16)]
    pieces = pl.pallas_call(
        functools.partial(backward_kernel, sizes, tm, width // dp, head_size),
        out_shape=piece_shapes,
        in_specs=[pl.BlockSpec(memory_space=pl.ANY)] + [vmem] * (5 + tm),
        out_specs=[vmem] * len(piece_shapes),
        scratch_shapes=[
            pltpu.VMEM((padded, share), F32),
            pltpu.VMEM((padded, share), F32),
            pltpu.VMEM((width, share), F32),
            pltpu.SMEM(meta.shape, jnp.int32),
            pltpu.SemaphoreType.DMA,
        ],
        compiler_params=pltpu.CompilerParams(vmem_limit_bytes=12 << 20),
        name="key_value_terms",
    )(meta, q4, v4, probs, slopes, normed_t, *[got[m] for m in sending_order(tm)])

    if direct:
        kept, away = pieces
        arrived = swap(away, "dp", dp, 1)
        chips = dp // 2
        part = width // dp
        summed = pl.pallas_call(
            pair_kernel,
            out_shape=[shape((part, share), BF16)] * chips,
            in_specs=[vmem] * 2,
            out_specs=[vmem] * chips,
            compiler_params=pltpu.CompilerParams(vmem_limit_bytes=4 << 20),
            name="sum_pair",
        )(kept, arrived)
        terms = [swap(summed[q], "dp", dp, 2 * q) for q in range(chips - 1, 0, -1)]
        terms.append(summed[0])
    else:
        terms = [lax.psum_scatter(pieces[0], "dp", scatter_dimension=0, tiled=True)]
    kv_grad = pl.pallas_call(
        sum_kernel,
        out_shape=shape((width // dp, share), F32),
        in_specs=[vmem] * len(terms),
        out_specs=vmem,
        compiler_params=pltpu.CompilerParams(vmem_limit_bytes=4 << 20),
        name="sum_groups",
    )(*terms)
    return layer_out, kv_grad


def solution(mesh):
    return jax.shard_map(
        on_device,
        mesh=mesh,
        in_specs=(
            P(("dp", "tm"), None),
            P(("dp", "tm"), None),
            P(),
            P(),
            P(),
            P(),
            P(),
            P(),
            P(),
            P("dp", None),
            P("dp", None),
            P("dp", None),
        ),
        out_specs=(P(("dp", "tm"), None), P("dp", "tm")),
        check_vma=False,
    )
```

```python
import functools
import math

import jax
import jax.numpy as jnp
from jax import lax
from jax.experimental import pallas as pl
from jax.experimental.pallas import tpu as pltpu
from jax.sharding import PartitionSpec as P

HEADS = 8
KERNEL = 31
BLOCK = 64
LC = 2
SPAN = (LC + 1) * BLOCK
HALO = 32
ROWS = HALO + BLOCK
KERNEL_GAP = HALO - (KERNEL - 1)
PAD = LC + 1
EPSILON = 1e-05
SOFT_CAP = 4.0
LANES = 128
SUB = 8

BF16 = jnp.bfloat16
F32 = jnp.float32


def dot_nn(a, b):
    return lax.dot_general(a, b, (((1,), (0,)), ((), ())), preferred_element_type=F32)


def dot_nt(a, b):
    return lax.dot_general(a, b, (((1,), (1,)), ((), ())), preferred_element_type=F32)


def dot_tn(a, b):
    return lax.dot_general(a, b, (((0,), (0,)), ((), ())), preferred_element_type=F32)


def norm_stats(values):
    row_mean = jnp.mean(values, axis=-1, keepdims=True)
    centred = values - row_mean
    scale_inv = lax.rsqrt(jnp.mean(centred * centred, axis=-1, keepdims=True) + EPSILON)
    return centred * scale_inv, scale_inv


def sending_order(tm):
    return (*range(2, tm), 1, 0)


class Layout:
    def __init__(self, meta_ref, utts, blocks):
        self.ref, self.utts, self.blocks = meta_ref, utts, blocks

    def me(self):
        return self.ref[0, 0]

    def dp(self):
        return self.ref[0, 1]

    def block_of(self, slot):
        found = jnp.int32(0)
        for b in range(self.blocks):
            found = jnp.where(self.ref[0, 2 + self.utts + b] == slot, jnp.int32(b), found)
        return found

    def position(self, block):
        start = jnp.int32(0)
        first = jnp.int32(0)
        for u in range(self.utts):
            first = jnp.where(block >= start, start, first)
            start = start + self.ref[0, 2 + u]
        return block - first

    def reach(self, block):
        safe = jnp.maximum(block, 0)
        left = self.ref[0, 2 + self.utts + self.blocks + safe]
        return jnp.minimum(left, self.position(safe))


def row_at(block, count=BLOCK, shift=0):
    return pl.ds(pl.multiple_of((block + PAD) * BLOCK + shift, math.gcd(BLOCK, shift)), count)


def diag_mask(heads, rows, head_size):
    shape = (heads * rows, heads * head_size)
    row_head = lax.broadcasted_iota(jnp.int32, shape, 0) // rows
    col_head = lax.broadcasted_iota(jnp.int32, shape, 1) // head_size
    return jnp.where(row_head == col_head, 1.0, 0.0).astype(F32)


def spread(rows, mask_b):
    copies = mask_b.shape[0] // rows.shape[0]
    return jnp.concatenate([rows] * copies, axis=0) * mask_b


def fold_heads(full, mask_f, rows):
    kept = full * mask_f
    total = kept[:rows]
    for h in range(1, full.shape[0] // rows):
        total = total + kept[h * rows : (h + 1) * rows]
    return total


def window_probs(diag_q, k_win, reach):
    unit = jnp.tanh(dot_nt(k_win, diag_q))
    exped = jnp.exp2(unit * (SOFT_CAP * math.log2(math.e)))
    parts = [exped[w * BLOCK : (w + 1) * BLOCK] for w in range(LC + 1)]
    sums = [jnp.sum(part, axis=0, keepdims=True) for part in parts]
    flags = [jnp.where(reach >= LC - w, 1.0, 0.0).astype(F32) for w in range(LC)]
    total = sums[LC]
    for w in range(LC):
        total = total + sums[w] * flags[w]
    inverse = 1.0 / total
    scaled = [parts[w] * (inverse * flags[w]) for w in range(LC)] + [parts[LC] * inverse]
    return jnp.concatenate(scaled, axis=0), unit


def taps_kernel(small_ref, wo_ref, taps_ref, wot_ref):
    wot_ref[...] = wo_ref[...].T
    for j in range(KERNEL):
        rows = jnp.broadcast_to(small_ref[j : j + 1], (SUB, small_ref.shape[1]))
        taps_ref[j * SUB : (j + 1) * SUB] = rows


def project_kernel(x_ref, g1_ref, wq_ref, wkv_ref, n_ref, q_ref, kv_ref):
    project(x_ref, g1_ref, wq_ref, wkv_ref, n_ref, q_ref, kv_ref)


def project(x_ref, g1_ref, wq_ref, wkv_ref, n_ref, q_ref, kv_ref):
    unit, _ = norm_stats(x_ref[...].astype(F32))
    normed = (unit * g1_ref[...]).astype(BF16)
    n_ref[...] = normed
    q_ref[...] = dot_nn(normed, wq_ref[...]).astype(BF16)
    kv_ref[...] = dot_nn(normed, wkv_ref[...]).astype(BF16)


def shifted_up(values, shift):
    return pltpu.roll(values, values.shape[0] - shift, axis=0) if shift else values


def forward_kernel(sizes, tm, head_size, *refs):
    tables_ref, grad_ref, wo_ref, wot_ref, small_ref, taps_ref = refs[:6]
    g1_ref, wq_ref, wkv_ref = refs[6:9]
    refs = refs[9:]
    x_refs = refs[:tm]
    q_refs, kv_refs = (refs[tm + k * (tm - 1) : tm + (k + 1) * (tm - 1)] for k in range(2))
    refs = refs[3 * tm - 2 :]
    half = tm // 2
    out_ref, n_last, q_last, kv_last = refs[:4]
    send_refs = refs[4 : 4 + tm][::-1]
    q_ref, kv_ref, tail_s, ctx_s, e_s, h_s, u_s, gr_s, gc_s, meta_ref, sem = refs[4 + tm :]
    fetch = pltpu.make_async_copy(tables_ref, meta_ref, sem)
    fetch.start()
    project(x_refs[-1], g1_ref, wq_ref, wkv_ref, n_last, q_last, kv_last)
    q_refs, kv_refs = (*q_refs, q_last), (*kv_refs, kv_last)
    fetch.wait()

    table = Layout(meta_ref, *sizes)
    me = table.me()
    local = table.blocks // tm
    width = out_ref.shape[1]
    hq = q_ref.shape[1]
    share = send_refs[0].shape[1]

    for ref in (q_ref, kv_ref):
        ref[: PAD * BLOCK] = jnp.zeros((PAD * BLOCK, ref.shape[1]), BF16)
    tail_s[:HALO] = jnp.zeros((HALO, width), BF16)
    for m in range(tm):
        for j in range(local):
            b = table.block_of((me ^ m) * local + j)
            here = slice(j * BLOCK, (j + 1) * BLOCK)
            q_ref[row_at(b)] = q_refs[m][here]
            kv_ref[row_at(b)] = kv_refs[m][here]
            after = pl.ds(pl.multiple_of((b + 1) * HALO, HALO), HALO)
            tail_s[after] = x_refs[m][(j + 1) * BLOCK - HALO : (j + 1) * BLOCK]

    mid_heads = 256 // BLOCK
    mid_f = diag_mask(mid_heads, BLOCK, head_size)
    lower = 1.0 / (SOFT_CAP * math.sqrt(head_size))
    mid_b = (mid_f * lower).astype(BF16)
    side_f = diag_mask(HEADS, HALO, head_size)
    side_b = (side_f * lower).astype(BF16)

    own = [table.block_of(me * local + i) for i in range(local)]
    keep = [jnp.where(table.position(c) >= 1, 1.0, 0.0).astype(F32) for c in own]
    for i, c in enumerate(own):
        for blk, shift, count, put in ((c - 1, HALO, HALO, 0), (c, 0, BLOCK, HALO)):
            reach = table.reach(blk)
            win = row_at(blk - LC, SPAN)
            at = row_at(blk, count, shift)
            if count == BLOCK:
                groups, mask_f, mask_b = HEADS // mid_heads, mid_f, mid_b
            else:
                groups, mask_f, mask_b = 1, side_f, side_b
            wide = hq // groups
            for g in range(groups):
                cols = slice(g * wide, (g + 1) * wide)
                vcols = slice(hq + g * wide, hq + (g + 1) * wide)
                probs, _ = window_probs(spread(q_ref[at, cols], mask_b), kv_ref[win, cols], reach)
                full = dot_tn(probs.astype(BF16), kv_ref[win, vcols])
                ctx_s[i * ROWS + put : i * ROWS + put + count, cols] = fold_heads(
                    full, mask_f, count
                ).astype(BF16)

    gain = small_ref[KERNEL + 1 : KERNEL + 2]
    product = dot_nn(ctx_s[...], wo_ref[...])
    scales = []
    for i, c in enumerate(own):
        here = slice(i * ROWS, (i + 1) * ROWS)
        tail = tail_s[pl.ds(pl.multiple_of(c * HALO, HALO), HALO)]
        rows = jnp.concatenate([tail, x_refs[0][i * BLOCK : (i + 1) * BLOCK]], axis=0)
        hidden = rows.astype(F32) + product[here]
        unit, inv = norm_stats(hidden)
        conv_in = (unit * gain).astype(BF16).astype(F32)
        e_s[i * ROWS : i * ROWS + HALO] = conv_in[:HALO] * keep[i]
        e_s[i * ROWS + HALO : (i + 1) * ROWS] = conv_in[HALO:]
        h_s[i * BLOCK : (i + 1) * BLOCK] = hidden[HALO:]
        u_s[here] = unit
        scales.append(inv)

    groups = BLOCK // SUB

    def conv(cols):
        bias = jnp.broadcast_to(small_ref[KERNEL : KERNEL + 1, cols], (SUB, LANES))
        taps = lambda j: taps_ref[j * SUB : (j + 1) * SUB, cols]
        for i in range(local):
            ext = e_s[i * ROWS : (i + 1) * ROWS, cols]
            acc = [bias] * groups
            for s in range(SUB):
                reps = (KERNEL - s + SUB - 1) // SUB
                skip, shift = divmod(s + KERNEL_GAP, SUB)
                moved = shifted_up(ext, shift)
                for a in range(reps):
                    tap = taps(SUB * a + s)
                    for r in range(groups):
                        at = (a + r + skip) * SUB
                        acc[r] = acc[r] + tap * moved[at : at + SUB]
            mixed = jnp.concatenate(acc, axis=0)
            gate = 0.5 * jnp.tanh(0.5 * mixed) + 0.5
            rows = slice(i * BLOCK, (i + 1) * BLOCK)
            out_ref[rows, cols] = (h_s[rows, cols] + mixed * gate).astype(BF16)
            slope = gate * (1.0 + mixed * (1.0 - gate))
            gm = grad_ref[rows, cols].astype(F32) * slope
            zeros = jnp.zeros((HALO, LANES), F32)
            padded = jnp.concatenate([zeros[:SUB], gm, zeros[:SUB]], axis=0)
            back = [None] * (ROWS // SUB)
            low = HALO // SUB - 1
            for s in range(SUB):
                reps = (KERNEL - s + SUB - 1) // SUB
                start = low if s else low + 1
                moved = shifted_up(padded, s)
                for a in range(reps):
                    tap = taps(KERNEL - 1 - SUB * a - s)
                    for g in range(start, ROWS // SUB):
                        r = g - a
                        piece = tap * moved[(g - low) * SUB : (g - low + 1) * SUB]
                        back[r] = piece if back[r] is None else back[r] + piece
            for r in range(ROWS // SUB):
                scale = keep[i] if r < HALO // SUB else 1.0
                gr_s[i * ROWS + r * SUB : i * ROWS + (r + 1) * SUB, cols] = back[r] * scale

    for k in range(0, width, LANES):
        conv(slice(k, k + LANES))

    for i in range(local):
        here = slice(i * ROWS, (i + 1) * ROWS)
        scaled = gr_s[here] * gain
        unit = u_s[here]
        first = jnp.mean(scaled, axis=-1, keepdims=True)
        second = jnp.mean(scaled * unit, axis=-1, keepdims=True)
        back = scales[i] * (scaled - first - unit * second)
        own_grad = grad_ref[i * BLOCK : (i + 1) * BLOCK].astype(F32) + back[HALO:]
        gc_s[i * ROWS : i * ROWS + HALO] = back[:HALO].astype(BF16)
        gc_s[i * ROWS + HALO : (i + 1) * ROWS] = own_grad.astype(BF16)
    for m in range(half):
        at = pl.ds(pl.multiple_of(((me ^ m) % half) * share, share), share)
        grad_context = dot_nn(gc_s[...], wot_ref[:, at]).astype(BF16)
        send_refs[m][...] = grad_context
        send_refs[m + half][...] = grad_context


def probs_kernel(sizes, tm, part, head_size, meta_ref, *refs):
    q_refs, kv_refs, n_refs = refs[:tm], refs[tm : 2 * tm], refs[2 * tm : 3 * tm]
    made_ref, out_ref, diag_ref, v4_ref, p_ref, pb_ref, d_ref, nt_ref, k4_ref, q4_ref = refs[3 * tm :]
    out_ref[...] = made_ref[...]
    table = Layout(meta_ref, *sizes)
    me = table.me()
    local = table.blocks // tm
    hq = q_refs[0].shape[1]
    width = nt_ref.shape[0]
    chip, core = table.dp() // 2, table.dp() % 2
    for q in range(width // part):
        at = pl.ds(q * part, part)
        if part < width:
            place = jnp.where(core == q % 2, 0, width // part // 2) + (chip ^ (q // 2))
            at = pl.ds(pl.multiple_of(place * part, part), part)
        for m in range(tm):
            rows = n_refs[m].shape[0]
            nt_ref[at, m * rows : (m + 1) * rows] = n_refs[m][:, q * part : (q + 1) * part].T
    share = q4_ref.shape[1]
    lead = pl.multiple_of((me % (tm // 2)) * share, share)
    for ref in (k4_ref, v4_ref):
        ref[: PAD * BLOCK] = jnp.zeros((PAD * BLOCK, share), BF16)
    for m in range(tm):
        for j in range(local):
            at = row_at(table.block_of((me ^ m) * local + j))
            here = slice(j * BLOCK, (j + 1) * BLOCK)
            q4_ref[at] = q_refs[m][here, pl.ds(lead, share)]
            k4_ref[at] = kv_refs[m][here, pl.ds(lead, share)]
            v4_ref[at] = kv_refs[m][here, pl.ds(pl.multiple_of(hq + lead, share), share)]
    heads = share // head_size
    lower = 1.0 / (SOFT_CAP * math.sqrt(head_size))
    mask_f = diag_mask(heads, BLOCK, head_size)
    mask_b, low_b = mask_f.astype(BF16), (mask_f * lower).astype(BF16)
    for c in range(table.blocks):
        own = slice((c + PAD) * BLOCK, (c + PAD + 1) * BLOCK)
        win = slice((c + PAD - LC) * BLOCK, (c + PAD + 1) * BLOCK)
        diag_ref[c] = spread(q4_ref[own], mask_b)
        diag_q = spread(q4_ref[own], low_b)
        probs, unit = window_probs(diag_q, k4_ref[win], table.reach(c))
        p_ref[c] = probs
        pb_ref[c] = probs.astype(BF16)
        d_ref[c] = probs * (1.0 - unit * unit) * (1.0 / math.sqrt(head_size))


def backward_kernel(sizes, tm, head_size, *refs):
    tables_ref, diag_ref, v4_ref, p_ref, pb_ref, d_ref, nt_ref = refs[:7]
    g_refs = dict(zip(sending_order(tm), refs[7 : 7 + tm]))
    out_refs = refs[7 + tm : -4]
    gt_s, t_s, meta_ref, sem = refs[-4:]
    fetch = pltpu.make_async_copy(tables_ref, meta_ref, sem)
    fetch.start()
    t_s[...] = jnp.zeros(t_s.shape, F32)
    fetch.wait()
    table = Layout(meta_ref, *sizes)
    me = table.me()
    blocks = table.blocks
    local = blocks // tm
    share = v4_ref.shape[1]
    mask_b = diag_mask(share // head_size, BLOCK, head_size).astype(BF16)

    places = [(m, j, table.block_of((me ^ m) * local + j)) for m in range(tm) for j in range(local)]
    for m, j, b in places:
        gt_s[row_at(b)] = g_refs[m][j * ROWS + HALO : (j + 1) * ROWS].astype(F32)
    gt_s[(PAD - 1) * BLOCK : PAD * BLOCK] = jnp.zeros((BLOCK, share), F32)
    for m, j, b in places:
        at = row_at(b, HALO, -HALO)
        gt_s[at] = gt_s[at] + g_refs[m][j * ROWS : j * ROWS + HALO].astype(F32)

    def spans(c):
        own = slice((c + PAD) * BLOCK, (c + PAD + 1) * BLOCK)
        win = slice((c + PAD - LC) * BLOCK, (c + PAD + 1) * BLOCK)
        return own, win, spread(gt_s[own].astype(BF16), mask_b)

    @pl.when(me >= tm // 2)
    def _():
        for c in range(blocks):
            own, win, diag_g = spans(c)
            t_s[win] = t_s[win] + dot_nn(pb_ref[c], diag_g)

    @pl.when(me < tm // 2)
    def _():
        for c in range(blocks):
            own, win, diag_g = spans(c)
            grad_probs = dot_nt(v4_ref[win], diag_g)
            probs = p_ref[c]
            delta = jnp.sum(probs * grad_probs, axis=0, keepdims=True)
            grad_raw = (grad_probs - delta) * d_ref[c]
            t_s[win] = t_s[win] + dot_nn(grad_raw.astype(BF16), diag_ref[c])

    terms = jnp.concatenate([t_s[row_at(b)].astype(BF16) for _, _, b in places], axis=0)
    full = dot_nn(nt_ref[...], terms)
    if len(out_refs) == 1:
        out_refs[0][...] = full.astype(BF16)
        return
    kept = full.shape[0] // 2
    out_refs[0][...] = full[:kept]
    out_refs[1][...] = full[kept:].astype(BF16)


def pair_kernel(kept_ref, got_ref, *out_refs):
    part = out_refs[0].shape[0]
    for q, ref in enumerate(out_refs):
        rows = slice(q * part, (q + 1) * part)
        ref[...] = (kept_ref[rows] + got_ref[rows].astype(F32)).astype(ref.dtype)


def sum_kernel(*refs):
    total = refs[0][...].astype(F32)
    for ref in refs[1:-1]:
        total = total + ref[...].astype(F32)
    refs[-1][...] = total


def on_device(
    frames,
    out_grad,
    norm1_gain,
    w_query,
    w_kv,
    w_out,
    norm2_gain,
    conv_kernel,
    conv_bias,
    utt_blocks,
    block_slot,
    left_count,
):
    tm = lax.axis_size("tm")
    dp = lax.axis_size("dp")
    rows, width = frames.shape
    blocks = block_slot.shape[1]
    utts = utt_blocks.shape[1]
    sizes = (utts, blocks)
    local = rows // BLOCK
    hq = w_query.shape[1]
    head_size = hq // HEADS
    kv_width = w_kv.shape[1]
    share = kv_width // tm
    padded = (blocks + PAD) * BLOCK

    def swap(value, axis, size, m):
        return lax.ppermute(value, axis, [(i, i ^ m) for i in range(size)])

    meta = jnp.concatenate(
        [
            lax.axis_index("tm").astype(jnp.int32).reshape(1, 1),
            lax.axis_index("dp").astype(jnp.int32).reshape(1, 1),
            utt_blocks,
            block_slot,
            left_count,
        ],
        axis=1,
    )
    small = jnp.concatenate(
        [conv_kernel, conv_bias.reshape(1, -1), norm2_gain.reshape(1, -1)], axis=0
    )

    smem = pl.BlockSpec(memory_space=pltpu.SMEM)
    vmem = pl.BlockSpec(memory_space=pltpu.VMEM)
    shape = jax.ShapeDtypeStruct

    taps, w_out_t = pl.pallas_call(
        taps_kernel,
        out_shape=[shape((KERNEL * SUB, width), F32), shape((width, hq), BF16)],
        in_specs=[vmem] * 2,
        out_specs=[vmem] * 2,
        compiler_params=pltpu.CompilerParams(vmem_limit_bytes=4 << 20),
        cost_estimate=pl.CostEstimate(flops=10**6, bytes_accessed=1 << 20, transcendentals=0),
        name="spread_taps",
    )(small, w_out)

    x, normed, queries, keys_values = {}, {}, {}, {}
    made = [shape((rows, w), BF16) for w in (width, hq, kv_width)]

    def project_shard(m, part):
        normed[m], queries[m], keys_values[m] = pl.pallas_call(
            project_kernel,
            out_shape=made,
            in_specs=[vmem] * 4,
            out_specs=[vmem] * 3,
            compiler_params=pltpu.CompilerParams(vmem_limit_bytes=4 << 20),
            cost_estimate=pl.CostEstimate(
                flops=2 * rows * width * (hq + kv_width), bytes_accessed=4 << 20, transcendentals=0
            ),
            name=f"project_rows_{m}",
        )(part, norm1_gain.reshape(1, -1), w_query, w_kv)

    project_shard(0, frames)
    x[0] = frames
    if tm == 4:
        x[2] = swap(frames, "tm", tm, 2)
        x[1] = swap(frames, "tm", tm, 1)
        facing, normed[0], taps, meta = lax.optimization_barrier((x[2], normed[0], taps, meta))
        x[3] = swap(facing, "tm", tm, 1)
        project_shard(2, facing)
        project_shard(1, x[1])
    else:
        for m in range(1, tm):
            x[m] = swap(frames, "tm", tm, m)
            if m < tm - 1:
                project_shard(m, x[m])

    def by_m(arrays):
        return [arrays[m] for m in sorted(arrays)]

    own_rows = local * ROWS
    results = pl.pallas_call(
        functools.partial(forward_kernel, sizes, tm, head_size),
        out_shape=[shape((rows, width), BF16)]
        + made
        + [shape((own_rows, share), BF16)] * tm,
        in_specs=[pl.BlockSpec(memory_space=pl.ANY)] + [vmem] * (6 + 3 * tm),
        out_specs=[vmem] * (tm + 4),
        scratch_shapes=[
            pltpu.VMEM((padded, hq), BF16),
            pltpu.VMEM((padded, kv_width), BF16),
            pltpu.VMEM(((blocks + 1) * HALO, width), BF16),
            pltpu.VMEM((own_rows, hq), BF16),
            pltpu.VMEM((own_rows, width), F32),
            pltpu.VMEM((rows, width), F32),
            pltpu.VMEM((own_rows, width), F32),
            pltpu.VMEM((own_rows, width), F32),
            pltpu.VMEM((own_rows, width), BF16),
            pltpu.SMEM(meta.shape, jnp.int32),
            pltpu.SemaphoreType.DMA,
        ],
        compiler_params=pltpu.CompilerParams(vmem_limit_bytes=16 << 20),
        name="forward_pass",
    )(
        meta,
        out_grad,
        w_out,
        w_out_t,
        small,
        taps,
        norm1_gain.reshape(1, -1),
        w_query,
        w_kv,
        *by_m(x),
        *by_m(queries),
        *by_m(keys_values),
    )
    made_out, normed[tm - 1], queries[tm - 1], keys_values[tm - 1] = results[:4]
    sends = results[:3:-1]
    got = {0: sends[0]}
    for m in range(tm - 1, 0, -1):
        got[m] = swap(sends[m], "tm", tm, m)

    direct = dp <= 8
    pair_width = share // head_size * BLOCK
    layer_out, diag_q, v4, probs, probs_b, slopes, normed_t = pl.pallas_call(
        functools.partial(probs_kernel, sizes, tm, width // dp if direct else width, head_size),
        out_shape=[shape((rows, width), BF16)]
        + [shape((blocks, pair_width, share), BF16), shape((padded, share), BF16)]
        + [shape((blocks, SPAN, pair_width), kind) for kind in (F32, BF16, F32)]
        + [shape((width, blocks * BLOCK), BF16)],
        in_specs=[smem] + [vmem] * (3 * tm + 1),
        out_specs=[vmem] * 7,
        scratch_shapes=[pltpu.VMEM((padded, share), BF16)] * 2,
        compiler_params=pltpu.CompilerParams(vmem_limit_bytes=8 << 20),
        name="window_probs",
        cost_estimate=pl.CostEstimate(
            flops=2 * 10**9, bytes_accessed=4 * 10**6, transcendentals=800000
        ),
    )(meta, *by_m(queries), *by_m(keys_values), *by_m(normed), made_out)

    half_width = width // 2
    if direct:
        piece_shapes = [shape((half_width, share), F32), shape((half_width, share), BF16)]
    else:
        piece_shapes = [shape((width, share), BF16)]
    pieces = pl.pallas_call(
        functools.partial(backward_kernel, sizes, tm, head_size),
        out_shape=piece_shapes,
        in_specs=[pl.BlockSpec(memory_space=pl.ANY)] + [vmem] * (6 + tm),
        out_specs=[vmem] * len(piece_shapes),
        scratch_shapes=[
            pltpu.VMEM((padded, share), F32),
            pltpu.VMEM((padded, share), F32),
            pltpu.SMEM(meta.shape, jnp.int32),
            pltpu.SemaphoreType.DMA,
        ],
        compiler_params=pltpu.CompilerParams(vmem_limit_bytes=12 << 20),
        name="key_value_terms",
    )(meta, diag_q, v4, probs, probs_b, slopes, normed_t, *[got[m] for m in sending_order(tm)])

    if direct:
        kept, away = pieces
        arrived = swap(away, "dp", dp, 1)
        chips = dp // 2
        part = width // dp
        summed = pl.pallas_call(
            pair_kernel,
            out_shape=[shape((part, share), BF16)] * chips,
            in_specs=[vmem] * 2,
            out_specs=[vmem] * chips,
            compiler_params=pltpu.CompilerParams(vmem_limit_bytes=4 << 20),
            name="sum_pair",
        )(kept, arrived)
        terms = [swap(summed[q], "dp", dp, 2 * q) for q in range(chips - 1, 0, -1)]
        terms.append(summed[0])
    else:
        terms = [lax.psum_scatter(pieces[0], "dp", scatter_dimension=0, tiled=True)]
    kv_grad = pl.pallas_call(
        sum_kernel,
        out_shape=shape((width // dp, share), F32),
        in_specs=[vmem] * len(terms),
        out_specs=vmem,
        compiler_params=pltpu.CompilerParams(vmem_limit_bytes=4 << 20),
        name="sum_groups",
    )(*terms)
    return layer_out, kv_grad


def solution(mesh):
    return jax.shard_map(
        on_device,
        mesh=mesh,
        in_specs=(
            P(("dp", "tm"), None),
            P(("dp", "tm"), None),
            P(),
            P(),
            P(),
            P(),
            P(),
            P(),
            P(),
            P("dp", None),
            P("dp", None),
            P("dp", None),
        ),
        out_specs=(P(("dp", "tm"), None), P("dp", "tm")),
        check_vma=False,
    )
```
